128 devices in a mesh: ctx: 32 (over x, y, core), fsdp: 4 (over z).
Axes of the slice: x: 4, y: 4, z: 4, core: 2. Of those that a mesh axis runs over, the one named last changes fastest.
Arguments:
- tokens: bfloat16 [4, 2, 2048, 1024], P('fsdp', None, 'ctx'), may hold values from -6 to 6
- doc_start: int32 [4, 2, 2048], P('fsdp', None, 'ctx'), may hold values from 0 to 4095, as said below
- cotangent: bfloat16 [4, 2, 2048, 1024], P('fsdp', None, 'ctx'), may hold values from -6 to 6
- w_in: bfloat16 [1024, 4096], P('fsdp'), may hold values from -0.1875 to 0.1875
- w_dt: bfloat16 [1024, 24], P('fsdp'), may hold values from -0.1875 to 0.1875
- conv_weight: bfloat16 [4, 1792], P(None, 'fsdp'), may hold values from -3 to 3
- conv_bias: bfloat16 [1792], P('fsdp'), may hold values from -0.5 to 0.5
- dt_bias: bfloat16 [24], P('fsdp'), may hold values from -3 to 0.5
- a_log: bfloat16 [24], P('fsdp'), may hold values from -9 to -1
- skip_gain: bfloat16 [24], P('fsdp'), may hold values from 0.5 to 1.5
- inner_gain: bfloat16 [1536], P('fsdp'), may hold values from 0.5 to 1.5
- mamba_out: bfloat16 [1536, 1024], P('fsdp'), may hold values from -0.15625 to 0.15625
- attn_out: bfloat16 [512, 1024], P('fsdp'), may hold values from -3 to 3
- mixer_gain: bfloat16 [1024], P('fsdp'), may hold values from 0.5 to 1.5
- ffn_gain: bfloat16 [1024], P('fsdp'), may hold values from 0.5 to 1.5
- w_gate_up: bfloat16 [1024, 4096], P('fsdp'), may hold values from -0.1875 to 0.1875
- w_down: bfloat16 [2048, 1024], P('fsdp'), may hold values from -0.125 to 0.125
Outputs:
- mixed: bfloat16 [4, 2, 2048, 1024], P('fsdp', None, 'ctx')
- grad_tokens: float32 [4, 2, 2048, 1024], P('fsdp', None, 'ctx')
- grad_w_in: float32 [1024, 4096], P('fsdp')
- grad_w_dt: float32 [1024, 24], P('fsdp')
- grad_conv_weight: float32 [4, 1792], P(None, 'fsdp')
- grad_conv_bias: float32 [1792], P('fsdp')
- grad_dt_bias: float32 [24], P('fsdp')
- grad_a_log: float32 [24], P('fsdp')
- grad_skip_gain: float32 [24], P('fsdp')
- grad_inner_gain: float32 [1536], P('fsdp')
- grad_mamba_out: float32 [1536, 1024], P('fsdp')
- grad_attn_out: float32 [512, 1024], P('fsdp')
- grad_mixer_gain: float32 [1024], P('fsdp')
- grad_ffn_gain: float32 [1024], P('fsdp')
- grad_w_gate_up: float32 [1024, 4096], P('fsdp')
- grad_w_down: float32 [2048, 1024], P('fsdp')
The draws below stay inside these ranges and needn't reach their ends.
Inputs may be any that keep to these rules, and one draw needn't show every extreme that they name: `doc_start`: the value at each place is the position of the first token of the document that holds that place's token; documents are contiguous runs of positions, so it never exceeds the place's own position and is constant within a document. In every sequence one document begins in the first 64 positions and runs through position 2111.
All inputs are finite; a program needn't handle non-finite values.
Results may differ from the reference program's by a relative error of at most 0.022.
Values may be sent and summed in bfloat16 or wider, within the bound.
No kernel may reach another device: no remote copies, remote signals or barrier semaphores. Data moves between devices by JAX's collectives and lax.ppermute only.
A program may use at most 320 MiB of HBM per device.

```python
import math
import jax
import jax.numpy as jnp
from jax import lax

D = 1024
FF = 2048
QHEADS = 8
KVHEADS = 2
HDIM = 64
MHEADS = 24
MDIM = 64
NSTATE = 128
KCONV = 4
BLK = 64
HALF = 2048
LEN = 4096
SEQS = 4
CH = 1792
PROJ = 4096


def draw_doc_start(key, part):
    key = jax.random.fold_in(key, 11)
    keys = jax.random.split(key, 3)
    block_count = LEN // (2 * BLK)
    first_cut = jax.random.randint(keys[0], (SEQS, 1), 0, BLK)
    long_end = jax.random.randint(keys[1], (SEQS, 1), (block_count + 1) * BLK, LEN + 1)
    extra_cuts = long_end + jax.random.randint(keys[2], (SEQS, 2), 0, LEN) % (LEN - long_end + 1)
    bounds = jnp.concatenate([jnp.zeros((SEQS, 1), jnp.int32), first_cut, long_end, extra_cuts], axis=1).astype(jnp.int32)
    places = jnp.arange(LEN, dtype=jnp.int32)
    natural = jnp.max(jnp.where(bounds[:, None, :] <= places[None, :, None], bounds[:, None, :], 0), axis=2)
    middle = LEN // 2
    later = natural[:, middle:].reshape(SEQS, block_count, BLK)[:, ::-1].reshape(SEQS, middle)
    return jnp.stack([natural[:, :middle], later], axis=1).astype(jnp.int32)


def block_levels(own_key, dims, cuts, low, largest):
    def one(position, parts):
        steps = jax.random.uniform(jax.random.fold_in(jax.random.fold_in(own_key, 6), position), (parts,), jnp.float32, low / len(cuts), largest / len(cuts))
        return jnp.repeat(jnp.exp(steps), dims[position] // parts).reshape((-1,) + (1,) * (len(dims) - position - 1))

    level = one(*cuts[0])
    for cut in cuts[1:]:
        level = level * one(*cut)
    return level


def scatter_about(rng, dims, scale, limit, cuts=(), kind=jnp.bfloat16):
    values = jax.random.normal(rng, dims, jnp.float32) * scale
    if len(cuts) > 0:
        values = block_levels(rng, dims, cuts, -0.22, 0.18) * values
    return jnp.clip(values, min=-limit, max=limit).astype(kind)


def setup_inputs(seed: int = 0) -> dict:
    arg_keys = jax.random.split(jax.random.key(seed), 18)
    return {
        "tokens": scatter_about(arg_keys[0], (SEQS, 2, HALF, D), 1.0, 6.0, ((0, 4), (2, 32))),
        "doc_start": draw_doc_start(jax.random.fold_in(arg_keys[17], 71), 0),
        "cotangent": scatter_about(arg_keys[2], (SEQS, 2, HALF, D), 1.0, 6.0, ((0, 4), (2, 32))),
        "w_in": scatter_about(arg_keys[3], (D, PROJ), D ** -0.5, 0.1875, ((0, 4),)),
        "w_dt": scatter_about(arg_keys[4], (D, MHEADS), D ** -0.5, 0.1875, ((0, 4),)),
        "conv_weight": scatter_about(arg_keys[5], (KCONV, CH), KCONV ** -0.5, 3.0, ((1, 4),)),
        "conv_bias": jnp.clip(jax.random.uniform(arg_keys[6], (CH,), jnp.float32, -0.5, 0.5) * block_levels(arg_keys[6], (CH,), ((0, 4),), -0.4, 0.0), -0.5, 0.5).astype(jnp.bfloat16),
        "dt_bias": jnp.clip(-3.0 + 3.5 * jax.random.uniform(arg_keys[7], (MHEADS,), jnp.float32) ** block_levels(arg_keys[7], (MHEADS,), ((0, 4),), -0.2, 0.2), -3.0, 0.5).astype(jnp.bfloat16),
        "a_log": jnp.clip(-9.0 + 8.0 * jax.random.uniform(arg_keys[8], (MHEADS,), jnp.float32) ** block_levels(arg_keys[8], (MHEADS,), ((0, 4),), -0.2, 0.2), -9.0, -1.0).astype(jnp.bfloat16),
        "skip_gain": jnp.clip(0.5 + 1.0 * jax.random.uniform(arg_keys[9], (MHEADS,), jnp.float32) ** block_levels(arg_keys[9], (MHEADS,), ((0, 4),), -0.2, 0.2), 0.5, 1.5).astype(jnp.bfloat16),
        "inner_gain": jnp.clip(1.0 + 0.1 * jax.random.normal(arg_keys[10], (MHEADS * MDIM,), jnp.float32), 0.5, 1.5).astype(jnp.bfloat16),
        "mamba_out": scatter_about(arg_keys[11], (MHEADS * MDIM, D), (MHEADS * MDIM) ** -0.5, 0.15625, ((0, 4),)),
        "attn_out": scatter_about(arg_keys[12], (QHEADS * HDIM, D), (max(1, QHEADS * HDIM * 32 // LEN)) ** -0.5, 3.0, ((0, 4),)),
        "mixer_gain": jnp.clip(1.0 + 0.1 * jax.random.normal(arg_keys[13], (D,), jnp.float32), 0.5, 1.5).astype(jnp.bfloat16),
        "ffn_gain": jnp.clip(1.0 + 0.1 * jax.random.normal(arg_keys[14], (D,), jnp.float32), 0.5, 1.5).astype(jnp.bfloat16),
        "w_gate_up": scatter_about(arg_keys[15], (D, 2 * FF), D ** -0.5, 0.1875, ((0, 4),)),
        "w_down": scatter_about(arg_keys[16], (FF, D), FF ** -0.5, 0.125, ((0, 4),)),
    }


@jax.custom_vjp
def low(v):
    return lax.optimization_barrier(v.astype(jnp.bfloat16)).astype(jnp.float32)

@jax.custom_vjp
def low_back(v):
    return v

def low_keep(v):
    return (low(v), None)

def low_pass(kept, grad):
    return (grad,)

def back_keep(v):
    return (v, None)

def back_low(kept, grad):
    return (low(grad),)
low.defvjp(low_keep, low_pass)
low_back.defvjp(back_keep, back_low)
HIGH = lax.Precision.HIGHEST
EPS = 1e-05
ROPE_BASE = 100000000000.0
NEG = -1e+30

def rms_scale(values, gain):
    return values * lax.rsqrt(lax.optimization_barrier(jnp.mean(values * values, axis=-1, keepdims=True)) + EPS) * gain

def gated_norm(mamba_y, gate_z, gain):
    return rms_scale(mamba_y * jax.nn.silu(gate_z), gain)

def swiglu(gate_val, up_val):
    return jax.nn.silu(gate_val) * up_val

def rope_tables(positions, width):
    middle = width // 2
    freq = jnp.exp(jnp.arange(middle, dtype=jnp.float32) * (-2.0 * math.log(ROPE_BASE) / width))
    angle = positions.astype(jnp.float32)[:, None] * freq[None, :]
    return (jnp.cos(angle), jnp.sin(angle))

def rotate(values, cos_table, sin_table):
    middle = values.shape[-1] // 2
    leading = values[..., :middle]
    trailing = values[..., middle:]
    cosine = cos_table[:, None, :]
    sine_part = sin_table[:, None, :]
    return jnp.concatenate([leading * cosine - trailing * sine_part, trailing * cosine + leading * sine_part], axis=-1)

def mamba_inputs(extended, raw_dt, positions, starts, conv_weight, conv_bias, dt_bias, a_log):
    length = positions.shape[0]
    tap_count = conv_weight.shape[0]
    summed = jnp.zeros((length, conv_weight.shape[1]), dtype=extended.dtype) + conv_bias
    for offset in range(tap_count):
        back_steps = tap_count - 1 - offset
        usable = (positions - back_steps >= starts)[:, None]
        summed = summed + jnp.where(usable, conv_weight[offset] * extended[offset:offset + length], 0.0)
    mixed_in = jax.nn.silu(summed)
    inner_width = MHEADS * MDIM
    states_x = mixed_in[:, :inner_width].reshape(length, MHEADS, MDIM)
    input_mat = mixed_in[:, inner_width:inner_width + NSTATE]
    output_mat = mixed_in[:, inner_width + NSTATE:]
    step_size = jax.nn.softplus(raw_dt + dt_bias)
    log_decay = -step_size * jnp.exp(a_log)
    return (states_x, input_mat, output_mat, step_size, log_decay)

def ssd_local(states_x, input_mat, output_mat, step_size, log_decay, positions, starts, skip_gain):
    running = jnp.cumsum(log_decay, axis=0)
    allowed = (positions[None, :] <= positions[:, None]) & (positions[None, :] >= starts[:, None])
    spread = running.T[:, :, None] - running.T[:, None, :]
    decay_mat = jnp.where(allowed[None], jnp.exp(jnp.where(allowed[None], spread, 0.0)), 0.0)
    intersection = jnp.dot(output_mat, input_mat.T, precision=HIGH)
    mixing = decay_mat * intersection[None] * step_size.T[:, None, :]
    result = jnp.einsum('hij,jhp->ihp', mixing, states_x, precision=HIGH) + skip_gain[None, :, None] * states_x
    carried = (starts < positions[0]).astype(running.dtype)
    state_weight = jnp.exp(running) * carried[:, None]
    final_weight = decay_mat[:, -1, :] * step_size.T
    state_out = jnp.einsum('hj,jhp,jn->hpn', final_weight, states_x, input_mat, precision=HIGH)
    return (result, state_out, state_weight)

def state_term(output_mat, state_weight, state_in):
    return state_weight[:, :, None] * jnp.einsum('in,hpn->ihp', output_mat, state_in, precision=HIGH)

def attention(query, keys, values, positions, starts):
    length = query.shape[0]
    block_rows = min(512, length)
    groups = QHEADS // KVHEADS
    score_scale = HDIM ** (-0.5)
    grouped = query.reshape(length // block_rows, block_rows, KVHEADS, groups, HDIM)

    def one_block(pieces):
        query_rows, query_pos, query_start = pieces
        scores = jnp.einsum('qkgd,tkd->kgqt', query_rows, keys, precision=HIGH) * score_scale
        allowed = (positions[None, :] <= query_pos[:, None]) & (positions[None, :] >= query_start[:, None])
        scores = jnp.where(allowed, scores, NEG)
        row_peak = lax.optimization_barrier(jnp.max(scores, axis=-1, keepdims=True))
        weights = jnp.where(allowed, jnp.exp(scores - row_peak), 0.0)
        probs = weights / lax.optimization_barrier(jnp.sum(weights, axis=-1, keepdims=True))
        block_out = jnp.einsum('kgqt,tkd->qkgd', probs, values, precision=HIGH)
        return block_out.reshape(block_rows, QHEADS * HDIM)
    outputs = lax.map(jax.checkpoint(one_block), (grouped, positions.reshape(-1, block_rows), starts.reshape(-1, block_rows)))
    return outputs.reshape(length, QHEADS * HDIM)

def layer(hidden_in, params, starts):
    w_in, w_dt, conv_weight, conv_bias, dt_bias, a_log, skip_gain, inner_gain, mamba_out, attn_out, mixer_gain, ffn_gain, w_gate_up, w_down = params
    length = hidden_in.shape[0]
    positions = jnp.arange(length, dtype=jnp.int32)
    inner_width = MHEADS * MDIM
    conv_width = inner_width + 2 * NSTATE
    query_width = QHEADS * HDIM
    kv_width = KVHEADS * HDIM
    act_one = low(rms_scale(hidden_in, mixer_gain))
    projected = low_back(jnp.dot(act_one, w_in, precision=HIGH))
    raw_dt = low_back(jnp.dot(act_one, w_dt, precision=HIGH))
    gate_z = projected[:, :inner_width]
    conv_in = projected[:, inner_width:inner_width + conv_width]
    query_start = inner_width + conv_width
    kv_start = query_start + query_width
    query_raw = projected[:, query_start:kv_start].reshape(length, QHEADS, HDIM)
    key_raw = projected[:, kv_start:kv_start + kv_width].reshape(length, KVHEADS, HDIM)
    value_raw = projected[:, kv_start + kv_width:].reshape(length, KVHEADS, HDIM)
    extended = jnp.concatenate([jnp.zeros((KCONV - 1, conv_width), hidden_in.dtype), conv_in], axis=0)
    states_x, input_mat, output_mat, step_size, log_decay = mamba_inputs(extended, raw_dt, positions, starts, conv_weight, conv_bias, dt_bias, a_log)
    block_count = length // BLK

    def blockwise(values):
        return values.reshape((block_count, BLK) + values.shape[1:])

    def span_step(state_in, pieces):
        xs_part, in_part, out_part, step_part, decay_part, pos_part, start_part = pieces
        result, state_out, state_weight = ssd_local(xs_part, in_part, out_part, step_part, decay_part, pos_part, start_part, skip_gain)
        result = result + state_term(out_part, state_weight, state_in)
        state_next = state_weight[-1][:, None, None] * state_in + state_out
        return (state_next, result)
    initial = jnp.zeros((MHEADS, MDIM, NSTATE), hidden_in.dtype)
    _, mamba_y = lax.scan(jax.checkpoint(span_step), initial, (blockwise(states_x), blockwise(input_mat), blockwise(output_mat), blockwise(step_size), blockwise(log_decay), blockwise(positions), blockwise(starts)))
    mamba_y = mamba_y.reshape(length, inner_width)
    act_mamba = low(gated_norm(mamba_y, gate_z, inner_gain))
    cos_table, sin_table = rope_tables(positions, HDIM)
    query = low(rotate(query_raw, cos_table, sin_table))
    keys = low(rotate(key_raw, cos_table, sin_table))
    values = low(value_raw)
    attended = attention(query, keys, values, positions, starts)
    act_attn = low(low_back(attended))
    mixer = low_back(jnp.dot(act_mamba, mamba_out, precision=HIGH) + jnp.dot(act_attn, attn_out, precision=HIGH))
    middle = hidden_in + mixer
    act_two = low(rms_scale(middle, ffn_gain))
    gate_up = low_back(jnp.dot(act_two, w_gate_up, precision=HIGH))
    inner = low(swiglu(gate_up[:, :FF], gate_up[:, FF:]))
    return middle + low_back(jnp.dot(inner, w_down, precision=HIGH))

def to_natural(array_in):
    block_count = array_in.shape[1] // BLK
    later = array_in[1].reshape((block_count, BLK) + array_in.shape[2:])[::-1].reshape(array_in.shape[1:])
    return jnp.concatenate([array_in[0], later], axis=0)

def from_natural(array_in):
    middle = array_in.shape[0] // 2
    block_count = middle // BLK
    later = array_in[middle:].reshape((block_count, BLK) + array_in.shape[1:])[::-1].reshape((middle,) + array_in.shape[1:])
    return jnp.stack([array_in[:middle], later])

def reference(tokens, doc_start, cotangent, w_in, w_dt, conv_weight, conv_bias, dt_bias, a_log, skip_gain, inner_gain, mamba_out, attn_out, mixer_gain, ffn_gain, w_gate_up, w_down):
    params = tuple((weight_arr.astype(jnp.float32) for weight_arr in (w_in, w_dt, conv_weight, conv_bias, dt_bias, a_log, skip_gain, inner_gain, mamba_out, attn_out, mixer_gain, ffn_gain, w_gate_up, w_down)))

    def one_sequence(totals, pieces):
        seq_tokens, seq_starts, seq_grad = pieces
        hidden_in = to_natural(seq_tokens).astype(jnp.float32)
        starts = to_natural(seq_starts).astype(jnp.int32)
        grad_out = to_natural(seq_grad).astype(jnp.float32)
        result, pullback = jax.vjp(lambda hidden_val, weight_val: layer(hidden_val, weight_val, starts), hidden_in, params)
        grad_hidden, grad_params = pullback(grad_out)
        totals = jax.tree.map(lambda total_val, new_val: total_val + new_val, totals, grad_params)
        return (totals, (from_natural(result.astype(jnp.bfloat16)), from_natural(grad_hidden)))
    zero_grads = jax.tree.map(jnp.zeros_like, params)
    totals, (mixed, grad_tokens) = lax.scan(one_sequence, zero_grads, (tokens, doc_start, cotangent))
    return (mixed, grad_tokens, totals[0], totals[1], totals[2], totals[3], totals[4], totals[5], totals[6], totals[7], totals[8], totals[9], totals[10], totals[11], totals[12], totals[13])
```

```python
import functools
import math

import jax
import jax.numpy as jnp
from jax import lax
from jax.experimental import pallas as pl
from jax.experimental.pallas import tpu as pltpu
from jax.sharding import PartitionSpec as P

D = 1024
FF = 2048
BLK = 64
HDIM = 64
NSTATE = 128
LOCAL_HEADS = 6
LX = 384
LBC = 256
LCONV = LX + LBC
LPROJ = 1280
EXT = 72
EPS = 1e-05
ROPE_BASE = 100000000000.0
NEG = -1e30
F32 = jnp.float32
BF16 = jnp.bfloat16
NN = ((1,), (0,))
NT = ((1,), (1,))
TN = ((0,), (0,))


def dotf(a, b, dims):
    return lax.dot_general(
        a, b, (dims, ((), ())), precision=lax.Precision.HIGHEST, preferred_element_type=F32
    )


def dotb(a, b, dims):
    return lax.dot_general(
        a.astype(BF16), b.astype(BF16), (dims, ((), ())), preferred_element_type=F32
    )


def iota(shape, dim):
    return lax.broadcasted_iota(jnp.int32, shape, dim)


def sigmoid(v):
    return 1.0 / (1.0 + jnp.exp(-v))


def ssd_prep(ext, dtr, st, base, pv):
    tpos = base + iota((BLK, LCONV), 0)
    stc = jnp.broadcast_to(st[:, :1], (BLK, LCONV))
    pre = jnp.broadcast_to(pv[4:5], (BLK, LCONV))
    for tap in range(4):
        use = (tpos - (3 - tap)) >= stc
        pre = pre + jnp.where(use, pv[tap : tap + 1] * ext[5 + tap : 5 + tap + BLK], 0.0)
    sg = sigmoid(pre)
    xc = pre * sg
    lin = dtr + pv[5:6, :128]
    dt = jnp.maximum(lin, 0.0) + jnp.log1p(jnp.exp(-jnp.abs(lin)))
    ea = jnp.exp(pv[6:7, :128])
    ell = -dt * ea
    tri = (iota((BLK, BLK), 1) <= iota((BLK, BLK), 0)).astype(F32)
    eye = (iota((BLK, BLK), 1) == iota((BLK, BLK), 0)).astype(F32)
    run = dotf(tri, ell, NN)
    run_t = dotf(ell, tri, ((0,), (1,)))
    dt_t = dotf(dt, eye, TN)
    allowed = (iota((BLK, BLK), 1) <= iota((BLK, BLK), 0)) & (
        (base + iota((BLK, BLK), 1)) >= st[:, :BLK]
    )
    sw = jnp.where(st < base, jnp.exp(run), 0.0)
    last_ok = (base + iota((BLK, 128), 0)) >= st[BLK - 1 : BLK]
    fwd_decay = jnp.where(
        last_ok, jnp.exp(jnp.where(last_ok, run[BLK - 1 : BLK] - run, 0.0)), 0.0
    )
    sel = (iota((128, LX), 1) // HDIM == iota((128, LX), 0)).astype(F32)
    return dict(
        pre=pre, sg=sg, xc=xc, lin=lin, dt=dt, ea=ea, ell=ell, run=run, run_t=run_t, dt_t=dt_t,
        allowed=allowed, sw=sw, fd=fwd_decay, fw=fwd_decay * dt, sel=sel, tri=tri, tpos=tpos, stc=stc,
    )


def decay_of(p, h):
    spread = p["run"][:, h : h + 1] - p["run_t"][h : h + 1, :]
    return jnp.where(p["allowed"], jnp.exp(jnp.where(p["allowed"], spread, 0.0)), 0.0)


def to_chunks(state, out_ref, nk, pr, extra):
    for k in range(nk):
        rows = [state[h * HDIM + k * pr : h * HDIM + (k + 1) * pr] for h in range(LOCAL_HEADS)]
        out_ref[0, k, 0] = jnp.concatenate(rows + extra, axis=0).astype(BF16)


def from_chunks(ref, nk, pr):
    parts = [ref[0, k, 0].astype(F32) for k in range(nk)]
    rows = []
    for h in range(LOCAL_HEADS):
        for k in range(nk):
            rows.append(parts[k][h * pr : (h + 1) * pr])
    return jnp.concatenate(rows, axis=0)


def block_base(idx_ref, nctx):
    half = pl.program_id(0) % 2
    i = idx_ref[0]
    return jnp.where(half == 0, i, 2 * nctx - 1 - i) * BLK


def ssd_fwd_kernel(nctx, nk, pr, idx_ref, ext_ref, dtr_ref, st_ref, pv_ref, y_ref, swx_ref, c_ref, s_ref):
    base = block_base(idx_ref, nctx)
    st = st_ref[0]
    p = ssd_prep(ext_ref[0], dtr_ref[0, 8:], st, base, pv_ref[...])
    x = p["xc"][:, :LX]
    bm = p["xc"][:, LX : LX + NSTATE].astype(BF16)
    cm = p["xc"][:, LX + NSTATE :].astype(BF16)
    inter = dotb(cm, bm, NT)
    xb = x.astype(BF16)
    outs = []
    for h in range(LOCAL_HEADS):
        mix = decay_of(p, h) * inter * p["dt_t"][h : h + 1]
        outs.append(dotb(mix, xb[:, h * HDIM : (h + 1) * HDIM], NN))
    y_ref[0] = jnp.concatenate(outs, axis=1) + pv_ref[7:8, :LX] * x
    swx_ref[0] = dotf(p["sw"], p["sel"], NN)
    c_ref[0] = cm
    fwx = dotf(p["fw"], p["sel"], NN)
    state = dotb(fwx * x, bm, TN)
    dec = jnp.where(
        st[BLK - 1 : BLK] < base,
        jnp.broadcast_to(jnp.exp(p["run_t"][:8, BLK - 1 : BLK]), (8, 128)),
        0.0,
    )
    high = dec.astype(BF16).astype(F32)
    to_chunks(state, s_ref, nk, pr, [high, dec - high])


def ssd_out_kernel(nk, pr, y_ref, swx_ref, c_ref, s_ref, z_ref, gain_ref, dep_ref, out_ref, u_ref, ss_ref):
    s_in = from_chunks(s_ref, nk, pr)
    y = y_ref[0] + swx_ref[0] * dotb(c_ref[0], s_in, NT)
    z = z_ref[0]
    u = y * (z * sigmoid(z))
    out_ref[0] = y
    u_ref[0] = (u * gain_ref[...]).astype(BF16)
    ss_ref[0] = jnp.broadcast_to(jnp.sum(u * u, axis=1, keepdims=True), (BLK, 128))


def split_in_kernel(w_ref, out_ref):
    for zz in range(4):
        kv = HDIM * (zz // 2)
        out_ref[zz, :, :LX] = w_ref[:, LX * zz : LX * zz + LX]
        out_ref[zz, :, LX : 2 * LX] = w_ref[:, 1536 + LX * zz : 1536 + LX * zz + LX]
        out_ref[zz, :, 2 * LX : 1024] = w_ref[:, 3072:3328]
        out_ref[zz, :, 1024:1152] = w_ref[:, 3328 + 128 * zz : 3456 + 128 * zz]
        out_ref[zz, :, 1152:1280] = jnp.concatenate(
            [w_ref[:, 3840 + kv : 3904 + kv], w_ref[:, 3968 + kv : 4032 + kv]], axis=1
        )


def split_gate_up_kernel(w_ref, out_ref):
    for zz in range(4):
        out_ref[zz, :, :512] = w_ref[:, 512 * zz : 512 * zz + 512]
        out_ref[zz, :, 512:] = w_ref[:, FF + 512 * zz : FF + 512 * zz + 512]


def total_kernel(n, got_ref, *refs):
    out_ref = refs[-1]

    def step(j, acc):
        return acc + got_ref[j].astype(F32)

    out_ref[...] = lax.fori_loop(1, n, step, got_ref[0].astype(F32))


def leak_kernel(nk, pr, dy_ref, swx_ref, c_ref, out_ref):
    to_chunks(dotb(swx_ref[0] * dy_ref[0], c_ref[0], TN), out_ref, nk, pr, [])


def ssd_bwd_kernel(
    nctx, nk, pr, idx_ref, ext_ref, dtr_ref, st_ref, pv_ref, dy_ref, s_ref, g_ref, *refs
):
    dext_ref, ddt_ref, misc_ref = refs[-3:]
    base = block_base(idx_ref, nctx)
    st = st_ref[0]
    ext = ext_ref[0]
    pv = pv_ref[...]
    p = ssd_prep(ext, dtr_ref[0, 8:], st, base, pv)
    sel = p["sel"]
    x = p["xc"][:, :LX]
    bm = p["xc"][:, LX : LX + NSTATE]
    cm = p["xc"][:, LX + NSTATE :]
    bmb, cmb, xb = bm.astype(BF16), cm.astype(BF16), x.astype(BF16)
    dy = dy_ref[0]
    dyb = dy.astype(BF16)
    s_in = from_chunks(s_ref, nk, pr)
    g_out = from_chunks(g_ref, nk, pr)
    s_inb, g_outb = s_in.astype(BF16), g_out.astype(BF16)
    inter = dotb(cmb, bmb, NT)
    swx = dotf(p["sw"], sel, NN)
    fwx = dotf(p["fw"], sel, NN)
    skip = pv[7:8, :LX]
    lane = iota((BLK, 128), 1)
    d_inter = jnp.zeros((BLK, BLK), F32)
    drun = jnp.zeros((BLK, 128), F32)
    dx_parts = []
    col_rows = []
    for h in range(LOCAL_HEADS):
        sl = slice(h * HDIM, (h + 1) * HDIM)
        dec = decay_of(p, h)
        dt_row = p["dt_t"][h : h + 1]
        dec_inter = dec * inter
        d_mix = dotb(dyb[:, sl], xb[:, sl], NT)
        dx_parts.append(dotb(dec_inter * dt_row, dyb[:, sl], TN))
        d_inter = d_inter + d_mix * dec * dt_row
        f = d_mix * dec_inter
        row = jnp.sum(f * dt_row, axis=1, keepdims=True)
        drun = drun + jnp.where(lane == h, row, 0.0)
        col_rows.append(jnp.sum(f, axis=0, keepdims=True))
    col_rows.append(jnp.zeros((2, BLK), F32))
    cols = jnp.concatenate(col_rows, axis=0)
    pick = (iota((8, 128), 0) == iota((8, 128), 1)).astype(F32)
    col = dotf(cols, pick, TN)
    ddt = col
    drun = drun - p["dt"] * col
    dx = jnp.concatenate(dx_parts, axis=1) + skip * dy
    dcm = dotb(d_inter, bmb, NN)
    dbm = dotb(d_inter, cmb, TN)
    swdy = swx * dy
    yin = dotb(cmb, s_inb, NT)
    drun = drun + dotf(swdy * yin, sel, NT)
    dcm = dcm + dotb(swdy, s_inb, NN)
    back = dotb(bmb, g_outb, NT)
    dbm = dbm + dotb(fwx * x, g_outb, NN)
    dx = dx + fwx * back
    dfw = dotf(x * back, sel, NT)
    ddt = ddt + dfw * p["fd"]
    tail = dfw * p["fw"]
    drun = drun - tail
    carry = jnp.sum(s_in * g_out, axis=1, keepdims=True)
    sel_t = (iota((LX, 128), 0) // HDIM == iota((LX, 128), 1)).astype(F32)
    last = jnp.sum(tail, axis=0, keepdims=True) + p["sw"][BLK - 1 : BLK] * jnp.sum(
        carry * sel_t, axis=0, keepdims=True
    )
    drun = drun + jnp.where(iota((BLK, 128), 0) == BLK - 1, last, 0.0)
    dell = dotf(p["tri"], drun, TN)
    ddt = ddt - p["ea"] * dell
    ddtraw = ddt * sigmoid(p["lin"])
    ddtraw = jnp.where(lane < LOCAL_HEADS, ddtraw, 0.0)
    zero8 = jnp.zeros((8, 128), F32)
    ddt_ref[0] = jnp.concatenate([zero8, ddtraw], axis=0).astype(BF16)
    dxc = jnp.concatenate([dx, dbm, dcm], axis=1)
    dpre = dxc * (p["sg"] * (1.0 + p["pre"] * (1.0 - p["sg"])))
    dext = jnp.zeros((EXT, LCONV), F32)
    rows = []
    for tap in range(4):
        use = (p["tpos"] - (3 - tap)) >= p["stc"]
        term = jnp.where(use, dpre, 0.0)
        rows.append(jnp.sum(term * ext[5 + tap : 5 + tap + BLK], axis=0, keepdims=True))
        term = term * pv[tap : tap + 1]
        pieces = [jnp.zeros((5 + tap, LCONV), F32), term]
        if tap < 3:
            pieces.append(jnp.zeros((3 - tap, LCONV), F32))
        dext = dext + jnp.concatenate(pieces, axis=0)
    dext_ref[0] = dext.astype(BF16)
    rows.append(jnp.sum(dpre, axis=0, keepdims=True))
    pad = jnp.zeros((1, LCONV - LX), F32)
    rows.append(jnp.concatenate([jnp.sum(dy * x, axis=0, keepdims=True), pad], axis=1))
    pad = jnp.zeros((1, LCONV - 128), F32)
    rows.append(jnp.concatenate([jnp.sum(ddtraw, axis=0, keepdims=True), pad], axis=1))
    rows.append(jnp.concatenate([jnp.sum(dell * p["ell"], axis=0, keepdims=True), pad], axis=1))
    misc_ref[0] = jnp.concatenate(rows, axis=0)


def scan_kernel(reverse, n, pr, st_ref, dec_ref, dep_ref, out_ref):
    rows = LOCAL_HEADS * pr

    def step(j, half, s):
        out_ref[j, half] = s.astype(BF16)
        d = dec_ref[j, half, rows : rows + 16].astype(F32)
        d = d[:LOCAL_HEADS] + d[8 : 8 + LOCAL_HEADS]
        d = jnp.broadcast_to(d[:, None, :], (LOCAL_HEADS, pr, 128)).reshape(rows, 128)
        return d * s + st_ref[j, half, :rows].astype(F32)

    first, second = (1, 0) if reverse else (0, 1)
    s = jnp.zeros((rows, 128), F32)
    s = lax.fori_loop(0, n, lambda j, s: step(j, first, s), s)
    lax.fori_loop(0, n, lambda j, s: step(n - 1 - j, second, s), s)


def unit_of(u, gi):
    if u < 4:
        return 1, 0, u
    is_a = u < 5 + gi
    rowset = jnp.where(is_a, 0, 1)
    half = jnp.where(is_a, 0, 1)
    return rowset, half, jnp.where(is_a, u - 4, u - 5)


def unit_mask(nctx, gs, i, rowset, half, g, st):
    shape = (2 * BLK, gs * BLK)
    row = iota(shape, 0) % BLK
    col = iota(shape, 1)
    qpos = jnp.where(rowset == 0, i, 2 * nctx - 1 - i) * BLK + row
    block = g * gs + col // BLK
    kpos = jnp.where(half == 0, block, 2 * nctx - 1 - block) * BLK + col % BLK
    return (kpos <= qpos) & (kpos >= st)


def attn_fwd_kernel(nctx, gs, idx_ref, q_ref, kv_ref, st_ref, dep_a, dep_b, o_ref, lse_ref, s_ref, m_ref, l_ref, acc_ref):
    i = idx_ref[0]
    gi = i // gs
    m_ref[...] = jnp.full(m_ref.shape, NEG, F32)
    l_ref[...] = jnp.zeros(l_ref.shape, F32)
    acc_ref[...] = jnp.zeros(acc_ref.shape, F32)
    for u in range(9):
        rowset, half, g = unit_of(u, gi)
        kv = kv_ref[pl.ds(g * gs, gs), 0, half].reshape(gs * BLK, 128)
        s = dotb(q_ref[0, rowset], kv[:, :HDIM], NT)
        ok = unit_mask(nctx, gs, i, rowset, half, g, st_ref[0, rowset, :, :1])
        s = jnp.where(ok, s, NEG)
        s_ref[u] = s
        m_ref[rowset] = jnp.maximum(m_ref[rowset], jnp.max(s, axis=1, keepdims=True))
    for u in range(9):
        rowset, half, g = unit_of(u, gi)
        kv = kv_ref[pl.ds(g * gs, gs), 0, half].reshape(gs * BLK, 128)
        w = jnp.exp(s_ref[u] - m_ref[rowset, :, :1])
        l_ref[rowset] = l_ref[rowset] + jnp.sum(w, axis=1, keepdims=True)
        acc_ref[rowset] = acc_ref[rowset] + dotb(w, kv[:, HDIM:], NN)
    o_ref[0] = acc_ref[...] / l_ref[:, :, :HDIM]
    lse_ref[0] = m_ref[...] + jnp.log(l_ref[...])


def attn_bwd_kernel(
    nctx, gs, idx_ref, q_ref, kv_ref, st_ref, o_ref, lse_ref, do_ref, dq_ref, dkv_ref, del_ref, acc_ref
):
    i = idx_ref[0]
    gi = i // gs
    acc_ref[...] = jnp.zeros(acc_ref.shape, F32)
    dq_ref[...] = jnp.zeros(dq_ref.shape, F32)
    delta = jnp.sum(do_ref[0].astype(F32) * o_ref[0], axis=2, keepdims=True)
    del_ref[...] = jnp.broadcast_to(delta, del_ref.shape)
    for u in range(9):
        rowset, half, g = unit_of(u, gi)
        kv = kv_ref[pl.ds(g * gs, gs), 0, half].reshape(gs * BLK, 128)
        q = q_ref[0, rowset]
        do = do_ref[0, rowset]
        s = dotb(q, kv[:, :HDIM], NT)
        ok = unit_mask(nctx, gs, i, rowset, half, g, st_ref[0, rowset, :, :1])
        prob = jnp.exp(jnp.where(ok, s, NEG) - lse_ref[0, rowset, :, :1])
        dp = dotb(do, kv[:, HDIM:], NT)
        ds = (prob * (dp - del_ref[rowset, :, :1])).astype(BF16)
        dkv = jnp.concatenate([dotb(ds, q, TN), dotb(prob, do, TN)], axis=1)
        acc_ref[half, g] = acc_ref[half, g] + dkv
        dq_ref[0, rowset] = dq_ref[0, rowset] + dotb(ds, kv[:, :HDIM], NN)
    dq_ref[...] = dq_ref[...] * (HDIM**-0.5)
    for g in range(4):
        for half in range(2):
            dkv_ref[g * gs : (g + 1) * gs, 0, half] = (
                acc_ref[half, g].astype(BF16).reshape(gs, BLK, 128)
            )


def spec(shape, index):
    return pl.BlockSpec(shape, index)


def per_pair(shape):
    return pl.BlockSpec((1,) + shape, lambda j: (j,) + (0,) * len(shape))


def whole(shape):
    return pl.BlockSpec(shape, lambda *j: (0,) * len(shape))


def chunk_spec(nk, rows):
    return pl.BlockSpec((1, nk, 1, rows, 128), lambda j: (j // 2, 0, j % 2, 0, 0))


ANY = pl.BlockSpec(memory_space=pl.ANY)
VMEM = pl.BlockSpec(memory_space=pltpu.VMEM)
SMEM = pl.BlockSpec(memory_space=pltpu.SMEM)
PARAMS = pltpu.CompilerParams(vmem_limit_bytes=48 * 1024 * 1024)


def cost(flops, moved, trans=0):
    return pl.CostEstimate(flops=flops // 1000, bytes_accessed=moved // 1000, transcendentals=0)


def sds(shape, dtype):
    return jax.ShapeDtypeStruct(shape, dtype)


def exchange(parts, axis):
    return lax.all_to_all(parts, axis, 0, 0, tiled=True)


def spread(part, axis):
    return exchange(jnp.broadcast_to(part[None], (lax.axis_size(axis),) + part.shape), axis)


def shifts():
    return [(k, [(a, (a + k) % 4) for a in range(4)]) for k in (1, 2, 3)]


def ring_exchange(parts, z):
    out = parts
    for k, perm in shifts():
        sent = lax.dynamic_index_in_dim(parts, (z + k) % 4, 0, keepdims=False)
        got = lax.ppermute(sent, "fsdp", perm)
        out = lax.dynamic_update_index_in_dim(out, got, (z - k) % 4, 0)
    return out


def ring_spread(part, z):
    out = jnp.broadcast_to(part[None], (4,) + part.shape)
    for k, perm in shifts():
        got = lax.ppermute(part, "fsdp", perm)
        out = lax.dynamic_update_index_in_dim(out, got, (z - k) % 4, 0)
    return out


def ring_sum(rows, z):
    parts = rows.astype(BF16).reshape((4, -1) + rows.shape[1:])
    total = lax.dynamic_index_in_dim(parts, z, 0, keepdims=False).astype(F32)
    for k, perm in shifts():
        sent = lax.dynamic_index_in_dim(parts, (z + k) % 4, 0, keepdims=False)
        total = total + lax.ppermute(sent, "fsdp", perm).astype(F32)
    return total


def as_rows(column):
    high = lax.reduce_precision(column, 8, 7)
    pair = jnp.stack([high, column - high], axis=-2).astype(BF16)
    pads = [(0, 0)] * (pair.ndim - 2) + [(0, 14), (0, D - 128)]
    return jnp.pad(pair, pads)


def from_rows(rows):
    pair = rows[..., :2, :128].astype(F32)
    return pair[..., 0, :] + pair[..., 1, :]


def rms_of(v):
    return lax.rsqrt(jnp.mean(v * v, axis=-1, keepdims=True) + EPS)


def rms_back(v, r, dn):
    n = v * r
    return r * (dn - n * jnp.mean(dn * n, axis=-1, keepdims=True))


def turn(values, cosine, sine):
    a, b = values[..., : HDIM // 2], values[..., HDIM // 2 :]
    return jnp.concatenate([a * cosine - b * sine, b * cosine + a * sine], axis=-1)


def matmul(a, b, dims=NN):
    return lax.dot_general(a, b, (dims, ((), ())), preferred_element_type=F32)


def per_device(
    tokens,
    doc_start,
    cotangent,
    w_in,
    w_dt,
    conv_weight,
    conv_bias,
    dt_bias,
    a_log,
    skip_gain,
    inner_gain,
    mamba_out,
    attn_out,
    mixer_gain,
    ffn_gain,
    w_gate_up,
    w_down,
):
    nctx = lax.axis_size("ctx")
    i = lax.axis_index("ctx")
    z = lax.axis_index("fsdp")
    nk = nctx // 4
    pr = HDIM // nk
    gs = nctx // 4
    rpc = 256 // nctx
    idx = i.astype(jnp.int32).reshape(1)
    last_device = i == nctx - 1
    up = [(a, a + 1) for a in range(nctx - 1)]
    down = [(b, a) for a, b in up]

    send_in = pl.pallas_call(
        split_in_kernel,
        in_specs=[VMEM],
        out_specs=VMEM,
        out_shape=sds((4, 256, LPROJ), BF16),
        compiler_params=PARAMS,
        cost_estimate=cost(0, 5 * 10**6),
        name="split_in",
    )(w_in)
    send_gu = pl.pallas_call(
        split_gate_up_kernel,
        in_specs=[VMEM],
        out_specs=VMEM,
        out_shape=sds((4, 256, 1024), BF16),
        compiler_params=PARAMS,
        cost_estimate=cost(0, 4 * 10**6),
        name="split_gate_up",
    )(w_gate_up)
    tok = tokens[0]
    tails = tok[:, BLK - 3 :, :]
    halo_first = lax.ppermute(tails[0], "ctx", up)
    halo_second = lax.ppermute(tails[1], "ctx", down)
    halo = jnp.stack([halo_first, jnp.where(last_device, tails[0], halo_second)])
    starts_own = doc_start[0]
    flat = jnp.concatenate(
        [
            w_dt.reshape(-1),
            conv_weight.reshape(-1),
            conv_bias,
            mixer_gain,
            ffn_gain,
            (starts_own // 64).astype(BF16).reshape(-1),
            (starts_own % 64).astype(BF16).reshape(-1),
        ]
    )
    flat = jnp.pad(flat, (0, 10 * D - flat.shape[0])).reshape(2, 5, D)
    wide = spread(jnp.concatenate([flat, halo, tok], axis=1), "fsdp")
    own_in = exchange(send_in, "fsdp").reshape(D, LPROJ)
    own_gu = ring_exchange(send_gu, z).reshape(D, 1024)
    grad_own = cotangent[0].reshape(128, D)
    grad_all = ring_spread(grad_own, z).reshape(512, D)
    flat = wide[:, :, :5, :].reshape(4, 10 * D)
    full_dt = flat[:, :6144].reshape(D, 24)
    own_dt = jnp.pad(lax.dynamic_slice_in_dim(full_dt, 6 * z, 6, axis=1), ((0, 0), (0, 122)))
    full_conv = flat[:, 6144:7936].reshape(4, 4, 448).transpose(1, 0, 2).reshape(4, 1792)
    full_bias = flat[:, 7936:8384].reshape(1, 1792)
    full_taps = jnp.concatenate([full_conv, full_bias], axis=0).astype(F32)
    mixer_scale = flat[:, 8384:8640].reshape(D).astype(F32)
    ffn_scale = flat[:, 8640:8896].reshape(D).astype(F32)
    starts = (
        flat[:, 8896:9024].astype(jnp.int32) * 64 + flat[:, 9024:9152].astype(jnp.int32)
    ).reshape(8, BLK)
    own_taps = jnp.concatenate(
        [lax.dynamic_slice_in_dim(full_taps, LX * z, LX, axis=1), full_taps[:, 1536:]], axis=1
    )

    def lanes(v):
        return jnp.pad(v.astype(F32), (0, LCONV - v.shape[0]))[None]

    pv = jnp.concatenate(
        [own_taps, lanes(dt_bias), lanes(a_log), lanes(jnp.repeat(skip_gain, HDIM))], axis=0
    )
    inner_scale = inner_gain.astype(F32)

    rows = 8 * EXT
    hidden_all = wide.reshape(rows, D).astype(F32)
    norm_one = hidden_all * rms_of(hidden_all)
    act_one = (norm_one * mixer_scale).astype(BF16)
    projected = matmul(act_one, own_in).reshape(8, EXT, LPROJ)
    raw_dt = matmul(act_one, own_dt).reshape(8, EXT, 128)
    gate_z = projected[:, 8:, :LX]
    conv_ext = projected[:, :, LX : LX + LCONV]

    blocks = jnp.stack([i, 2 * nctx - 1 - i])
    positions = blocks[:, None] * BLK + jnp.arange(BLK, dtype=jnp.int32)[None, :]
    freq = jnp.exp(
        jnp.arange(HDIM // 2, dtype=F32) * (-2.0 * math.log(ROPE_BASE) / HDIM)
    )
    angle = positions.astype(F32)[:, :, None] * freq
    cosine, sine = jnp.cos(angle), jnp.sin(angle)
    tables = (cosine[None, :, :, None, :], sine[None, :, :, None, :])
    query = projected[:, 8:, 1024:1152].reshape(4, 2, BLK, 2, HDIM)
    query = turn(query, *tables).astype(BF16) * jnp.asarray(HDIM**-0.5, BF16)
    query = query.transpose(0, 1, 3, 2, 4).reshape(4, 2, 2 * BLK, HDIM)
    key = projected[:, 8:, 1152:1216].reshape(4, 2, BLK, 1, HDIM)
    key = turn(key, *tables).astype(BF16).reshape(4, 2, BLK, HDIM)
    value = projected[:, 8:, 1216:1280].astype(BF16).reshape(4, 2, BLK, HDIM)
    kv_own = jnp.concatenate([key, value], axis=-1)

    st_wide = jnp.broadcast_to(starts[:, :, None], (8, BLK, 128))
    srows = LOCAL_HEADS * pr
    ssd_in = (idx, conv_ext, raw_dt, st_wide, pv)
    ssd_in_specs = [
        SMEM,
        per_pair((EXT, LCONV)),
        per_pair((EXT, 128)),
        per_pair((BLK, 128)),
        whole((8, LCONV)),
    ]
    y_local, swx, c_mat, state_out = pl.pallas_call(
        functools.partial(ssd_fwd_kernel, nctx, nk, pr),
        grid=(8,),
        in_specs=ssd_in_specs,
        out_specs=[
            per_pair((BLK, LX)),
            per_pair((BLK, LX)),
            per_pair((BLK, 128)),
            chunk_spec(nk, srows + 16),
        ],
        out_shape=[
            sds((8, BLK, LX), F32),
            sds((8, BLK, LX), F32),
            sds((8, BLK, 128), BF16),
            sds((4, nk, 2, srows + 16, 128), BF16),
        ],
        compiler_params=PARAMS,
        cost_estimate=cost(2 * 10**9, 6 * 10**6),
        name="ssd_fwd",
    )(*ssd_in)
    got = exchange(state_out.reshape(nctx, 2, srows + 16, 128), "ctx")
    kv_all = lax.all_gather(kv_own, "ctx")

    def chain(reverse, terms, after):
        return pl.pallas_call(
            functools.partial(scan_kernel, reverse, nctx, pr),
            in_specs=[VMEM, VMEM, ANY],
            out_specs=VMEM,
            out_shape=sds((nctx, 2, srows, 128), BF16),
            compiler_params=PARAMS,
            cost_estimate=cost(10**7, 3 * 10**6),
            name="chain",
        )(terms, got, after)

    entry = exchange(chain(False, got, kv_all), "ctx").reshape(4, nk, 2, srows, 128)

    st_rows = jnp.broadcast_to(
        starts.reshape(4, 2, 1, BLK, 1), (4, 2, 2, BLK, 128)
    ).reshape(4, 2, 2 * BLK, 128)
    row_spec = pl.BlockSpec((1, 2, 2 * BLK, HDIM), lambda s: (s, 0, 0, 0))
    wide_spec = pl.BlockSpec((1, 2, 2 * BLK, 128), lambda s: (s, 0, 0, 0))
    kv_spec = pl.BlockSpec((nctx, 1, 2, BLK, 128), lambda s: (0, s, 0, 0, 0))
    attn_o, lse = pl.pallas_call(
        functools.partial(attn_fwd_kernel, nctx, gs),
        grid=(4,),
        in_specs=[SMEM, row_spec, kv_spec, wide_spec, ANY, ANY],
        out_specs=[row_spec, wide_spec],
        out_shape=[sds((4, 2, 2 * BLK, HDIM), F32), sds((4, 2, 2 * BLK, 128), F32)],
        scratch_shapes=[
            pltpu.VMEM((9, 2 * BLK, gs * BLK), F32),
            pltpu.VMEM((2, 2 * BLK, 128), F32),
            pltpu.VMEM((2, 2 * BLK, 128), F32),
            pltpu.VMEM((2, 2 * BLK, HDIM), F32),
        ],
        compiler_params=PARAMS,
        cost_estimate=cost(4 * 10**9, 8 * 10**6, 2 * 10**6),
        name="attn_fwd",
    )(idx, query, kv_all, st_rows, own_gu, grad_all)
    act_attn = (
        attn_o.reshape(4, 2, 2, BLK, HDIM).transpose(0, 1, 3, 2, 4).reshape(512, 128).astype(BF16)
    )

    mamba_y, scaled_u, squares = pl.pallas_call(
        functools.partial(ssd_out_kernel, nk, pr),
        grid=(8,),
        in_specs=[
            per_pair((BLK, LX)),
            per_pair((BLK, LX)),
            per_pair((BLK, 128)),
            chunk_spec(nk, srows),
            per_pair((BLK, LX)),
            whole((1, LX)),
            ANY,
        ],
        out_specs=[per_pair((BLK, LX)), per_pair((BLK, LX)), per_pair((BLK, 128))],
        out_shape=[
            sds((8, BLK, LX), F32),
            sds((8, BLK, LX), BF16),
            sds((8, BLK, 128), F32),
        ],
        compiler_params=PARAMS,
        cost_estimate=cost(10**9, 6 * 10**6),
        name="ssd_out",
    )(y_local, swx, c_mat, entry, gate_z, inner_scale[None], attn_o)

    def gather_sum(part_rows):
        got_rows = exchange(part_rows.astype(BF16).reshape((4, -1) + part_rows.shape[1:]), "fsdp")
        return jnp.sum(got_rows.astype(F32), axis=0)

    attn_mid = ring_sum(matmul(act_attn, attn_out), z)
    scaled_part = matmul(scaled_u.reshape(512, LX), mamba_out).astype(BF16).reshape(4, 128, D)
    square_rows = as_rows(squares[:, :, 0].reshape(4, 128))
    got_part = exchange(jnp.concatenate([scaled_part, square_rows], axis=1), "fsdp")
    scaled_mid = jnp.sum(got_part[:, :128].astype(F32), axis=0)
    square_sum = jnp.sum(from_rows(got_part[:, 128:]), axis=0)
    own_r = lax.rsqrt(square_sum.reshape(128, 1) * (1.0 / 1536) + EPS)
    mamba_mid = scaled_mid * own_r
    middle = tok.reshape(128, D).astype(F32) + mamba_mid + attn_mid
    mid_r = rms_of(middle)
    norm_two = middle * mid_r
    def spread_rows(values, column):
        sent = jnp.concatenate([values.astype(BF16), as_rows(column.reshape(128))], axis=0)
        got_rows = spread(sent, "fsdp").reshape(4, 144, D)
        return got_rows[:, :128].reshape(512, D), from_rows(got_rows[:, 128:]).reshape(512, 1)

    act_two, inner_r = spread_rows(norm_two * ffn_scale, own_r)
    y_flat = mamba_y.reshape(512, LX)
    z_flat = gate_z.reshape(512, LX)
    z_sig = sigmoid(z_flat)
    z_silu = z_flat * z_sig
    norm_in = y_flat * z_silu * inner_r
    act_mamba = (norm_in * inner_scale).astype(BF16)

    gate_up = matmul(act_two, own_gu)
    gate_val, up_val = gate_up[:, :512], gate_up[:, 512:]
    gate_sig = sigmoid(gate_val)
    gate_silu = gate_val * gate_sig
    inner = (gate_silu * up_val).astype(BF16)
    grad_inner = matmul(grad_all, w_down, NT)
    grad_gate = grad_inner * up_val * (gate_sig * (1.0 + gate_val * (1.0 - gate_sig)))
    grad_gu = jnp.concatenate([grad_gate, grad_inner * gate_silu], axis=1).astype(BF16)
    grad_act_two = gather_sum(matmul(grad_gu, own_gu, NT))
    mixed = (middle + ring_sum(matmul(inner, w_down), z)).astype(BF16).reshape(1, 2, BLK, D)
    grad_down = matmul(inner, grad_all, TN).astype(BF16)
    grad_gate_up = matmul(act_two, grad_gu, TN).astype(BF16)
    grad_ffn_gain = jnp.sum(grad_act_two * norm_two, axis=0)
    grad_middle = grad_own.astype(F32) + rms_back(middle, mid_r, grad_act_two * ffn_scale)
    own_mix = grad_middle.astype(BF16)
    own_dots = jnp.sum(own_mix.astype(F32) * mamba_mid, axis=1) * (1.0 / 1536)
    grad_mix, dots = spread_rows(own_mix, own_dots)

    grad_m = matmul(grad_mix, mamba_out, NT)
    grad_n = grad_m * inner_scale
    grad_attn = matmul(grad_mix, attn_out, NT).astype(BF16)
    grad_attn = (
        grad_attn.reshape(4, 2, BLK, 2, HDIM).transpose(0, 1, 3, 2, 4).reshape(4, 2, 2 * BLK, HDIM)
    )
    grad_mamba_out = matmul(act_mamba, grad_mix, TN).astype(BF16)
    grad_attn_out = matmul(act_attn, grad_mix, TN).astype(BF16)
    totals = lax.psum((grad_gate_up, grad_down, grad_mamba_out, grad_attn_out), "ctx")
    total_gate_up, total_down, total_mamba_out, total_attn_out = totals
    total_gate_up = ring_exchange(total_gate_up.reshape(4, 256, 1024), z)
    total_gate_up = total_gate_up.reshape(4, 256, 2, 512).transpose(1, 2, 0, 3).reshape(256, 4096)
    grad_inner_gain = jnp.sum(grad_m * norm_in, axis=0)
    grad_u = inner_r * (grad_n - norm_in * dots)
    grad_y = (grad_u * z_silu).reshape(8, BLK, LX)
    grad_z = grad_u * y_flat * (z_sig * (1.0 + z_flat * (1.0 - z_sig)))

    leak = pl.pallas_call(
        functools.partial(leak_kernel, nk, pr),
        grid=(8,),
        in_specs=[per_pair((BLK, LX)), per_pair((BLK, LX)), per_pair((BLK, 128))],
        out_specs=chunk_spec(nk, srows),
        out_shape=sds((4, nk, 2, srows, 128), BF16),
        compiler_params=PARAMS,
        cost_estimate=cost(10**9, 4 * 10**6),
        name="leak",
    )(grad_y, swx, c_mat)
    got_leak = exchange(leak.reshape(nctx, 2, srows, 128), "ctx")
    grad_query, grad_kv = pl.pallas_call(
        functools.partial(attn_bwd_kernel, nctx, gs),
        grid=(4,),
        in_specs=[SMEM, row_spec, kv_spec, wide_spec, row_spec, wide_spec, row_spec],
        out_specs=[row_spec, kv_spec],
        out_shape=[sds((4, 2, 2 * BLK, HDIM), F32), sds((nctx, 4, 2, BLK, 128), BF16)],
        scratch_shapes=[
            pltpu.VMEM((2, 2 * BLK, 128), F32),
            pltpu.VMEM((2, 4, gs * BLK, 128), F32),
        ],
        compiler_params=PARAMS,
        cost_estimate=cost(8 * 10**9, 16 * 10**6, 2 * 10**6),
        name="attn_bwd",
    )(idx, query, kv_all, st_rows, attn_o, lse, grad_attn)
    grad_exit = exchange(chain(True, got_leak, grad_kv), "ctx").reshape(4, nk, 2, srows, 128)
    grad_kv = pl.pallas_call(
        functools.partial(total_kernel, nctx),
        in_specs=[VMEM] + [ANY] * 4,
        out_specs=VMEM,
        out_shape=sds((4, 2, BLK, 128), F32),
        compiler_params=PARAMS,
        cost_estimate=cost(2 * 10**6, 4 * 10**6),
        name="total_kv",
    )(exchange(grad_kv, "ctx"), *totals)
    back = (tables[0], -tables[1])
    grad_key = turn(grad_kv[..., :HDIM].reshape(4, 2, BLK, 1, HDIM), *back).reshape(8, BLK, HDIM)
    grad_value = grad_kv[..., HDIM:].reshape(8, BLK, HDIM)
    grad_query = grad_query.reshape(4, 2, 2, BLK, HDIM).transpose(0, 1, 3, 2, 4)
    grad_query = turn(grad_query, *back).reshape(8, BLK, 128)

    grad_ext, grad_dt, misc = pl.pallas_call(
        functools.partial(ssd_bwd_kernel, nctx, nk, pr),
        grid=(8,),
        in_specs=ssd_in_specs
        + [per_pair((BLK, LX)), chunk_spec(nk, srows), chunk_spec(nk, srows)],
        out_specs=[per_pair((EXT, LCONV)), per_pair((EXT, 128)), per_pair((8, LCONV))],
        out_shape=[
            sds((8, EXT, LCONV), BF16),
            sds((8, EXT, 128), BF16),
            sds((8, 8, LCONV), F32),
        ],
        compiler_params=PARAMS,
        cost_estimate=cost(4 * 10**9, 8 * 10**6),
        name="ssd_bwd",
    )(*ssd_in, grad_y, entry, grad_exit)

    def lead(v):
        return jnp.pad(v.astype(BF16), ((0, 0), (8, 0), (0, 0)))

    grad_proj = jnp.concatenate(
        [
            lead(grad_z.reshape(8, BLK, LX)),
            grad_ext,
            lead(jnp.concatenate([grad_query, grad_key, grad_value], axis=-1)),
        ],
        axis=-1,
    ).reshape(rows, LPROJ)
    grad_dt = grad_dt.reshape(rows, 128)
    grad_act = matmul(grad_proj, own_in, NT) + matmul(grad_dt, own_dt, NT)

    got_act = ring_sum(grad_act, z).reshape(2, EXT, D)
    halo_back = got_act[:, 5:8].astype(BF16)
    to_first = lax.ppermute(halo_back[0], "ctx", down).astype(F32)
    to_second = lax.ppermute(jnp.where(last_device, 0.0, halo_back[1]), "ctx", up).astype(F32)
    to_first = to_first + jnp.where(last_device, got_act[1, 5:8], 0.0)
    tail_add = jnp.pad(jnp.stack([to_first, to_second]), ((0, 0), (BLK - 3, 0), (0, 0)))
    own_act = (got_act[:, 8:] + tail_add).reshape(128, D)
    hidden = tok.reshape(128, D).astype(F32)
    grad_tokens = grad_middle + rms_back(hidden, rms_of(hidden), own_act * mixer_scale)
    grad_tokens = grad_tokens.reshape(1, 2, BLK, D)

    def permuted(v):
        return v.reshape(4, nctx, rpc, -1).swapaxes(0, 1)

    grad_in = matmul(act_one, grad_proj, TN).astype(BF16)
    grad_dtw = matmul(act_one, grad_dt, TN)
    misc = jnp.sum(misc, axis=0)
    grad_skip = jnp.sum(misc[5, :LX].reshape(LOCAL_HEADS, HDIM), axis=1)
    small = jnp.concatenate(
        [misc[:5].reshape(-1), misc[6, :6], misc[7, :6], grad_skip, grad_inner_gain]
    )
    small = jnp.pad(small, (0, 3840 - small.shape[0])).reshape(1, 256, 15)
    small = jnp.broadcast_to(small, (4, 256, 15)).reshape(D, 15)
    grad_mixer_gain = jnp.sum(grad_act * norm_one, axis=0)
    extras = jnp.concatenate(
        [
            grad_dtw[:, :6],
            grad_mixer_gain[:, None],
            grad_ffn_gain[:, None],
            small,
            jnp.zeros((D, 105), F32),
        ],
        axis=1,
    ).astype(BF16)
    sent = permuted(jnp.concatenate([grad_in, extras], axis=1))
    summed = pl.pallas_call(
        functools.partial(total_kernel, nctx),
        in_specs=[VMEM],
        out_specs=VMEM,
        out_shape=sds((4, rpc, LPROJ + 128), F32),
        compiler_params=PARAMS,
        cost_estimate=cost(2 * 10**6, 4 * 10**6),
        name="total",
    )(exchange(sent, "ctx"))
    owned = exchange(summed, "fsdp")

    def side(lo, hi):
        return jnp.concatenate([owned[zz, :, lo:hi] for zz in range(4)], axis=1)

    def shared(lo, hi):
        return jnp.concatenate(
            [owned[0, :, lo:hi] + owned[1, :, lo:hi], owned[2, :, lo:hi] + owned[3, :, lo:hi]], axis=1
        )

    final = jnp.concatenate(
        [
            side(0, 384),
            side(384, 768),
            jnp.sum(owned[:, :, 768:1024], axis=0),
            side(1024, 1152),
            shared(1152, 1216),
            shared(1216, 1280),
            side(1280, 1304),
            jnp.zeros((rpc, 32), F32),
        ],
        axis=1,
    ).astype(BF16)
    final = spread(final, "ctx").reshape(256, 4224).astype(F32)
    total_in = final[:, :4096]
    extra = final[:, 4096:4192].reshape(256, 4, 24)
    total_dt = extra[:, :, :6].reshape(256, 24)
    total_mixer = jnp.sum(extra[:, :, 6], axis=1)
    total_ffn = jnp.sum(extra[:, :, 7], axis=1)
    small = extra[:, :, 8:23].transpose(1, 0, 2).reshape(4, 3840)
    taps = small[:, :3200].reshape(4, 5, LCONV)
    taps = jnp.concatenate(
        [
            taps[:, :, :LX].transpose(1, 0, 2).reshape(5, 1536),
            jnp.sum(taps[:, :, LX:], axis=0),
        ],
        axis=1,
    )
    taps = lax.dynamic_slice_in_dim(taps, 448 * z, 448, axis=1)
    mine = lax.dynamic_slice_in_dim(small, z, 1, axis=0)[0]
    return (
        mixed,
        grad_tokens,
        total_in,
        total_dt,
        taps[:4],
        taps[4],
        mine[3200:3206],
        mine[3206:3212],
        mine[3212:3218],
        mine[3218:3602],
        total_mamba_out.astype(F32),
        total_attn_out.astype(F32),
        total_mixer,
        total_ffn,
        total_gate_up.astype(F32),
        total_down.astype(F32),
    )


def solution(mesh):
    row = P("fsdp", None)
    vec = P("fsdp")
    act = P("fsdp", None, "ctx", None)
    return jax.shard_map(
        per_device,
        mesh=mesh,
        in_specs=(
            act, P("fsdp", None, "ctx"), act, row, row, P(None, "fsdp"), vec, vec, vec, vec, vec,
            row, row, vec, vec, row, row,
        ),
        out_specs=(
            act, act, row, row, P(None, "fsdp"), vec, vec, vec, vec, vec, row, row, vec, vec, row, row,
        ),
        check_vma=False,
    )
```

```python
import functools
import math

import jax
import jax.numpy as jnp
from jax import lax
from jax.experimental import pallas as pl
from jax.experimental.pallas import tpu as pltpu
from jax.sharding import PartitionSpec as P

D = 1024
FF = 2048
BLK = 64
HDIM = 64
NSTATE = 128
LOCAL_HEADS = 6
LX = 384
LBC = 256
LCONV = LX + LBC
LPROJ = 1280
EXT = 72
EPS = 1e-05
ROPE_BASE = 100000000000.0
NEG = -1e30
F32 = jnp.float32
BF16 = jnp.bfloat16
NN = ((1,), (0,))
NT = ((1,), (1,))
TN = ((0,), (0,))


def dotf(a, b, dims):
    return lax.dot_general(
        a, b, (dims, ((), ())), precision=lax.Precision.HIGHEST, preferred_element_type=F32
    )


def dotb(a, b, dims):
    return lax.dot_general(
        a.astype(BF16), b.astype(BF16), (dims, ((), ())), preferred_element_type=F32
    )


def iota(shape, dim):
    return lax.broadcasted_iota(jnp.int32, shape, dim)


def sigmoid(v):
    return 1.0 / (1.0 + jnp.exp(-v))


def ssd_prep(ext, dtr, st, base, pv):
    tpos = base + iota((BLK, LCONV), 0)
    stc = jnp.broadcast_to(st[:, :1], (BLK, LCONV))
    pre = jnp.broadcast_to(pv[4:5], (BLK, LCONV))
    for tap in range(4):
        use = (tpos - (3 - tap)) >= stc
        pre = pre + jnp.where(use, pv[tap : tap + 1] * ext[5 + tap : 5 + tap + BLK], 0.0)
    sg = sigmoid(pre)
    xc = pre * sg
    lin = dtr + pv[5:6, :128]
    dt = jnp.maximum(lin, 0.0) + jnp.log1p(jnp.exp(-jnp.abs(lin)))
    ea = jnp.exp(pv[6:7, :128])
    ell = -dt * ea
    tri = (iota((BLK, BLK), 1) <= iota((BLK, BLK), 0)).astype(F32)
    eye = (iota((BLK, BLK), 1) == iota((BLK, BLK), 0)).astype(F32)
    run = dotf(tri, ell, NN)
    run_t = dotf(ell, tri, ((0,), (1,)))
    dt_t = dotf(dt, eye, TN)
    allowed = (iota((BLK, BLK), 1) <= iota((BLK, BLK), 0)) & (
        (base + iota((BLK, BLK), 1)) >= st[:, :BLK]
    )
    sw = jnp.where(st < base, jnp.exp(run), 0.0)
    last_ok = (base + iota((BLK, 128), 0)) >= st[BLK - 1 : BLK]
    fwd_decay = jnp.where(
        last_ok, jnp.exp(jnp.where(last_ok, run[BLK - 1 : BLK] - run, 0.0)), 0.0
    )
    sel = (iota((128, LX), 1) // HDIM == iota((128, LX), 0)).astype(F32)
    return dict(
        pre=pre, sg=sg, xc=xc, lin=lin, dt=dt, ea=ea, ell=ell, run=run, run_t=run_t, dt_t=dt_t,
        allowed=allowed, sw=sw, fd=fwd_decay, fw=fwd_decay * dt, sel=sel, tri=tri, tpos=tpos, stc=stc,
    )


def decay_of(p, h):
    spread = p["run"][:, h : h + 1] - p["run_t"][h : h + 1, :]
    return jnp.where(p["allowed"], jnp.exp(jnp.where(p["allowed"], spread, 0.0)), 0.0)


def to_chunks(state, out_ref, nk, pr, extra):
    for k in range(nk):
        rows = [state[h * HDIM + k * pr : h * HDIM + (k + 1) * pr] for h in range(LOCAL_HEADS)]
        out_ref[0, k, 0] = jnp.concatenate(rows + extra, axis=0).astype(BF16)


def from_chunks(ref, nk, pr):
    parts = [ref[0, k, 0].astype(F32) for k in range(nk)]
    rows = []
    for h in range(LOCAL_HEADS):
        for k in range(nk):
            rows.append(parts[k][h * pr : (h + 1) * pr])
    return jnp.concatenate(rows, axis=0)


def block_base(idx_ref, nctx):
    half = pl.program_id(0) % 2
    i = idx_ref[0]
    return jnp.where(half == 0, i, 2 * nctx - 1 - i) * BLK


def ssd_fwd_kernel(nctx, nk, pr, idx_ref, ext_ref, dtr_ref, st_ref, pv_ref, y_ref, swx_ref, c_ref, s_ref):
    base = block_base(idx_ref, nctx)
    st = st_ref[0]
    p = ssd_prep(ext_ref[0], dtr_ref[0, 8:], st, base, pv_ref[...])
    x = p["xc"][:, :LX]
    bm = p["xc"][:, LX : LX + NSTATE].astype(BF16)
    cm = p["xc"][:, LX + NSTATE :].astype(BF16)
    inter = dotb(cm, bm, NT)
    xb = x.astype(BF16)
    outs = []
    for h in range(LOCAL_HEADS):
        mix = decay_of(p, h) * inter * p["dt_t"][h : h + 1]
        outs.append(dotb(mix, xb[:, h * HDIM : (h + 1) * HDIM], NN))
    y_ref[0] = jnp.concatenate(outs, axis=1) + pv_ref[7:8, :LX] * x
    swx_ref[0] = dotf(p["sw"], p["sel"], NN)
    c_ref[0] = cm
    fwx = dotf(p["fw"], p["sel"], NN)
    state = dotb(fwx * x, bm, TN)
    dec = jnp.where(
        st[BLK - 1 : BLK] < base,
        jnp.broadcast_to(jnp.exp(p["run_t"][:8, BLK - 1 : BLK]), (8, 128)),
        0.0,
    )
    high = dec.astype(BF16).astype(F32)
    to_chunks(state, s_ref, nk, pr, [high, dec - high])


def ssd_out_kernel(nk, pr, y_ref, swx_ref, c_ref, s_ref, z_ref, gain_ref, dep_ref, out_ref, u_ref, ss_ref):
    s_in = from_chunks(s_ref, nk, pr)
    y = y_ref[0] + swx_ref[0] * dotb(c_ref[0], s_in, NT)
    z = z_ref[0]
    u = y * (z * sigmoid(z))
    out_ref[0] = y
    u_ref[0] = (u * gain_ref[...]).astype(BF16)
    ss_ref[0] = jnp.broadcast_to(jnp.sum(u * u, axis=1, keepdims=True), (BLK, 128))


def split_in_kernel(w_ref, out_ref):
    for zz in range(4):
        kv = HDIM * (zz // 2)
        out_ref[zz, :, :LX] = w_ref[:, LX * zz : LX * zz + LX]
        out_ref[zz, :, LX : 2 * LX] = w_ref[:, 1536 + LX * zz : 1536 + LX * zz + LX]
        out_ref[zz, :, 2 * LX : 1024] = w_ref[:, 3072:3328]
        out_ref[zz, :, 1024:1152] = w_ref[:, 3328 + 128 * zz : 3456 + 128 * zz]
        out_ref[zz, :, 1152:1280] = jnp.concatenate(
            [w_ref[:, 3840 + kv : 3904 + kv], w_ref[:, 3968 + kv : 4032 + kv]], axis=1
        )


def split_gate_up_kernel(w_ref, out_ref):
    for zz in range(4):
        out_ref[zz, :, :512] = w_ref[:, 512 * zz : 512 * zz + 512]
        out_ref[zz, :, 512:] = w_ref[:, FF + 512 * zz : FF + 512 * zz + 512]


def total_kernel(n, got_ref, dep_ref, out_ref):
    def step(j, acc):
        return acc + got_ref[j].astype(F32)

    out_ref[...] = lax.fori_loop(1, n, step, got_ref[0].astype(F32))


def pack_kernel(nj, rj, kin_ref, gin_ref, kex_ref, gex_ref, gu_ref, o_ref, out_ref):
    for a in range(4):
        part = (kin_ref[a].astype(F32) + gin_ref[a].astype(F32)).astype(BF16)
        out_ref[:, a, :, :LPROJ] = part.reshape(nj, rj, LPROJ)
        part = (kex_ref[a].astype(F32) + gex_ref[a].astype(F32)).astype(BF16)
        out_ref[:, a, :, LPROJ:1408] = part.reshape(nj, rj, 128)
        out_ref[:, a, :, 1408:2432] = gu_ref[a].reshape(nj, rj, 1024)
    out_ref[:, :, :, 2432:] = o_ref[...].reshape(nj, 4, rj, 1024)


def assemble_kernel(owned_ref, o_ref, out_ref):
    def put(lo, value):
        out_ref[:, lo : lo + value.shape[1]] = value.astype(BF16)

    shared = owned_ref[0, :, 768:1024]
    for zz in range(4):
        put(LX * zz, owned_ref[zz, :, :LX])
        put(1536 + LX * zz, owned_ref[zz, :, LX : 2 * LX])
        put(3328 + 128 * zz, owned_ref[zz, :, 1024:1152])
        put(4096 + 512 * zz, owned_ref[zz, :, 1408:1920])
        put(6144 + 512 * zz, owned_ref[zz, :, 1920:2432])
        put(8320 + 1024 * zz, o_ref[zz])
        if zz > 0:
            shared = shared + owned_ref[zz, :, 768:1024]
    put(3072, shared)
    first = owned_ref[0, :, 1152:1280] + owned_ref[1, :, 1152:1280]
    second = owned_ref[2, :, 1152:1280] + owned_ref[3, :, 1152:1280]
    put(3840, jnp.concatenate([first[:, :HDIM], second[:, :HDIM]], axis=1))
    put(3968, jnp.concatenate([first[:, HDIM:], second[:, HDIM:]], axis=1))
    extras = [owned_ref[zz, :, 1280:1304] for zz in range(4)]
    extras.append(jnp.zeros((extras[0].shape[0], 32), F32))
    put(8192, jnp.concatenate(extras, axis=1))


def unpack_kernel(nj, rj, core_ref, mine_ref, other_ref, in_ref, gu_ref, ex_ref, down_ref, mo_ref, ao_ref):
    half = pl.program_id(0)
    core = core_ref[0]

    def write(src):
        in_ref[...] = src[:, :, :4096].reshape(128, 4096).astype(F32)
        gu_ref[...] = src[:, :, 4096:8192].reshape(128, 4096).astype(F32)
        ex_ref[...] = src[:, :, 8192:8320].reshape(128, 128).astype(F32)
        for j in range(nj):
            for a in range(4):
                row = j * 4 * rj + a * rj
                part = src[j, :, 8320 + 1024 * a : 9344 + 1024 * a].astype(F32)

                @pl.when(half == 0)
                def _():
                    down_ref[row : row + rj] = part

                @pl.when(half == 1)
                def _():
                    if row < 384:
                        mo_ref[row : row + rj] = part
                    else:
                        ao_ref[row - 384 : row - 384 + rj] = part

    @pl.when(half == core)
    def _():
        write(mine_ref)

    @pl.when(half != core)
    def _():
        write(other_ref)


def leak_kernel(nk, pr, dy_ref, swx_ref, c_ref, out_ref):
    to_chunks(dotb(swx_ref[0] * dy_ref[0], c_ref[0], TN), out_ref, nk, pr, [])


def ssd_bwd_kernel(
    nctx, nk, pr, idx_ref, ext_ref, dtr_ref, st_ref, pv_ref, dy_ref, s_ref, g_ref, *refs
):
    dext_ref, ddt_ref, misc_ref = refs[-3:]
    base = block_base(idx_ref, nctx)
    st = st_ref[0]
    ext = ext_ref[0]
    pv = pv_ref[...]
    p = ssd_prep(ext, dtr_ref[0, 8:], st, base, pv)
    sel = p["sel"]
    x = p["xc"][:, :LX]
    bm = p["xc"][:, LX : LX + NSTATE]
    cm = p["xc"][:, LX + NSTATE :]
    bmb, cmb, xb = bm.astype(BF16), cm.astype(BF16), x.astype(BF16)
    dy = dy_ref[0]
    dyb = dy.astype(BF16)
    s_in = from_chunks(s_ref, nk, pr)
    g_out = from_chunks(g_ref, nk, pr)
    s_inb, g_outb = s_in.astype(BF16), g_out.astype(BF16)
    inter = dotb(cmb, bmb, NT)
    swx = dotf(p["sw"], sel, NN)
    fwx = dotf(p["fw"], sel, NN)
    skip = pv[7:8, :LX]
    lane = iota((BLK, 128), 1)
    d_inter = jnp.zeros((BLK, BLK), F32)
    drun = jnp.zeros((BLK, 128), F32)
    dx_parts = []
    col_rows = []
    for h in range(LOCAL_HEADS):
        sl = slice(h * HDIM, (h + 1) * HDIM)
        dec = decay_of(p, h)
        dt_row = p["dt_t"][h : h + 1]
        dec_inter = dec * inter
        d_mix = dotb(dyb[:, sl], xb[:, sl], NT)
        dx_parts.append(dotb(dec_inter * dt_row, dyb[:, sl], TN))
        d_inter = d_inter + d_mix * dec * dt_row
        f = d_mix * dec_inter
        row = jnp.sum(f * dt_row, axis=1, keepdims=True)
        drun = drun + jnp.where(lane == h, row, 0.0)
        col_rows.append(jnp.sum(f, axis=0, keepdims=True))
    col_rows.append(jnp.zeros((2, BLK), F32))
    cols = jnp.concatenate(col_rows, axis=0)
    pick = (iota((8, 128), 0) == iota((8, 128), 1)).astype(F32)
    col = dotf(cols, pick, TN)
    ddt = col
    drun = drun - p["dt"] * col
    dx = jnp.concatenate(dx_parts, axis=1) + skip * dy
    dcm = dotb(d_inter, bmb, NN)
    dbm = dotb(d_inter, cmb, TN)
    swdy = swx * dy
    yin = dotb(cmb, s_inb, NT)
    drun = drun + dotf(swdy * yin, sel, NT)
    dcm = dcm + dotb(swdy, s_inb, NN)
    back = dotb(bmb, g_outb, NT)
    dbm = dbm + dotb(fwx * x, g_outb, NN)
    dx = dx + fwx * back
    dfw = dotf(x * back, sel, NT)
    ddt = ddt + dfw * p["fd"]
    tail = dfw * p["fw"]
    drun = drun - tail
    carry = jnp.sum(s_in * g_out, axis=1, keepdims=True)
    sel_t = (iota((LX, 128), 0) // HDIM == iota((LX, 128), 1)).astype(F32)
    last = jnp.sum(tail, axis=0, keepdims=True) + p["sw"][BLK - 1 : BLK] * jnp.sum(
        carry * sel_t, axis=0, keepdims=True
    )
    drun = drun + jnp.where(iota((BLK, 128), 0) == BLK - 1, last, 0.0)
    dell = dotf(p["tri"], drun, TN)
    ddt = ddt - p["ea"] * dell
    ddtraw = ddt * sigmoid(p["lin"])
    ddtraw = jnp.where(lane < LOCAL_HEADS, ddtraw, 0.0)
    zero8 = jnp.zeros((8, 128), F32)
    ddt_ref[0] = jnp.concatenate([zero8, ddtraw], axis=0).astype(BF16)
    dxc = jnp.concatenate([dx, dbm, dcm], axis=1)
    dpre = dxc * (p["sg"] * (1.0 + p["pre"] * (1.0 - p["sg"])))
    dext = jnp.zeros((EXT, LCONV), F32)
    rows = []
    for tap in range(4):
        use = (p["tpos"] - (3 - tap)) >= p["stc"]
        term = jnp.where(use, dpre, 0.0)
        rows.append(jnp.sum(term * ext[5 + tap : 5 + tap + BLK], axis=0, keepdims=True))
        term = term * pv[tap : tap + 1]
        pieces = [jnp.zeros((5 + tap, LCONV), F32), term]
        if tap < 3:
            pieces.append(jnp.zeros((3 - tap, LCONV), F32))
        dext = dext + jnp.concatenate(pieces, axis=0)
    dext_ref[0] = dext.astype(BF16)
    rows.append(jnp.sum(dpre, axis=0, keepdims=True))
    pad = jnp.zeros((1, LCONV - LX), F32)
    rows.append(jnp.concatenate([jnp.sum(dy * x, axis=0, keepdims=True), pad], axis=1))
    pad = jnp.zeros((1, LCONV - 128), F32)
    rows.append(jnp.concatenate([jnp.sum(ddtraw, axis=0, keepdims=True), pad], axis=1))
    rows.append(jnp.concatenate([jnp.sum(dell * p["ell"], axis=0, keepdims=True), pad], axis=1))
    misc_ref[0] = jnp.concatenate(rows, axis=0)


def scan_kernel(reverse, n, pr, st_ref, dec_ref, *refs):
    out_ref = refs[-1]
    rows = LOCAL_HEADS * pr

    def step(j, half, s):
        out_ref[j, half] = s.astype(BF16)
        d = dec_ref[j, half, rows : rows + 16].astype(F32)
        d = d[:LOCAL_HEADS] + d[8 : 8 + LOCAL_HEADS]
        d = jnp.broadcast_to(d[:, None, :], (LOCAL_HEADS, pr, 128)).reshape(rows, 128)
        return d * s + st_ref[j, half, :rows].astype(F32)

    first, second = (1, 0) if reverse else (0, 1)
    s = jnp.zeros((rows, 128), F32)
    s = lax.fori_loop(0, n, lambda j, s: step(j, first, s), s)
    lax.fori_loop(0, n, lambda j, s: step(n - 1 - j, second, s), s)


def unit_of(u, gi):
    if u < 4:
        return 1, 0, u
    is_a = u < 5 + gi
    rowset = jnp.where(is_a, 0, 1)
    half = jnp.where(is_a, 0, 1)
    return rowset, half, jnp.where(is_a, u - 4, u - 5)


def unit_mask(nctx, gs, i, rowset, half, g, st):
    shape = (2 * BLK, gs * BLK)
    row = iota(shape, 0) % BLK
    col = iota(shape, 1)
    qpos = jnp.where(rowset == 0, i, 2 * nctx - 1 - i) * BLK + row
    block = g * gs + col // BLK
    kpos = jnp.where(half == 0, block, 2 * nctx - 1 - block) * BLK + col % BLK
    return (kpos <= qpos) & (kpos >= st)


def attn_fwd_kernel(nctx, gs, idx_ref, q_ref, kv_ref, st_ref, dep_a, dep_b, o_ref, lse_ref, s_ref, m_ref, l_ref, acc_ref):
    i = idx_ref[0]
    gi = i // gs
    m_ref[...] = jnp.full(m_ref.shape, NEG, F32)
    l_ref[...] = jnp.zeros(l_ref.shape, F32)
    acc_ref[...] = jnp.zeros(acc_ref.shape, F32)
    for u in range(9):
        rowset, half, g = unit_of(u, gi)
        kv = kv_ref[pl.ds(g * gs, gs), 0, half].reshape(gs * BLK, 128)
        s = dotb(q_ref[0, rowset], kv[:, :HDIM], NT)
        ok = unit_mask(nctx, gs, i, rowset, half, g, st_ref[0, rowset, :, :1])
        s = jnp.where(ok, s, NEG)
        s_ref[u] = s
        m_ref[rowset] = jnp.maximum(m_ref[rowset], jnp.max(s, axis=1, keepdims=True))
    for u in range(9):
        rowset, half, g = unit_of(u, gi)
        kv = kv_ref[pl.ds(g * gs, gs), 0, half].reshape(gs * BLK, 128)
        w = jnp.exp(s_ref[u] - m_ref[rowset, :, :1])
        l_ref[rowset] = l_ref[rowset] + jnp.sum(w, axis=1, keepdims=True)
        acc_ref[rowset] = acc_ref[rowset] + dotb(w, kv[:, HDIM:], NN)
    o_ref[0] = acc_ref[...] / l_ref[:, :, :HDIM]
    lse_ref[0] = m_ref[...] + jnp.log(l_ref[...])


def attn_bwd_kernel(
    nctx, gs, idx_ref, q_ref, kv_ref, st_ref, o_ref, lse_ref, do_ref, dq_ref, dkv_ref, del_ref, acc_ref
):
    i = idx_ref[0]
    gi = i // gs
    acc_ref[...] = jnp.zeros(acc_ref.shape, F32)
    dq_ref[...] = jnp.zeros(dq_ref.shape, F32)
    delta = jnp.sum(do_ref[0].astype(F32) * o_ref[0], axis=2, keepdims=True)
    del_ref[...] = jnp.broadcast_to(delta, del_ref.shape)
    for u in range(9):
        rowset, half, g = unit_of(u, gi)
        kv = kv_ref[pl.ds(g * gs, gs), 0, half].reshape(gs * BLK, 128)
        q = q_ref[0, rowset]
        do = do_ref[0, rowset]
        s = dotb(q, kv[:, :HDIM], NT)
        ok = unit_mask(nctx, gs, i, rowset, half, g, st_ref[0, rowset, :, :1])
        prob = jnp.exp(jnp.where(ok, s, NEG) - lse_ref[0, rowset, :, :1])
        dp = dotb(do, kv[:, HDIM:], NT)
        ds = (prob * (dp - del_ref[rowset, :, :1])).astype(BF16)
        dkv = jnp.concatenate([dotb(ds, q, TN), dotb(prob, do, TN)], axis=1)
        acc_ref[half, g] = acc_ref[half, g] + dkv
        dq_ref[0, rowset] = dq_ref[0, rowset] + dotb(ds, kv[:, :HDIM], NN)
    dq_ref[...] = dq_ref[...] * (HDIM**-0.5)
    for g in range(4):
        for half in range(2):
            dkv_ref[g * gs : (g + 1) * gs, 0, half] = (
                acc_ref[half, g].astype(BF16).reshape(gs, BLK, 128)
            )


def spec(shape, index):
    return pl.BlockSpec(shape, index)


def per_pair(shape):
    return pl.BlockSpec((1,) + shape, lambda j: (j,) + (0,) * len(shape))


def whole(shape):
    return pl.BlockSpec(shape, lambda *j: (0,) * len(shape))


def chunk_spec(nk, rows):
    return pl.BlockSpec((1, nk, 1, rows, 128), lambda j: (j // 2, 0, j % 2, 0, 0))


ANY = pl.BlockSpec(memory_space=pl.ANY)
VMEM = pl.BlockSpec(memory_space=pltpu.VMEM)
SMEM = pl.BlockSpec(memory_space=pltpu.SMEM)
PARAMS = pltpu.CompilerParams(vmem_limit_bytes=48 * 1024 * 1024)


def cost(flops, moved, trans=0):
    return pl.CostEstimate(flops=flops // 1000, bytes_accessed=moved // 1000, transcendentals=0)


def sds(shape, dtype):
    return jax.ShapeDtypeStruct(shape, dtype)


def exchange(parts, axis):
    return lax.all_to_all(parts, axis, 0, 0, tiled=True)


def spread(part, axis):
    return exchange(jnp.broadcast_to(part[None], (lax.axis_size(axis),) + part.shape), axis)


def shifts():
    return [(k, [(a, (a + k) % 4) for a in range(4)]) for k in (1, 2, 3)]


def ring_exchange(parts, z):
    out = parts
    for k, perm in shifts():
        sent = lax.dynamic_index_in_dim(parts, (z + k) % 4, 0, keepdims=False)
        got = lax.ppermute(sent, "fsdp", perm)
        out = lax.dynamic_update_index_in_dim(out, got, (z - k) % 4, 0)
    return out


def ring_spread(part, z):
    out = jnp.broadcast_to(part[None], (4,) + part.shape)
    for k, perm in shifts():
        got = lax.ppermute(part, "fsdp", perm)
        out = lax.dynamic_update_index_in_dim(out, got, (z - k) % 4, 0)
    return out


def ring_sum(rows, z):
    parts = rows.astype(BF16).reshape((4, -1) + rows.shape[1:])
    total = lax.dynamic_index_in_dim(parts, z, 0, keepdims=False).astype(F32)
    for k, perm in shifts():
        sent = lax.dynamic_index_in_dim(parts, (z + k) % 4, 0, keepdims=False)
        total = total + lax.ppermute(sent, "fsdp", perm).astype(F32)
    return total


def as_rows(column):
    high = lax.reduce_precision(column, 8, 7)
    pair = jnp.stack([high, column - high], axis=-2).astype(BF16)
    pads = [(0, 0)] * (pair.ndim - 2) + [(0, 14), (0, D - 128)]
    return jnp.pad(pair, pads)


def from_rows(rows):
    pair = rows[..., :2, :128].astype(F32)
    return pair[..., 0, :] + pair[..., 1, :]


def rms_of(v):
    return lax.rsqrt(jnp.mean(v * v, axis=-1, keepdims=True) + EPS)


def rms_back(v, r, dn):
    n = v * r
    return r * (dn - n * jnp.mean(dn * n, axis=-1, keepdims=True))


def turn(values, cosine, sine):
    a, b = values[..., : HDIM // 2], values[..., HDIM // 2 :]
    return jnp.concatenate([a * cosine - b * sine, b * cosine + a * sine], axis=-1)


def matmul(a, b, dims=NN):
    return lax.dot_general(a, b, (dims, ((), ())), preferred_element_type=F32)


def per_device(
    tokens,
    doc_start,
    cotangent,
    w_in,
    w_dt,
    conv_weight,
    conv_bias,
    dt_bias,
    a_log,
    skip_gain,
    inner_gain,
    mamba_out,
    attn_out,
    mixer_gain,
    ffn_gain,
    w_gate_up,
    w_down,
):
    nctx = lax.axis_size("ctx")
    i = lax.axis_index("ctx")
    z = lax.axis_index("fsdp")
    nk = nctx // 4
    pr = HDIM // nk
    gs = nctx // 4
    rpc = 256 // nctx
    idx = i.astype(jnp.int32).reshape(1)
    last_device = i == nctx - 1
    up = [(a, a + 1) for a in range(nctx - 1)]
    down = [(b, a) for a, b in up]

    send_in = pl.pallas_call(
        split_in_kernel,
        in_specs=[VMEM],
        out_specs=VMEM,
        out_shape=sds((4, 256, LPROJ), BF16),
        compiler_params=PARAMS,
        cost_estimate=cost(0, 5 * 10**6),
        name="split_in",
    )(w_in)
    send_gu = pl.pallas_call(
        split_gate_up_kernel,
        in_specs=[VMEM],
        out_specs=VMEM,
        out_shape=sds((4, 256, 1024), BF16),
        compiler_params=PARAMS,
        cost_estimate=cost(0, 4 * 10**6),
        name="split_gate_up",
    )(w_gate_up)
    tok = tokens[0]
    tails = tok[:, BLK - 3 :, :]
    halo_first = lax.ppermute(tails[0], "ctx", up)
    halo_second = lax.ppermute(tails[1], "ctx", down)
    halo = jnp.stack([halo_first, jnp.where(last_device, tails[0], halo_second)])
    starts_own = doc_start[0]
    flat = jnp.concatenate(
        [
            w_dt.reshape(-1),
            conv_weight.reshape(-1),
            conv_bias,
            mixer_gain,
            ffn_gain,
            (starts_own // 64).astype(BF16).reshape(-1),
            (starts_own % 64).astype(BF16).reshape(-1),
        ]
    )
    flat = jnp.pad(flat, (0, 10 * D - flat.shape[0])).reshape(2, 5, D)
    wide = ring_spread(jnp.concatenate([flat, halo, tok], axis=1), z)
    own_in = exchange(send_in, "fsdp").reshape(D, LPROJ)
    own_gu = ring_exchange(send_gu, z).reshape(D, 1024)
    grad_own = cotangent[0].reshape(128, D)
    grad_all = ring_spread(grad_own, z).reshape(512, D)
    flat = wide[:, :, :5, :].reshape(4, 10 * D)
    full_dt = flat[:, :6144].reshape(D, 24)
    own_dt = jnp.pad(lax.dynamic_slice_in_dim(full_dt, 6 * z, 6, axis=1), ((0, 0), (0, 122)))
    full_conv = flat[:, 6144:7936].reshape(4, 4, 448).transpose(1, 0, 2).reshape(4, 1792)
    full_bias = flat[:, 7936:8384].reshape(1, 1792)
    full_taps = jnp.concatenate([full_conv, full_bias], axis=0).astype(F32)
    mixer_scale = flat[:, 8384:8640].reshape(D).astype(F32)
    ffn_scale = flat[:, 8640:8896].reshape(D).astype(F32)
    starts = (
        flat[:, 8896:9024].astype(jnp.int32) * 64 + flat[:, 9024:9152].astype(jnp.int32)
    ).reshape(8, BLK)
    own_taps = jnp.concatenate(
        [lax.dynamic_slice_in_dim(full_taps, LX * z, LX, axis=1), full_taps[:, 1536:]], axis=1
    )

    def lanes(v):
        return jnp.pad(v.astype(F32), (0, LCONV - v.shape[0]))[None]

    pv = jnp.concatenate(
        [own_taps, lanes(dt_bias), lanes(a_log), lanes(jnp.repeat(skip_gain, HDIM))], axis=0
    )
    inner_scale = inner_gain.astype(F32)

    rows = 8 * EXT
    hidden_all = wide.reshape(rows, D).astype(F32)
    norm_one = hidden_all * rms_of(hidden_all)
    act_one = (norm_one * mixer_scale).astype(BF16)
    projected = matmul(act_one, own_in).reshape(8, EXT, LPROJ)
    raw_dt = matmul(act_one, own_dt).reshape(8, EXT, 128)
    gate_z = projected[:, 8:, :LX]
    conv_ext = projected[:, :, LX : LX + LCONV]

    blocks = jnp.stack([i, 2 * nctx - 1 - i])
    positions = blocks[:, None] * BLK + jnp.arange(BLK, dtype=jnp.int32)[None, :]
    freq = jnp.exp(
        jnp.arange(HDIM // 2, dtype=F32) * (-2.0 * math.log(ROPE_BASE) / HDIM)
    )
    angle = positions.astype(F32)[:, :, None] * freq
    cosine, sine = jnp.cos(angle), jnp.sin(angle)
    tables = (cosine[None, :, :, None, :], sine[None, :, :, None, :])
    query = projected[:, 8:, 1024:1152].reshape(4, 2, BLK, 2, HDIM)
    query = turn(query, *tables).astype(BF16) * jnp.asarray(HDIM**-0.5, BF16)
    query = query.transpose(0, 1, 3, 2, 4).reshape(4, 2, 2 * BLK, HDIM)
    key = projected[:, 8:, 1152:1216].reshape(4, 2, BLK, 1, HDIM)
    key = turn(key, *tables).astype(BF16).reshape(4, 2, BLK, HDIM)
    value = projected[:, 8:, 1216:1280].astype(BF16).reshape(4, 2, BLK, HDIM)
    kv_own = jnp.concatenate([key, value], axis=-1)

    st_wide = jnp.broadcast_to(starts[:, :, None], (8, BLK, 128))
    srows = LOCAL_HEADS * pr
    ssd_in = (idx, conv_ext, raw_dt, st_wide, pv)
    ssd_in_specs = [
        SMEM,
        per_pair((EXT, LCONV)),
        per_pair((EXT, 128)),
        per_pair((BLK, 128)),
        whole((8, LCONV)),
    ]
    y_local, swx, c_mat, state_out = pl.pallas_call(
        functools.partial(ssd_fwd_kernel, nctx, nk, pr),
        grid=(8,),
        in_specs=ssd_in_specs,
        out_specs=[
            per_pair((BLK, LX)),
            per_pair((BLK, LX)),
            per_pair((BLK, 128)),
            chunk_spec(nk, srows + 16),
        ],
        out_shape=[
            sds((8, BLK, LX), F32),
            sds((8, BLK, LX), F32),
            sds((8, BLK, 128), BF16),
            sds((4, nk, 2, srows + 16, 128), BF16),
        ],
        compiler_params=PARAMS,
        cost_estimate=cost(2 * 10**9, 6 * 10**6),
        name="ssd_fwd",
    )(*ssd_in)
    got = exchange(state_out.reshape(nctx, 2, srows + 16, 128), "ctx")
    kv_all = lax.all_gather(kv_own, "ctx")

    def chain(reverse, terms, *after):
        return pl.pallas_call(
            functools.partial(scan_kernel, reverse, nctx, pr),
            in_specs=[VMEM, VMEM] + [ANY] * len(after),
            out_specs=VMEM,
            out_shape=sds((nctx, 2, srows, 128), BF16),
            compiler_params=PARAMS,
            cost_estimate=cost(10**7, 3 * 10**6),
            name="chain",
        )(terms, got, *after)

    entry = exchange(chain(False, got), "ctx").reshape(4, nk, 2, srows, 128)

    st_rows = jnp.broadcast_to(
        starts.reshape(4, 2, 1, BLK, 1), (4, 2, 2, BLK, 128)
    ).reshape(4, 2, 2 * BLK, 128)
    row_spec = pl.BlockSpec((1, 2, 2 * BLK, HDIM), lambda s: (s, 0, 0, 0))
    wide_spec = pl.BlockSpec((1, 2, 2 * BLK, 128), lambda s: (s, 0, 0, 0))
    kv_spec = pl.BlockSpec((nctx, 1, 2, BLK, 128), lambda s: (0, s, 0, 0, 0))
    attn_o, lse = pl.pallas_call(
        functools.partial(attn_fwd_kernel, nctx, gs),
        grid=(4,),
        in_specs=[SMEM, row_spec, kv_spec, wide_spec, ANY, ANY],
        out_specs=[row_spec, wide_spec],
        out_shape=[sds((4, 2, 2 * BLK, HDIM), F32), sds((4, 2, 2 * BLK, 128), F32)],
        scratch_shapes=[
            pltpu.VMEM((9, 2 * BLK, gs * BLK), F32),
            pltpu.VMEM((2, 2 * BLK, 128), F32),
            pltpu.VMEM((2, 2 * BLK, 128), F32),
            pltpu.VMEM((2, 2 * BLK, HDIM), F32),
        ],
        compiler_params=PARAMS,
        cost_estimate=cost(4 * 10**9, 8 * 10**6, 2 * 10**6),
        name="attn_fwd",
    )(idx, query, kv_all, st_rows, own_gu, grad_all)
    act_attn = (
        attn_o.reshape(4, 2, 2, BLK, HDIM).transpose(0, 1, 3, 2, 4).reshape(512, 128).astype(BF16)
    )

    mamba_y, scaled_u, squares = pl.pallas_call(
        functools.partial(ssd_out_kernel, nk, pr),
        grid=(8,),
        in_specs=[
            per_pair((BLK, LX)),
            per_pair((BLK, LX)),
            per_pair((BLK, 128)),
            chunk_spec(nk, srows),
            per_pair((BLK, LX)),
            whole((1, LX)),
            ANY,
        ],
        out_specs=[per_pair((BLK, LX)), per_pair((BLK, LX)), per_pair((BLK, 128))],
        out_shape=[
            sds((8, BLK, LX), F32),
            sds((8, BLK, LX), BF16),
            sds((8, BLK, 128), F32),
        ],
        compiler_params=PARAMS,
        cost_estimate=cost(10**9, 6 * 10**6),
        name="ssd_out",
    )(y_local, swx, c_mat, entry, gate_z, inner_scale[None], attn_o)

    def gather_sum(part_rows):
        got_rows = exchange(part_rows.astype(BF16).reshape((4, -1) + part_rows.shape[1:]), "fsdp")
        return jnp.sum(got_rows.astype(F32), axis=0)

    attn_mid = ring_sum(matmul(act_attn, attn_out), z)
    scaled_part = matmul(scaled_u.reshape(512, LX), mamba_out).astype(BF16).reshape(4, 128, D)
    square_rows = as_rows(squares[:, :, 0].reshape(4, 128))
    got_part = exchange(jnp.concatenate([scaled_part, square_rows], axis=1), "fsdp")
    scaled_mid = jnp.sum(got_part[:, :128].astype(F32), axis=0)
    square_sum = jnp.sum(from_rows(got_part[:, 128:]), axis=0)
    own_r = lax.rsqrt(square_sum.reshape(128, 1) * (1.0 / 1536) + EPS)
    mamba_mid = scaled_mid * own_r
    middle = tok.reshape(128, D).astype(F32) + mamba_mid + attn_mid
    mid_r = rms_of(middle)
    norm_two = middle * mid_r
    def spread_rows(values, column):
        sent = jnp.concatenate([values.astype(BF16), as_rows(column.reshape(128))], axis=0)
        got_rows = spread(sent, "fsdp").reshape(4, 144, D)
        return got_rows[:, :128].reshape(512, D), from_rows(got_rows[:, 128:]).reshape(512, 1)

    act_two, inner_r = spread_rows(norm_two * ffn_scale, own_r)
    y_flat = mamba_y.reshape(512, LX)
    z_flat = gate_z.reshape(512, LX)
    z_sig = sigmoid(z_flat)
    z_silu = z_flat * z_sig
    norm_in = y_flat * z_silu * inner_r
    act_mamba = (norm_in * inner_scale).astype(BF16)

    gate_up = matmul(act_two, own_gu)
    gate_val, up_val = gate_up[:, :512], gate_up[:, 512:]
    gate_sig = sigmoid(gate_val)
    gate_silu = gate_val * gate_sig
    inner = (gate_silu * up_val).astype(BF16)
    grad_inner = matmul(grad_all, w_down, NT)
    grad_gate = grad_inner * up_val * (gate_sig * (1.0 + gate_val * (1.0 - gate_sig)))
    grad_gu = jnp.concatenate([grad_gate, grad_inner * gate_silu], axis=1).astype(BF16)
    grad_act_two = gather_sum(matmul(grad_gu, own_gu, NT))
    mixed = (middle + ring_sum(matmul(inner, w_down), z)).astype(BF16).reshape(1, 2, BLK, D)
    grad_down = matmul(inner, grad_all, TN).astype(BF16)
    grad_gate_up = matmul(act_two, grad_gu, TN).astype(BF16)
    grad_ffn_gain = jnp.sum(grad_act_two * norm_two, axis=0)
    grad_middle = grad_own.astype(F32) + rms_back(middle, mid_r, grad_act_two * ffn_scale)
    own_mix = grad_middle.astype(BF16)
    own_dots = jnp.sum(own_mix.astype(F32) * mamba_mid, axis=1) * (1.0 / 1536)
    grad_mix, dots = spread_rows(own_mix, own_dots)

    grad_m = matmul(grad_mix, mamba_out, NT)
    grad_n = grad_m * inner_scale
    grad_attn = matmul(grad_mix, attn_out, NT).astype(BF16)
    grad_attn = (
        grad_attn.reshape(4, 2, BLK, 2, HDIM).transpose(0, 1, 3, 2, 4).reshape(4, 2, 2 * BLK, HDIM)
    )
    grad_mamba_out = matmul(act_mamba, grad_mix, TN).astype(BF16)
    grad_attn_out = matmul(act_attn, grad_mix, TN).astype(BF16)
    core = i % 2
    pair = [(a, a ^ 1) for a in range(nctx)]

    def halves(v):
        v = v.reshape(4, 2, 128, v.shape[-1])
        keep = lax.dynamic_index_in_dim(v, core, 1, keepdims=False)
        give = lax.dynamic_index_in_dim(v, 1 - core, 1, keepdims=False)
        return keep, lax.ppermute(give, "ctx", pair)

    kept, taken = halves(grad_gate_up)
    pair_gu = (kept.astype(F32) + taken.astype(F32)).astype(BF16)
    out_grads = jnp.concatenate([grad_mamba_out, grad_attn_out], axis=0)
    kept = jnp.where(core == 0, grad_down, out_grads)
    taken = lax.ppermute(jnp.where(core == 0, out_grads, grad_down), "ctx", pair)
    pair_o = (kept.astype(F32) + taken.astype(F32)).astype(BF16)
    grad_inner_gain = jnp.sum(grad_m * norm_in, axis=0)
    grad_u = inner_r * (grad_n - norm_in * dots)
    grad_y = (grad_u * z_silu).reshape(8, BLK, LX)
    grad_z = grad_u * y_flat * (z_sig * (1.0 + z_flat * (1.0 - z_sig)))

    leak = pl.pallas_call(
        functools.partial(leak_kernel, nk, pr),
        grid=(8,),
        in_specs=[per_pair((BLK, LX)), per_pair((BLK, LX)), per_pair((BLK, 128))],
        out_specs=chunk_spec(nk, srows),
        out_shape=sds((4, nk, 2, srows, 128), BF16),
        compiler_params=PARAMS,
        cost_estimate=cost(10**9, 4 * 10**6),
        name="leak",
    )(grad_y, swx, c_mat)
    got_leak = exchange(leak.reshape(nctx, 2, srows, 128), "ctx")
    grad_query, grad_kv = pl.pallas_call(
        functools.partial(attn_bwd_kernel, nctx, gs),
        grid=(4,),
        in_specs=[SMEM, row_spec, kv_spec, wide_spec, row_spec, wide_spec, row_spec],
        out_specs=[row_spec, kv_spec],
        out_shape=[sds((4, 2, 2 * BLK, HDIM), F32), sds((nctx, 4, 2, BLK, 128), BF16)],
        scratch_shapes=[
            pltpu.VMEM((2, 2 * BLK, 128), F32),
            pltpu.VMEM((2, 4, gs * BLK, 128), F32),
        ],
        compiler_params=PARAMS,
        cost_estimate=cost(8 * 10**9, 16 * 10**6, 2 * 10**6),
        name="attn_bwd",
    )(idx, query, kv_all, st_rows, attn_o, lse, grad_attn)
    grad_exit = exchange(chain(True, got_leak, grad_kv, pair_gu, pair_o), "ctx").reshape(4, nk, 2, srows, 128)
    grad_kv = pl.pallas_call(
        functools.partial(total_kernel, nctx),
        in_specs=[VMEM, ANY],
        out_specs=VMEM,
        out_shape=sds((4, 2, BLK, 128), F32),
        compiler_params=PARAMS,
        cost_estimate=cost(2 * 10**6, 4 * 10**6),
        name="total_kv",
    )(exchange(grad_kv, "ctx"), mixed)
    back = (tables[0], -tables[1])
    grad_key = turn(grad_kv[..., :HDIM].reshape(4, 2, BLK, 1, HDIM), *back).reshape(8, BLK, HDIM)
    grad_value = grad_kv[..., HDIM:].reshape(8, BLK, HDIM)
    grad_query = grad_query.reshape(4, 2, 2, BLK, HDIM).transpose(0, 1, 3, 2, 4)
    grad_query = turn(grad_query, *back).reshape(8, BLK, 128)

    grad_ext, grad_dt, misc = pl.pallas_call(
        functools.partial(ssd_bwd_kernel, nctx, nk, pr),
        grid=(8,),
        in_specs=ssd_in_specs
        + [per_pair((BLK, LX)), chunk_spec(nk, srows), chunk_spec(nk, srows)],
        out_specs=[per_pair((EXT, LCONV)), per_pair((EXT, 128)), per_pair((8, LCONV))],
        out_shape=[
            sds((8, EXT, LCONV), BF16),
            sds((8, EXT, 128), BF16),
            sds((8, 8, LCONV), F32),
        ],
        compiler_params=PARAMS,
        cost_estimate=cost(4 * 10**9, 8 * 10**6),
        name="ssd_bwd",
    )(*ssd_in, grad_y, entry, grad_exit)

    def lead(v):
        return jnp.pad(v.astype(BF16), ((0, 0), (8, 0), (0, 0)))

    grad_proj = jnp.concatenate(
        [
            lead(grad_z.reshape(8, BLK, LX)),
            grad_ext,
            lead(jnp.concatenate([grad_query, grad_key, grad_value], axis=-1)),
        ],
        axis=-1,
    ).reshape(rows, LPROJ)
    grad_dt = grad_dt.reshape(rows, 128)
    grad_act = matmul(grad_proj, own_in, NT) + matmul(grad_dt, own_dt, NT)

    got_act = ring_sum(grad_act, z).reshape(2, EXT, D)
    halo_back = got_act[:, 5:8].astype(BF16)
    to_first = lax.ppermute(halo_back[0], "ctx", down).astype(F32)
    to_second = lax.ppermute(jnp.where(last_device, 0.0, halo_back[1]), "ctx", up).astype(F32)
    to_first = to_first + jnp.where(last_device, got_act[1, 5:8], 0.0)
    tail_add = jnp.pad(jnp.stack([to_first, to_second]), ((0, 0), (BLK - 3, 0), (0, 0)))
    own_act = (got_act[:, 8:] + tail_add).reshape(128, D)
    hidden = tok.reshape(128, D).astype(F32)
    grad_tokens = grad_middle + rms_back(hidden, rms_of(hidden), own_act * mixer_scale)
    grad_tokens = grad_tokens.reshape(1, 2, BLK, D)

    grad_in = matmul(act_one, grad_proj, TN).astype(BF16)
    grad_dtw = matmul(act_one, grad_dt, TN)
    misc = jnp.sum(misc, axis=0)
    grad_skip = jnp.sum(misc[5, :LX].reshape(LOCAL_HEADS, HDIM), axis=1)
    small = jnp.concatenate(
        [misc[:5].reshape(-1), misc[6, :6], misc[7, :6], grad_skip, grad_inner_gain]
    )
    small = jnp.pad(small, (0, 3840 - small.shape[0])).reshape(1, 256, 15)
    small = jnp.broadcast_to(small, (4, 256, 15)).reshape(D, 15)
    grad_mixer_gain = jnp.sum(grad_act * norm_one, axis=0)
    extras = jnp.concatenate(
        [
            grad_dtw[:, :6],
            grad_mixer_gain[:, None],
            grad_ffn_gain[:, None],
            small,
            jnp.zeros((D, 105), F32),
        ],
        axis=1,
    ).astype(BF16)
    nj = nctx // 2
    rj = 128 // nj
    groups = [[2 * j + c for j in range(nj)] for c in range(2)]
    kept_in, taken_in = halves(grad_in)
    kept_ex, taken_ex = halves(extras)
    sent = pl.pallas_call(
        functools.partial(pack_kernel, nj, rj),
        in_specs=[VMEM] * 6,
        out_specs=VMEM,
        out_shape=sds((nj, 4, rj, 3456), BF16),
        compiler_params=PARAMS,
        cost_estimate=cost(0, 7 * 10**6),
        name="pack",
    )(kept_in, taken_in, kept_ex, taken_ex, pair_gu, pair_o)
    summed = pl.pallas_call(
        functools.partial(total_kernel, nj),
        in_specs=[VMEM, ANY],
        out_specs=VMEM,
        out_shape=sds((4, rj, 3456), F32),
        compiler_params=PARAMS,
        cost_estimate=cost(2 * 10**6, 4 * 10**6),
        name="total",
    )(lax.all_to_all(sent, "ctx", 0, 0, axis_index_groups=groups, tiled=True), got_act)
    owned = exchange(summed[:, :, :2432], "fsdp")
    final = pl.pallas_call(
        assemble_kernel,
        in_specs=[VMEM] * 2,
        out_specs=VMEM,
        out_shape=sds((rj, 12416), BF16),
        compiler_params=PARAMS,
        cost_estimate=cost(0, 10**6),
        name="assemble",
    )(owned, summed[:, :, 2432:])
    mine_all = lax.all_to_all(
        jnp.broadcast_to(final[None], (nj, rj, 12416)),
        "ctx", 0, 0, axis_index_groups=groups, tiled=True,
    )
    other_all = lax.ppermute(mine_all, "ctx", pair)
    half_spec = pl.BlockSpec((128, 4096), lambda h: (h, 0))
    total_in, total_gate_up, extra, total_down, total_mamba_out, total_attn_out = pl.pallas_call(
        functools.partial(unpack_kernel, nj, rj),
        grid=(2,),
        in_specs=[SMEM, whole((nj, rj, 12416)), whole((nj, rj, 12416))],
        out_specs=[
            half_spec,
            half_spec,
            pl.BlockSpec((128, 128), lambda h: (h, 0)),
            whole((512, 1024)),
            whole((384, 1024)),
            whole((128, 1024)),
        ],
        out_shape=[
            sds((256, 4096), F32),
            sds((256, 4096), F32),
            sds((256, 128), F32),
            sds((512, 1024), F32),
            sds((384, 1024), F32),
            sds((128, 1024), F32),
        ],
        compiler_params=PARAMS,
        cost_estimate=cost(0, 10**7),
        name="unpack",
    )(core.astype(jnp.int32).reshape(1), mine_all, other_all)
    extra = extra[:, :96].reshape(256, 4, 24)
    total_dt = extra[:, :, :6].reshape(256, 24)
    total_mixer = jnp.sum(extra[:, :, 6], axis=1)
    total_ffn = jnp.sum(extra[:, :, 7], axis=1)
    small = extra[:, :, 8:23].transpose(1, 0, 2).reshape(4, 3840)
    taps = small[:, :3200].reshape(4, 5, LCONV)
    taps = jnp.concatenate(
        [
            taps[:, :, :LX].transpose(1, 0, 2).reshape(5, 1536),
            jnp.sum(taps[:, :, LX:], axis=0),
        ],
        axis=1,
    )
    taps = lax.dynamic_slice_in_dim(taps, 448 * z, 448, axis=1)
    mine = lax.dynamic_slice_in_dim(small, z, 1, axis=0)[0]
    return (
        mixed,
        grad_tokens,
        total_in,
        total_dt,
        taps[:4],
        taps[4],
        mine[3200:3206],
        mine[3206:3212],
        mine[3212:3218],
        mine[3218:3602],
        total_mamba_out,
        total_attn_out,
        total_mixer,
        total_ffn,
        total_gate_up,
        total_down,
    )


def solution(mesh):
    row = P("fsdp", None)
    vec = P("fsdp")
    act = P("fsdp", None, "ctx", None)
    return jax.shard_map(
        per_device,
        mesh=mesh,
        in_specs=(
            act, P("fsdp", None, "ctx"), act, row, row, P(None, "fsdp"), vec, vec, vec, vec, vec,
            row, row, vec, vec, row, row,
        ),
        out_specs=(
            act, act, row, row, P(None, "fsdp"), vec, vec, vec, vec, vec, row, row, vec, vec, row, row,
        ),
        check_vma=False,
    )
```

```python
import functools
import math

import jax
import jax.numpy as jnp
from jax import lax
from jax.experimental import pallas as pl
from jax.experimental.pallas import tpu as pltpu
from jax.sharding import PartitionSpec as P

D = 1024
FF = 2048
BLK = 64
HDIM = 64
NSTATE = 128
LOCAL_HEADS = 6
LX = 384
LBC = 256
LCONV = LX + LBC
LPROJ = 1280
EXT = 72
EPS = 1e-05
ROPE_BASE = 100000000000.0
NEG = -1e30
F32 = jnp.float32
BF16 = jnp.bfloat16
NN = ((1,), (0,))
NT = ((1,), (1,))
TN = ((0,), (0,))


def dotf(a, b, dims):
    return lax.dot_general(
        a, b, (dims, ((), ())), precision=lax.Precision.HIGHEST, preferred_element_type=F32
    )


def dotb(a, b, dims):
    return lax.dot_general(
        a.astype(BF16), b.astype(BF16), (dims, ((), ())), preferred_element_type=F32
    )


def iota(shape, dim):
    return lax.broadcasted_iota(jnp.int32, shape, dim)


def sigmoid(v):
    return 1.0 / (1.0 + jnp.exp(-v))


def ssd_prep(ext, dtr, st, base, pv):
    tpos = base + iota((BLK, LCONV), 0)
    stc = jnp.broadcast_to(st[:, :1], (BLK, LCONV))
    pre = jnp.broadcast_to(pv[4:5], (BLK, LCONV))
    for tap in range(4):
        use = (tpos - (3 - tap)) >= stc
        pre = pre + jnp.where(use, pv[tap : tap + 1] * ext[5 + tap : 5 + tap + BLK], 0.0)
    sg = sigmoid(pre)
    xc = pre * sg
    lin = dtr + pv[5:6, :128]
    dt = jnp.maximum(lin, 0.0) + jnp.log1p(jnp.exp(-jnp.abs(lin)))
    ea = jnp.exp(pv[6:7, :128])
    ell = -dt * ea
    tri = (iota((BLK, BLK), 1) <= iota((BLK, BLK), 0)).astype(F32)
    eye = (iota((BLK, BLK), 1) == iota((BLK, BLK), 0)).astype(F32)
    run = dotf(tri, ell, NN)
    run_t = dotf(ell, tri, ((0,), (1,)))
    dt_t = dotf(dt, eye, TN)
    allowed = (iota((BLK, BLK), 1) <= iota((BLK, BLK), 0)) & (
        (base + iota((BLK, BLK), 1)) >= st[:, :BLK]
    )
    sw = jnp.where(st < base, jnp.exp(run), 0.0)
    last_ok = (base + iota((BLK, 128), 0)) >= st[BLK - 1 : BLK]
    fwd_decay = jnp.where(
        last_ok, jnp.exp(jnp.where(last_ok, run[BLK - 1 : BLK] - run, 0.0)), 0.0
    )
    sel = (iota((128, LX), 1) // HDIM == iota((128, LX), 0)).astype(F32)
    return dict(
        pre=pre, sg=sg, xc=xc, lin=lin, dt=dt, ea=ea, ell=ell, run=run, run_t=run_t, dt_t=dt_t,
        allowed=allowed, sw=sw, fd=fwd_decay, fw=fwd_decay * dt, sel=sel, tri=tri, tpos=tpos, stc=stc,
    )


def decay_of(p, h):
    spread = p["run"][:, h : h + 1] - p["run_t"][h : h + 1, :]
    return jnp.where(p["allowed"], jnp.exp(jnp.where(p["allowed"], spread, 0.0)), 0.0)


def to_chunks(state, out_ref, nk, pr, extra):
    for k in range(nk):
        rows = [state[h * HDIM + k * pr : h * HDIM + (k + 1) * pr] for h in range(LOCAL_HEADS)]
        out_ref[0, k, 0] = jnp.concatenate(rows + extra, axis=0).astype(BF16)


def from_chunks(ref, nk, pr):
    parts = [ref[0, k, 0].astype(F32) for k in range(nk)]
    rows = []
    for h in range(LOCAL_HEADS):
        for k in range(nk):
            rows.append(parts[k][h * pr : (h + 1) * pr])
    return jnp.concatenate(rows, axis=0)


def block_base(idx_ref, nctx):
    half = pl.program_id(0) % 2
    i = idx_ref[0]
    return jnp.where(half == 0, i, 2 * nctx - 1 - i) * BLK


def proj_kernel(x_ref, w_ref, wdt_ref, gain_ref, *refs):
    z_ref, ext_ref, dtr_ref, qkv_ref, act_ref = refs[-5:]
    x = x_ref[...].astype(F32)
    r = lax.rsqrt(jnp.mean(x * x, axis=1, keepdims=True) + EPS)
    act_ref[...] = (x * r * gain_ref[...]).astype(BF16)
    a = act_ref[...]

    def columns(lo, width):
        p = lax.dot_general(a, w_ref[:, lo : lo + width], (NN, ((), ())), preferred_element_type=F32)
        return p.reshape(8, EXT, width)

    z_ref[:, :, :256] = columns(0, 256)[:, 8:]
    both = columns(256, 256)
    z_ref[:, :, 256:] = both[:, 8:, :128]
    ext_ref[:, :, :128] = both[:, :, 128:]
    ext_ref[:, :, 128:384] = columns(512, 256)
    ext_ref[:, :, 384:] = columns(768, 256)
    qkv_ref[...] = columns(1024, 256)[:, 8:]
    p = lax.dot_general(a, wdt_ref[...], (NN, ((), ())), preferred_element_type=F32)
    dtr_ref[...] = p.reshape(8, EXT, 128)


def mid_kernel(u_ref, w_ref, ss_ref, dep_ref, out_ref):
    eye = iota((128, 128), 0) == iota((128, 128), 1)
    for a in range(4):
        part = lax.dot_general(
            u_ref[128 * a : 128 * a + 128], w_ref[...], (NN, ((), ())), preferred_element_type=F32
        )
        out_ref[a, :128] = part.astype(BF16)
        row = jnp.sum(jnp.where(eye, ss_ref[128 * a : 128 * a + 128], 0.0), axis=0, keepdims=True)
        high = row.astype(BF16).astype(F32)
        pair = jnp.concatenate([high, row - high, jnp.zeros((14, 128), F32)], axis=0)
        pair = jnp.concatenate([pair, jnp.zeros((16, D - 128), F32)], axis=1)
        out_ref[a, 128:] = pair.astype(BF16)


def hold_kernel(value_ref, dep_ref, out_ref):
    out_ref[...] = value_ref[...]


def down_kernel(inner_ref, w_ref, dep_ref, out_ref):
    out_ref[...] = lax.dot_general(
        inner_ref[...], w_ref[...], (NN, ((), ())), preferred_element_type=F32
    ).astype(BF16)


def ssd_fwd_kernel(nctx, nk, pr, idx_ref, ext_ref, dtr_ref, st_ref, pv_ref, y_ref, swx_ref, c_ref, s_ref):
    base = block_base(idx_ref, nctx)
    st = st_ref[0]
    p = ssd_prep(ext_ref[0], dtr_ref[0, 8:], st, base, pv_ref[...])
    x = p["xc"][:, :LX]
    bm = p["xc"][:, LX : LX + NSTATE].astype(BF16)
    cm = p["xc"][:, LX + NSTATE :].astype(BF16)
    inter = dotb(cm, bm, NT)
    xb = x.astype(BF16)
    outs = []
    for h in range(LOCAL_HEADS):
        mix = decay_of(p, h) * inter * p["dt_t"][h : h + 1]
        outs.append(dotb(mix, xb[:, h * HDIM : (h + 1) * HDIM], NN))
    y_ref[0] = jnp.concatenate(outs, axis=1) + pv_ref[7:8, :LX] * x
    swx_ref[0] = dotf(p["sw"], p["sel"], NN)
    c_ref[0] = cm
    fwx = dotf(p["fw"], p["sel"], NN)
    state = dotb(fwx * x, bm, TN)
    dec = jnp.where(
        st[BLK - 1 : BLK] < base,
        jnp.broadcast_to(jnp.exp(p["run_t"][:8, BLK - 1 : BLK]), (8, 128)),
        0.0,
    )
    high = dec.astype(BF16).astype(F32)
    to_chunks(state, s_ref, nk, pr, [high, dec - high])


def ssd_out_kernel(nk, pr, y_ref, swx_ref, c_ref, s_ref, z_ref, gain_ref, dep_ref, out_ref, u_ref, ss_ref):
    s_in = from_chunks(s_ref, nk, pr)
    y = y_ref[0] + swx_ref[0] * dotb(c_ref[0], s_in, NT)
    z = z_ref[0]
    u = y * (z * sigmoid(z))
    out_ref[0] = y
    u_ref[0] = (u * gain_ref[...]).astype(BF16)
    ss_ref[0] = jnp.broadcast_to(jnp.sum(u * u, axis=1, keepdims=True), (BLK, 128))


def split_in_kernel(w_ref, out_ref):
    for zz in range(4):
        kv = HDIM * (zz // 2)
        out_ref[zz, :, :LX] = w_ref[:, LX * zz : LX * zz + LX]
        out_ref[zz, :, LX : 2 * LX] = w_ref[:, 1536 + LX * zz : 1536 + LX * zz + LX]
        out_ref[zz, :, 2 * LX : 1024] = w_ref[:, 3072:3328]
        out_ref[zz, :, 1024:1152] = w_ref[:, 3328 + 128 * zz : 3456 + 128 * zz]
        out_ref[zz, :, 1152:1280] = jnp.concatenate(
            [w_ref[:, 3840 + kv : 3904 + kv], w_ref[:, 3968 + kv : 4032 + kv]], axis=1
        )


def split_gate_up_kernel(w_ref, out_ref):
    for zz in range(4):
        out_ref[zz, :, :512] = w_ref[:, 512 * zz : 512 * zz + 512]
        out_ref[zz, :, 512:] = w_ref[:, FF + 512 * zz : FF + 512 * zz + 512]


def total_kernel(n, got_ref, *refs):
    out_ref = refs[-1]

    def step(j, acc):
        return acc + got_ref[j].astype(F32)

    out_ref[...] = lax.fori_loop(1, n, step, got_ref[0].astype(F32))


def pack_kernel(nj, rj, kin_ref, gin_ref, kex_ref, gex_ref, dep_ref, out_ref):
    for a in range(4):
        part = (kin_ref[a].astype(F32) + gin_ref[a].astype(F32)).astype(BF16)
        out_ref[:, a, :, :LPROJ] = part.reshape(nj, rj, LPROJ)
        part = (kex_ref[a].astype(F32) + gex_ref[a].astype(F32)).astype(BF16)
        out_ref[:, a, :, LPROJ:] = part.reshape(nj, rj, 128)


def pack_early_kernel(nj, rj, gu_ref, o_ref, out_ref):
    for a in range(4):
        out_ref[:, a, :, :1024] = gu_ref[a].reshape(nj, rj, 1024)
    out_ref[:, :, :, 1024:] = o_ref[...].reshape(nj, 4, rj, 1024)


def totals_kernel(n, got_ref, early_ref, dep_ref, out_ref, o_ref):
    def step(j, acc):
        return acc[0] + got_ref[j].astype(F32), acc[1] + early_ref[j].astype(F32)

    first = (got_ref[0].astype(F32), early_ref[0].astype(F32))
    late, early = lax.fori_loop(1, n, step, first)
    out_ref[:, :, :1408] = late
    out_ref[:, :, 1408:] = early[:, :, :1024]
    o_ref[...] = early[:, :, 1024:]


def assemble_kernel(owned_ref, o_ref, out_ref):
    def put(lo, value):
        out_ref[:, lo : lo + value.shape[1]] = value.astype(BF16)

    shared = owned_ref[0, :, 768:1024]
    for zz in range(4):
        put(LX * zz, owned_ref[zz, :, :LX])
        put(1536 + LX * zz, owned_ref[zz, :, LX : 2 * LX])
        put(3328 + 128 * zz, owned_ref[zz, :, 1024:1152])
        put(4096 + 512 * zz, owned_ref[zz, :, 1408:1920])
        put(6144 + 512 * zz, owned_ref[zz, :, 1920:2432])
        put(8320 + 1024 * zz, o_ref[zz])
        if zz > 0:
            shared = shared + owned_ref[zz, :, 768:1024]
    put(3072, shared)
    first = owned_ref[0, :, 1152:1280] + owned_ref[1, :, 1152:1280]
    second = owned_ref[2, :, 1152:1280] + owned_ref[3, :, 1152:1280]
    put(3840, jnp.concatenate([first[:, :HDIM], second[:, :HDIM]], axis=1))
    put(3968, jnp.concatenate([first[:, HDIM:], second[:, HDIM:]], axis=1))
    extras = [owned_ref[zz, :, 1280:1302] for zz in range(4)]
    extras.append(jnp.zeros((extras[0].shape[0], 40), F32))
    put(8192, jnp.concatenate(extras, axis=1))


def unpack_kernel(nj, rj, core_ref, mine_ref, other_ref, w_ref, in_ref, mix_ref, gu_ref, ex_ref, down_ref, mo_ref, ao_ref):
    half = pl.program_id(0)
    core = core_ref[0]

    def write(src):
        total = src[:, :, :4096].reshape(128, 4096).astype(F32)
        in_ref[...] = total
        mix = jnp.sum(total * w_ref[...].astype(F32), axis=1, keepdims=True)
        mix_ref[...] = jnp.broadcast_to(mix, (128, 128))
        gu_ref[...] = src[:, :, 4096:8192].reshape(128, 4096).astype(F32)
        ex_ref[...] = src[:, :, 8192:8320].reshape(128, 128).astype(F32)
        for j in range(nj):
            for a in range(4):
                row = j * 4 * rj + a * rj
                part = src[j, :, 8320 + 1024 * a : 9344 + 1024 * a].astype(F32)

                @pl.when(half == 0)
                def _():
                    down_ref[row : row + rj] = part

                @pl.when(half == 1)
                def _():
                    if row < 384:
                        mo_ref[row : row + rj] = part
                    else:
                        ao_ref[row - 384 : row - 384 + rj] = part

    @pl.when(half == core)
    def _():
        write(mine_ref)

    @pl.when(half != core)
    def _():
        write(other_ref)


def leak_kernel(nk, pr, dy_ref, swx_ref, c_ref, out_ref):
    to_chunks(dotb(swx_ref[0] * dy_ref[0], c_ref[0], TN), out_ref, nk, pr, [])


def ssd_bwd_kernel(
    nctx, nk, pr, idx_ref, ext_ref, dtr_ref, st_ref, pv_ref, dy_ref, s_ref, g_ref, *refs
):
    dext_ref, ddt_ref, misc_ref = refs[-3:]
    base = block_base(idx_ref, nctx)
    st = st_ref[0]
    ext = ext_ref[0]
    pv = pv_ref[...]
    p = ssd_prep(ext, dtr_ref[0, 8:], st, base, pv)
    sel = p["sel"]
    x = p["xc"][:, :LX]
    bm = p["xc"][:, LX : LX + NSTATE]
    cm = p["xc"][:, LX + NSTATE :]
    bmb, cmb, xb = bm.astype(BF16), cm.astype(BF16), x.astype(BF16)
    dy = dy_ref[0]
    dyb = dy.astype(BF16)
    s_in = from_chunks(s_ref, nk, pr)
    g_out = from_chunks(g_ref, nk, pr)
    s_inb, g_outb = s_in.astype(BF16), g_out.astype(BF16)
    inter = dotb(cmb, bmb, NT)
    swx = dotf(p["sw"], sel, NN)
    fwx = dotf(p["fw"], sel, NN)
    skip = pv[7:8, :LX]
    lane = iota((BLK, 128), 1)
    d_inter = jnp.zeros((BLK, BLK), F32)
    drun = jnp.zeros((BLK, 128), F32)
    dx_parts = []
    col_rows = []
    for h in range(LOCAL_HEADS):
        sl = slice(h * HDIM, (h + 1) * HDIM)
        dec = decay_of(p, h)
        dt_row = p["dt_t"][h : h + 1]
        dec_inter = dec * inter
        d_mix = dotb(dyb[:, sl], xb[:, sl], NT)
        dx_parts.append(dotb(dec_inter * dt_row, dyb[:, sl], TN))
        d_inter = d_inter + d_mix * dec * dt_row
        f = d_mix * dec_inter
        row = jnp.sum(f * dt_row, axis=1, keepdims=True)
        drun = drun + jnp.where(lane == h, row, 0.0)
        col_rows.append(jnp.sum(f, axis=0, keepdims=True))
    col_rows.append(jnp.zeros((2, BLK), F32))
    cols = jnp.concatenate(col_rows, axis=0)
    pick = (iota((8, 128), 0) == iota((8, 128), 1)).astype(F32)
    col = dotf(cols, pick, TN)
    ddt = col
    drun = drun - p["dt"] * col
    dx = jnp.concatenate(dx_parts, axis=1) + skip * dy
    dcm = dotb(d_inter, bmb, NN)
    dbm = dotb(d_inter, cmb, TN)
    swdy = swx * dy
    yin = dotb(cmb, s_inb, NT)
    drun = drun + dotf(swdy * yin, sel, NT)
    dcm = dcm + dotb(swdy, s_inb, NN)
    back = dotb(bmb, g_outb, NT)
    dbm = dbm + dotb(fwx * x, g_outb, NN)
    dx = dx + fwx * back
    dfw = dotf(x * back, sel, NT)
    ddt = ddt + dfw * p["fd"]
    tail = dfw * p["fw"]
    drun = drun - tail
    carry = jnp.sum(s_in * g_out, axis=1, keepdims=True)
    sel_t = (iota((LX, 128), 0) // HDIM == iota((LX, 128), 1)).astype(F32)
    last = jnp.sum(tail, axis=0, keepdims=True) + p["sw"][BLK - 1 : BLK] * jnp.sum(
        carry * sel_t, axis=0, keepdims=True
    )
    drun = drun + jnp.where(iota((BLK, 128), 0) == BLK - 1, last, 0.0)
    dell = dotf(p["tri"], drun, TN)
    ddt = ddt - p["ea"] * dell
    ddtraw = ddt * sigmoid(p["lin"])
    ddtraw = jnp.where(lane < LOCAL_HEADS, ddtraw, 0.0)
    zero8 = jnp.zeros((8, 128), F32)
    ddt_ref[0] = jnp.concatenate([zero8, ddtraw], axis=0).astype(BF16)
    dxc = jnp.concatenate([dx, dbm, dcm], axis=1)
    dpre = dxc * (p["sg"] * (1.0 + p["pre"] * (1.0 - p["sg"])))
    dext = jnp.zeros((EXT, LCONV), F32)
    rows = []
    for tap in range(4):
        use = (p["tpos"] - (3 - tap)) >= p["stc"]
        term = jnp.where(use, dpre, 0.0)
        rows.append(jnp.sum(term * ext[5 + tap : 5 + tap + BLK], axis=0, keepdims=True))
        term = term * pv[tap : tap + 1]
        pieces = [jnp.zeros((5 + tap, LCONV), F32), term]
        if tap < 3:
            pieces.append(jnp.zeros((3 - tap, LCONV), F32))
        dext = dext + jnp.concatenate(pieces, axis=0)
    dext_ref[0] = dext.astype(BF16)
    rows.append(jnp.sum(dpre, axis=0, keepdims=True))
    pad = jnp.zeros((1, LCONV - LX), F32)
    rows.append(jnp.concatenate([jnp.sum(dy * x, axis=0, keepdims=True), pad], axis=1))
    pad = jnp.zeros((1, LCONV - 128), F32)
    rows.append(jnp.concatenate([jnp.sum(ddtraw, axis=0, keepdims=True), pad], axis=1))
    rows.append(jnp.concatenate([jnp.sum(dell * p["ell"], axis=0, keepdims=True), pad], axis=1))
    misc_ref[0] = jnp.concatenate(rows, axis=0)


def scan_kernel(reverse, n, pr, st_ref, dec_ref, *refs):
    out_ref = refs[-1]
    rows = LOCAL_HEADS * pr

    def step(j, half, s):
        out_ref[j, half] = s.astype(BF16)
        d = dec_ref[j, half, rows : rows + 16].astype(F32)
        d = d[:LOCAL_HEADS] + d[8 : 8 + LOCAL_HEADS]
        d = jnp.broadcast_to(d[:, None, :], (LOCAL_HEADS, pr, 128)).reshape(rows, 128)
        return d * s + st_ref[j, half, :rows].astype(F32)

    first, second = (1, 0) if reverse else (0, 1)
    s = jnp.zeros((rows, 128), F32)
    s = lax.fori_loop(0, n, lambda j, s: step(j, first, s), s)
    lax.fori_loop(0, n, lambda j, s: step(n - 1 - j, second, s), s)


def unit_of(u, gi):
    if u < 4:
        return 1, 0, u
    is_a = u < 5 + gi
    rowset = jnp.where(is_a, 0, 1)
    half = jnp.where(is_a, 0, 1)
    return rowset, half, jnp.where(is_a, u - 4, u - 5)


def unit_mask(nctx, gs, i, rowset, half, g, st):
    shape = (2 * BLK, gs * BLK)
    row = iota(shape, 0) % BLK
    col = iota(shape, 1)
    qpos = jnp.where(rowset == 0, i, 2 * nctx - 1 - i) * BLK + row
    block = g * gs + col // BLK
    kpos = jnp.where(half == 0, block, 2 * nctx - 1 - block) * BLK + col % BLK
    return (kpos <= qpos) & (kpos >= st)


def attn_fwd_kernel(nctx, gs, idx_ref, q_ref, kv_ref, st_ref, dep_a, dep_b, o_ref, lse_ref, s_ref, m_ref, l_ref, acc_ref):
    i = idx_ref[0]
    gi = i // gs
    m_ref[...] = jnp.full(m_ref.shape, NEG, F32)
    l_ref[...] = jnp.zeros(l_ref.shape, F32)
    acc_ref[...] = jnp.zeros(acc_ref.shape, F32)
    for u in range(9):
        rowset, half, g = unit_of(u, gi)
        kv = kv_ref[pl.ds(g * gs, gs), 0, half].reshape(gs * BLK, 128)
        s = dotb(q_ref[0, rowset], kv[:, :HDIM], NT)
        ok = unit_mask(nctx, gs, i, rowset, half, g, st_ref[0, rowset, :, :1])
        s = jnp.where(ok, s, NEG)
        s_ref[u] = s
        m_ref[rowset] = jnp.maximum(m_ref[rowset], jnp.max(s, axis=1, keepdims=True))
    for u in range(9):
        rowset, half, g = unit_of(u, gi)
        kv = kv_ref[pl.ds(g * gs, gs), 0, half].reshape(gs * BLK, 128)
        w = jnp.exp(s_ref[u] - m_ref[rowset, :, :1])
        l_ref[rowset] = l_ref[rowset] + jnp.sum(w, axis=1, keepdims=True)
        acc_ref[rowset] = acc_ref[rowset] + dotb(w, kv[:, HDIM:], NN)
    o_ref[0] = acc_ref[...] / l_ref[:, :, :HDIM]
    lse_ref[0] = m_ref[...] + jnp.log(l_ref[...])


def attn_bwd_kernel(
    nctx, gs, idx_ref, q_ref, kv_ref, st_ref, o_ref, lse_ref, do_ref, *refs
):
    dq_ref, keep_ref, give_ref, del_ref, acc_ref = refs[-5:]
    i = idx_ref[0]
    gi = i // gs
    acc_ref[...] = jnp.zeros(acc_ref.shape, F32)
    dq_ref[...] = jnp.zeros(dq_ref.shape, F32)
    delta = jnp.sum(do_ref[0].astype(F32) * o_ref[0], axis=2, keepdims=True)
    del_ref[...] = jnp.broadcast_to(delta, del_ref.shape)
    for u in range(9):
        rowset, half, g = unit_of(u, gi)
        kv = kv_ref[pl.ds(g * gs, gs), 0, half].reshape(gs * BLK, 128)
        q = q_ref[0, rowset]
        do = do_ref[0, rowset]
        s = dotb(q, kv[:, :HDIM], NT)
        ok = unit_mask(nctx, gs, i, rowset, half, g, st_ref[0, rowset, :, :1])
        prob = jnp.exp(jnp.where(ok, s, NEG) - lse_ref[0, rowset, :, :1])
        dp = dotb(do, kv[:, HDIM:], NT)
        ds = (prob * (dp - del_ref[rowset, :, :1])).astype(BF16)
        dkv = jnp.concatenate([dotb(ds, q, TN), dotb(prob, do, TN)], axis=1)
        acc_ref[half, g] = acc_ref[half, g] + dkv
        dq_ref[0, rowset] = dq_ref[0, rowset] + dotb(ds, kv[:, :HDIM], NN)
    dq_ref[...] = dq_ref[...] * (HDIM**-0.5)

    def write(even_ref, odd_ref):
        for src in range(4 * gs):
            g, at = src // gs, (src % gs) * BLK
            ref = odd_ref if src % 2 else even_ref
            for half in range(2):
                ref[src // 2, 0, half] = acc_ref[half, g, at : at + BLK].astype(BF16)

    @pl.when(i % 2 == 0)
    def _():
        write(keep_ref, give_ref)

    @pl.when(i % 2 == 1)
    def _():
        write(give_ref, keep_ref)


def spec(shape, index):
    return pl.BlockSpec(shape, index)


def per_pair(shape):
    return pl.BlockSpec((1,) + shape, lambda j: (j,) + (0,) * len(shape))


def whole(shape):
    return pl.BlockSpec(shape, lambda *j: (0,) * len(shape))


def chunk_spec(nk, rows):
    return pl.BlockSpec((1, nk, 1, rows, 128), lambda j: (j // 2, 0, j % 2, 0, 0))


ANY = pl.BlockSpec(memory_space=pl.ANY)
VMEM = pl.BlockSpec(memory_space=pltpu.VMEM)
SMEM = pl.BlockSpec(memory_space=pltpu.SMEM)
PARAMS = pltpu.CompilerParams(vmem_limit_bytes=48 * 1024 * 1024)


def cost(flops, moved, trans=0):
    return pl.CostEstimate(flops=flops // 1000, bytes_accessed=moved // 1000, transcendentals=0)


def sds(shape, dtype):
    return jax.ShapeDtypeStruct(shape, dtype)


def exchange(parts, axis):
    return lax.all_to_all(parts, axis, 0, 0, tiled=True)


def spread(part, axis):
    return exchange(jnp.broadcast_to(part[None], (lax.axis_size(axis),) + part.shape), axis)


def shifts():
    return [(k, [(a, (a + k) % 4) for a in range(4)]) for k in (1, 2, 3)]


def ring_exchange(parts, z):
    out = parts
    for k, perm in shifts():
        sent = lax.dynamic_index_in_dim(parts, (z + k) % 4, 0, keepdims=False)
        got = lax.ppermute(sent, "fsdp", perm)
        out = lax.dynamic_update_index_in_dim(out, got, (z - k) % 4, 0)
    return out


def ring_spread(part, z):
    out = jnp.broadcast_to(part[None], (4,) + part.shape)
    for k, perm in shifts():
        got = lax.ppermute(part, "fsdp", perm)
        out = lax.dynamic_update_index_in_dim(out, got, (z - k) % 4, 0)
    return out


def ring_sum(rows, z):
    parts = rows.astype(BF16).reshape((4, -1) + rows.shape[1:])
    total = lax.dynamic_index_in_dim(parts, z, 0, keepdims=False).astype(F32)
    for k, perm in shifts():
        sent = lax.dynamic_index_in_dim(parts, (z + k) % 4, 0, keepdims=False)
        total = total + lax.ppermute(sent, "fsdp", perm).astype(F32)
    return total


def as_rows(column):
    high = lax.reduce_precision(column, 8, 7)
    pair = jnp.stack([high, column - high], axis=-2).astype(BF16)
    pads = [(0, 0)] * (pair.ndim - 2) + [(0, 14), (0, D - 128)]
    return jnp.pad(pair, pads)


def from_rows(rows):
    pair = rows[..., :2, :128].astype(F32)
    return pair[..., 0, :] + pair[..., 1, :]


def rms_of(v):
    return lax.rsqrt(jnp.mean(v * v, axis=-1, keepdims=True) + EPS)


def rms_back(v, r, dn):
    n = v * r
    return r * (dn - n * jnp.mean(dn * n, axis=-1, keepdims=True))


def turn(values, cosine, sine):
    a, b = values[..., : HDIM // 2], values[..., HDIM // 2 :]
    return jnp.concatenate([a * cosine - b * sine, b * cosine + a * sine], axis=-1)


def matmul(a, b, dims=NN):
    return lax.dot_general(a, b, (dims, ((), ())), preferred_element_type=F32)


def per_device(
    tokens,
    doc_start,
    cotangent,
    w_in,
    w_dt,
    conv_weight,
    conv_bias,
    dt_bias,
    a_log,
    skip_gain,
    inner_gain,
    mamba_out,
    attn_out,
    mixer_gain,
    ffn_gain,
    w_gate_up,
    w_down,
):
    nctx = lax.axis_size("ctx")
    i = lax.axis_index("ctx")
    z = lax.axis_index("fsdp")
    nk = nctx // 4
    pr = HDIM // nk
    gs = nctx // 4
    rpc = 256 // nctx
    idx = i.astype(jnp.int32).reshape(1)
    last_device = i == nctx - 1
    up = [(a, a + 1) for a in range(nctx - 1)]
    down = [(b, a) for a, b in up]

    send_in = pl.pallas_call(
        split_in_kernel,
        in_specs=[VMEM],
        out_specs=VMEM,
        out_shape=sds((4, 256, LPROJ), BF16),
        compiler_params=PARAMS,
        cost_estimate=cost(0, 5 * 10**6),
        name="split_in",
    )(w_in)
    send_gu = pl.pallas_call(
        split_gate_up_kernel,
        in_specs=[VMEM],
        out_specs=VMEM,
        out_shape=sds((4, 256, 1024), BF16),
        compiler_params=PARAMS,
        cost_estimate=cost(0, 4 * 10**6),
        name="split_gate_up",
    )(w_gate_up)
    tok = tokens[0]
    tails = tok[:, BLK - 3 :, :]
    halo_first = lax.ppermute(tails[0], "ctx", up)
    halo_second = lax.ppermute(tails[1], "ctx", down)
    halo = jnp.stack([halo_first, jnp.where(last_device, tails[0], halo_second)])
    starts_own = doc_start[0]
    flat = jnp.concatenate(
        [
            w_dt.reshape(-1),
            conv_weight.reshape(-1),
            conv_bias,
            mixer_gain,
            ffn_gain,
            (starts_own // 64).astype(BF16).reshape(-1),
            (starts_own % 64).astype(BF16).reshape(-1),
        ]
    )
    flat = jnp.pad(flat, (0, 10 * D - flat.shape[0])).reshape(2, 5, D)
    wide = ring_spread(jnp.concatenate([flat, halo, tok], axis=1), z)
    own_in = exchange(send_in, "fsdp").reshape(D, LPROJ)
    own_gu = ring_exchange(send_gu, z).reshape(D, 1024)
    grad_own = cotangent[0].reshape(128, D)
    grad_all = ring_spread(grad_own, z).reshape(512, D)
    flat = wide[:, :, :5, :].reshape(4, 10 * D)
    full_dt = flat[:, :6144].reshape(D, 24)
    own_dt = jnp.pad(lax.dynamic_slice_in_dim(full_dt, 6 * z, 6, axis=1), ((0, 0), (0, 122)))
    full_conv = flat[:, 6144:7936].reshape(4, 4, 448).transpose(1, 0, 2).reshape(4, 1792)
    full_bias = flat[:, 7936:8384].reshape(1, 1792)
    full_taps = jnp.concatenate([full_conv, full_bias], axis=0).astype(F32)
    mixer_scale = flat[:, 8384:8640].reshape(D).astype(F32)
    ffn_scale = flat[:, 8640:8896].reshape(D).astype(F32)
    starts = (
        flat[:, 8896:9024].astype(jnp.int32) * 64 + flat[:, 9024:9152].astype(jnp.int32)
    ).reshape(8, BLK)
    own_taps = jnp.concatenate(
        [lax.dynamic_slice_in_dim(full_taps, LX * z, LX, axis=1), full_taps[:, 1536:]], axis=1
    )

    def lanes(v):
        return jnp.pad(v.astype(F32), (0, LCONV - v.shape[0]))[None]

    pv = jnp.concatenate(
        [own_taps, lanes(dt_bias), lanes(a_log), lanes(jnp.repeat(skip_gain, HDIM))], axis=0
    )
    inner_scale = inner_gain.astype(F32)

    rows = 8 * EXT
    st_wide = jnp.broadcast_to(starts[:, :, None], (8, BLK, 128))
    gate_z, conv_ext, raw_dt, qkv, act_one = pl.pallas_call(
        proj_kernel,
        in_specs=[VMEM] * 4 + [ANY] * 2,
        out_specs=[VMEM] * 5,
        out_shape=[
            sds((8, BLK, LX), F32),
            sds((8, EXT, LCONV), F32),
            sds((8, EXT, 128), F32),
            sds((8, BLK, 256), F32),
            sds((rows, D), BF16),
        ],
        compiler_params=PARAMS,
        cost_estimate=cost(2 * 10**9, 8 * 10**6),
        name="proj",
    )(wide.reshape(rows, D), own_in, own_dt, mixer_scale[None], pv, st_wide)

    blocks = jnp.stack([i, 2 * nctx - 1 - i])
    positions = blocks[:, None] * BLK + jnp.arange(BLK, dtype=jnp.int32)[None, :]
    freq = jnp.exp(
        jnp.arange(HDIM // 2, dtype=F32) * (-2.0 * math.log(ROPE_BASE) / HDIM)
    )
    angle = positions.astype(F32)[:, :, None] * freq
    cosine, sine = jnp.cos(angle), jnp.sin(angle)
    tables = (cosine[None, :, :, None, :], sine[None, :, :, None, :])
    query = qkv[:, :, :128].reshape(4, 2, BLK, 2, HDIM)
    query = turn(query, *tables).astype(BF16) * jnp.asarray(HDIM**-0.5, BF16)
    query = query.transpose(0, 1, 3, 2, 4).reshape(4, 2, 2 * BLK, HDIM)
    key = qkv[:, :, 128:192].reshape(4, 2, BLK, 1, HDIM)
    key = turn(key, *tables).astype(BF16).reshape(4, 2, BLK, HDIM)
    value = qkv[:, :, 192:].astype(BF16).reshape(4, 2, BLK, HDIM)
    kv_own = jnp.concatenate([key, value], axis=-1)

    srows = LOCAL_HEADS * pr
    ssd_in = (idx, conv_ext, raw_dt, st_wide, pv)
    ssd_in_specs = [
        SMEM,
        per_pair((EXT, LCONV)),
        per_pair((EXT, 128)),
        per_pair((BLK, 128)),
        whole((8, LCONV)),
    ]
    y_local, swx, c_mat, state_out = pl.pallas_call(
        functools.partial(ssd_fwd_kernel, nctx, nk, pr),
        grid=(8,),
        in_specs=ssd_in_specs,
        out_specs=[
            per_pair((BLK, LX)),
            per_pair((BLK, LX)),
            per_pair((BLK, 128)),
            chunk_spec(nk, srows + 16),
        ],
        out_shape=[
            sds((8, BLK, LX), F32),
            sds((8, BLK, LX), F32),
            sds((8, BLK, 128), BF16),
            sds((4, nk, 2, srows + 16, 128), BF16),
        ],
        compiler_params=PARAMS,
        cost_estimate=cost(2 * 10**9, 6 * 10**6),
        name="ssd_fwd",
    )(*ssd_in)
    got = exchange(state_out.reshape(nctx, 2, srows + 16, 128), "ctx")
    kv_all = lax.all_gather(kv_own, "ctx")

    st_rows = jnp.broadcast_to(
        starts.reshape(4, 2, 1, BLK, 1), (4, 2, 2, BLK, 128)
    ).reshape(4, 2, 2 * BLK, 128)
    def chain(reverse, terms, *after):
        return pl.pallas_call(
            functools.partial(scan_kernel, reverse, nctx, pr),
            in_specs=[VMEM, VMEM] + [ANY] * len(after),
            out_specs=VMEM,
            out_shape=sds((nctx, 2, srows, 128), BF16),
            compiler_params=PARAMS,
            cost_estimate=cost(10**7, 3 * 10**6),
            name="chain",
        )(terms, got, *after)

    entry = exchange(chain(False, got, own_gu, grad_all, query, st_rows), "ctx").reshape(4, nk, 2, srows, 128)

    row_spec = pl.BlockSpec((1, 2, 2 * BLK, HDIM), lambda s: (s, 0, 0, 0))
    wide_spec = pl.BlockSpec((1, 2, 2 * BLK, 128), lambda s: (s, 0, 0, 0))
    kv_spec = pl.BlockSpec((nctx, 1, 2, BLK, 128), lambda s: (0, s, 0, 0, 0))
    attn_o, lse = pl.pallas_call(
        functools.partial(attn_fwd_kernel, nctx, gs),
        grid=(4,),
        in_specs=[SMEM, row_spec, kv_spec, wide_spec, ANY, ANY],
        out_specs=[row_spec, wide_spec],
        out_shape=[sds((4, 2, 2 * BLK, HDIM), F32), sds((4, 2, 2 * BLK, 128), F32)],
        scratch_shapes=[
            pltpu.VMEM((9, 2 * BLK, gs * BLK), F32),
            pltpu.VMEM((2, 2 * BLK, 128), F32),
            pltpu.VMEM((2, 2 * BLK, 128), F32),
            pltpu.VMEM((2, 2 * BLK, HDIM), F32),
        ],
        compiler_params=PARAMS,
        cost_estimate=cost(4 * 10**9, 8 * 10**6, 2 * 10**6),
        name="attn_fwd",
    )(idx, query, kv_all, st_rows, own_gu, grad_all)
    act_attn = (
        attn_o.reshape(4, 2, 2, BLK, HDIM).transpose(0, 1, 3, 2, 4).reshape(512, 128).astype(BF16)
    )

    mamba_y, scaled_u, squares = pl.pallas_call(
        functools.partial(ssd_out_kernel, nk, pr),
        grid=(8,),
        in_specs=[
            per_pair((BLK, LX)),
            per_pair((BLK, LX)),
            per_pair((BLK, 128)),
            chunk_spec(nk, srows),
            per_pair((BLK, LX)),
            whole((1, LX)),
            ANY,
        ],
        out_specs=[per_pair((BLK, LX)), per_pair((BLK, LX)), per_pair((BLK, 128))],
        out_shape=[
            sds((8, BLK, LX), F32),
            sds((8, BLK, LX), BF16),
            sds((8, BLK, 128), F32),
        ],
        compiler_params=PARAMS,
        cost_estimate=cost(10**9, 6 * 10**6),
        name="ssd_out",
    )(y_local, swx, c_mat, entry, gate_z, inner_scale[None], attn_o)

    def gather_sum(part_rows):
        got_rows = exchange(part_rows.astype(BF16).reshape((4, -1) + part_rows.shape[1:]), "fsdp")
        return jnp.sum(got_rows.astype(F32), axis=0)

    attn_mid = ring_sum(matmul(act_attn, attn_out), z)
    part_rows = pl.pallas_call(
        mid_kernel,
        in_specs=[VMEM] * 3 + [ANY],
        out_specs=VMEM,
        out_shape=sds((4, 144, D), BF16),
        compiler_params=PARAMS,
        cost_estimate=cost(4 * 10**8, 3 * 10**6),
        name="mid_part",
    )(scaled_u.reshape(512, LX), mamba_out, squares.reshape(512, 128), attn_mid)
    got_part = exchange(part_rows, "fsdp")
    scaled_mid = jnp.sum(got_part[:, :128].astype(F32), axis=0)
    square_sum = jnp.sum(from_rows(got_part[:, 128:]), axis=0)
    own_r = lax.rsqrt(square_sum.reshape(128, 1) * (1.0 / 1536) + EPS)
    mamba_mid = scaled_mid * own_r
    middle = tok.reshape(128, D).astype(F32) + mamba_mid + attn_mid
    mid_r = rms_of(middle)
    norm_two = middle * mid_r
    def spread_rows(values, column):
        sent = jnp.concatenate([values.astype(BF16), as_rows(column.reshape(128))], axis=0)
        got_rows = spread(sent, "fsdp").reshape(4, 144, D)
        return got_rows[:, :128].reshape(512, D), from_rows(got_rows[:, 128:]).reshape(512, 1)

    act_two, inner_r = spread_rows(norm_two * ffn_scale, own_r)
    y_flat = mamba_y.reshape(512, LX)
    z_flat = gate_z.reshape(512, LX)
    z_sig = sigmoid(z_flat)
    z_silu = z_flat * z_sig
    norm_in = y_flat * z_silu * inner_r
    act_mamba = (norm_in * inner_scale).astype(BF16)

    gate_up = matmul(act_two, own_gu)
    gate_val, up_val = gate_up[:, :512], gate_up[:, 512:]
    gate_sig = sigmoid(gate_val)
    gate_silu = gate_val * gate_sig
    inner = (gate_silu * up_val).astype(BF16)
    grad_inner = matmul(grad_all, w_down, NT)
    grad_gate = grad_inner * up_val * (gate_sig * (1.0 + gate_val * (1.0 - gate_sig)))
    grad_gu = jnp.concatenate([grad_gate, grad_inner * gate_silu], axis=1).astype(BF16)
    grad_act_two = gather_sum(matmul(grad_gu, own_gu, NT))
    grad_down = matmul(inner, grad_all, TN).astype(BF16)
    grad_gate_up = matmul(act_two, grad_gu, TN).astype(BF16)
    grad_ffn_gain = jnp.sum(grad_act_two * norm_two, axis=0)
    grad_middle = grad_own.astype(F32) + rms_back(middle, mid_r, grad_act_two * ffn_scale)
    own_mix = grad_middle.astype(BF16)
    own_dots = jnp.sum(own_mix.astype(F32) * mamba_mid, axis=1) * (1.0 / 1536)
    grad_mix, dots = spread_rows(own_mix, own_dots)

    down_part = pl.pallas_call(
        down_kernel,
        in_specs=[VMEM, VMEM, ANY],
        out_specs=VMEM,
        out_shape=sds((512, D), BF16),
        compiler_params=PARAMS,
        cost_estimate=cost(5 * 10**8, 3 * 10**6),
        name="down",
    )(inner, w_down, grad_mix)
    mixed = (middle + ring_sum(down_part, z)).astype(BF16).reshape(1, 2, BLK, D)

    grad_m = matmul(grad_mix, mamba_out, NT)
    grad_n = grad_m * inner_scale
    grad_attn = matmul(grad_mix, attn_out, NT).astype(BF16)
    grad_attn = (
        grad_attn.reshape(4, 2, BLK, 2, HDIM).transpose(0, 1, 3, 2, 4).reshape(4, 2, 2 * BLK, HDIM)
    )
    grad_mamba_out = matmul(act_mamba, grad_mix, TN).astype(BF16)
    grad_attn_out = matmul(act_attn, grad_mix, TN).astype(BF16)
    core = i % 2
    pair = [(a, a ^ 1) for a in range(nctx)]

    def halves(v):
        v = v.reshape(4, 2, 128, v.shape[-1])
        keep = lax.dynamic_index_in_dim(v, core, 1, keepdims=False)
        give = lax.dynamic_index_in_dim(v, 1 - core, 1, keepdims=False)
        return keep, lax.ppermute(give, "ctx", pair)

    kept, taken = halves(grad_gate_up)
    pair_gu = (kept.astype(F32) + taken.astype(F32)).astype(BF16)
    out_grads = jnp.concatenate([grad_mamba_out, grad_attn_out], axis=0)
    kept = jnp.where(core == 0, grad_down, out_grads)
    taken = lax.ppermute(jnp.where(core == 0, out_grads, grad_down), "ctx", pair)
    pair_o = (kept.astype(F32) + taken.astype(F32)).astype(BF16)
    grad_inner_gain = jnp.sum(grad_m * norm_in, axis=0)
    grad_u = inner_r * (grad_n - norm_in * dots)
    grad_y = (grad_u * z_silu).reshape(8, BLK, LX)
    grad_z = grad_u * y_flat * (z_sig * (1.0 + z_flat * (1.0 - z_sig)))

    leak = pl.pallas_call(
        functools.partial(leak_kernel, nk, pr),
        grid=(8,),
        in_specs=[per_pair((BLK, LX)), per_pair((BLK, LX)), per_pair((BLK, 128))],
        out_specs=chunk_spec(nk, srows),
        out_shape=sds((4, nk, 2, srows, 128), BF16),
        compiler_params=PARAMS,
        cost_estimate=cost(10**9, 4 * 10**6),
        name="leak",
    )(grad_y, swx, c_mat)
    got_leak = exchange(leak.reshape(nctx, 2, srows, 128), "ctx")
    half_kv_spec = pl.BlockSpec((nctx // 2, 1, 2, BLK, 128), lambda s: (0, s, 0, 0, 0))
    grad_query, keep_kv, give_kv = pl.pallas_call(
        functools.partial(attn_bwd_kernel, nctx, gs),
        grid=(4,),
        in_specs=[SMEM, row_spec, kv_spec, wide_spec, row_spec, wide_spec, row_spec] + [ANY] * 5,
        out_specs=[row_spec, half_kv_spec, half_kv_spec],
        out_shape=[
            sds((4, 2, 2 * BLK, HDIM), F32),
            sds((nctx // 2, 4, 2, BLK, 128), BF16),
            sds((nctx // 2, 4, 2, BLK, 128), BF16),
        ],
        scratch_shapes=[
            pltpu.VMEM((2, 2 * BLK, 128), F32),
            pltpu.VMEM((2, 4, gs * BLK, 128), F32),
        ],
        compiler_params=PARAMS,
        cost_estimate=cost(8 * 10**9, 16 * 10**6, 2 * 10**6),
        name="attn_bwd",
    )(
        idx, query, kv_all, st_rows, attn_o, lse, grad_attn,
        leak, grad_gate_up, grad_down, grad_mamba_out, grad_attn_out,
    )
    chained = chain(True, got_leak, give_kv)
    grad_exit = exchange(chained, "ctx").reshape(4, nk, 2, srows, 128)
    give_kv = pl.pallas_call(
        hold_kernel,
        in_specs=[VMEM, ANY],
        out_specs=VMEM,
        out_shape=sds(give_kv.shape, BF16),
        compiler_params=PARAMS,
        cost_estimate=cost(0, 4 * 10**6),
        name="hold",
    )(give_kv, chained)
    taken_kv = lax.ppermute(give_kv, "ctx", pair)
    pair_kv = (keep_kv.astype(F32) + taken_kv.astype(F32)).astype(BF16)
    nj = nctx // 2
    rj = 128 // nj
    groups = [[2 * j + c for j in range(nj)] for c in range(2)]
    grad_ext, grad_dt, misc = pl.pallas_call(
        functools.partial(ssd_bwd_kernel, nctx, nk, pr),
        grid=(8,),
        in_specs=ssd_in_specs
        + [per_pair((BLK, LX)), chunk_spec(nk, srows), chunk_spec(nk, srows)],
        out_specs=[per_pair((EXT, LCONV)), per_pair((EXT, 128)), per_pair((8, LCONV))],
        out_shape=[
            sds((8, EXT, LCONV), BF16),
            sds((8, EXT, 128), BF16),
            sds((8, 8, LCONV), F32),
        ],
        compiler_params=PARAMS,
        cost_estimate=cost(4 * 10**9, 8 * 10**6),
        name="ssd_bwd",
    )(*ssd_in, grad_y, entry, grad_exit)

    grad_dt = grad_dt.reshape(rows, 128)
    grad_dtw = matmul(act_one, grad_dt, TN)
    misc = jnp.sum(misc, axis=0)
    grad_skip = jnp.sum(misc[5, :LX].reshape(LOCAL_HEADS, HDIM), axis=1)
    small = jnp.concatenate(
        [misc[:5].reshape(-1), misc[6, :6], misc[7, :6], grad_skip, grad_inner_gain]
    )
    small = jnp.pad(small, (0, 3840 - small.shape[0])).reshape(1, 256, 15)
    small = jnp.broadcast_to(small, (4, 256, 15)).reshape(D, 15)
    extras = jnp.concatenate(
        [
            grad_dtw[:, :6],
            grad_ffn_gain[:, None],
            small,
            jnp.zeros((D, 106), F32),
        ],
        axis=1,
    ).astype(BF16)
    early = pl.pallas_call(
        functools.partial(pack_early_kernel, nj, rj),
        in_specs=[VMEM] * 2,
        out_specs=VMEM,
        out_shape=sds((nj, 4, rj, 2048), BF16),
        compiler_params=PARAMS,
        cost_estimate=cost(0, 4 * 10**6),
        name="pack_early",
    )(pair_gu, pair_o)

    def core_exchange(parts):
        return lax.all_to_all(parts, "ctx", 0, 0, axis_index_groups=groups, tiled=True)

    grad_kv = pl.pallas_call(
        functools.partial(total_kernel, nj),
        in_specs=[VMEM] + [ANY] * 3,
        out_specs=VMEM,
        out_shape=sds((4, 2, BLK, 128), F32),
        compiler_params=PARAMS,
        cost_estimate=cost(2 * 10**6, 4 * 10**6),
        name="total_kv",
    )(core_exchange(pair_kv), mixed, early, extras)
    got_early = core_exchange(early)
    back = (tables[0], -tables[1])
    grad_key = turn(grad_kv[..., :HDIM].reshape(4, 2, BLK, 1, HDIM), *back).reshape(8, BLK, HDIM)
    grad_value = grad_kv[..., HDIM:].reshape(8, BLK, HDIM)
    grad_query = grad_query.reshape(4, 2, 2, BLK, HDIM).transpose(0, 1, 3, 2, 4)
    grad_query = turn(grad_query, *back).reshape(8, BLK, 128)

    def lead(v):
        return jnp.pad(v.astype(BF16), ((0, 0), (8, 0), (0, 0)))

    grad_proj = jnp.concatenate(
        [
            lead(grad_z.reshape(8, BLK, LX)),
            grad_ext,
            lead(jnp.concatenate([grad_query, grad_key, grad_value], axis=-1)),
        ],
        axis=-1,
    ).reshape(rows, LPROJ)
    grad_act = matmul(grad_proj, own_in, NT) + matmul(grad_dt, own_dt, NT)

    got_act = ring_sum(grad_act, z).reshape(2, EXT, D)
    halo_back = got_act[:, 5:8].astype(BF16)
    to_first = lax.ppermute(halo_back[0], "ctx", down).astype(F32)
    to_second = lax.ppermute(jnp.where(last_device, 0.0, halo_back[1]), "ctx", up).astype(F32)
    to_first = to_first + jnp.where(last_device, got_act[1, 5:8], 0.0)
    tail_add = jnp.pad(jnp.stack([to_first, to_second]), ((0, 0), (BLK - 3, 0), (0, 0)))
    own_act = (got_act[:, 8:] + tail_add).reshape(128, D)
    hidden = tok.reshape(128, D).astype(F32)
    grad_tokens = grad_middle + rms_back(hidden, rms_of(hidden), own_act * mixer_scale)
    grad_tokens = grad_tokens.reshape(1, 2, BLK, D)

    grad_in = matmul(act_one, grad_proj, TN).astype(BF16)
    kept_in, taken_in = halves(grad_in)
    kept_ex, taken_ex = halves(extras)
    sent = pl.pallas_call(
        functools.partial(pack_kernel, nj, rj),
        in_specs=[VMEM] * 4 + [ANY],
        out_specs=VMEM,
        out_shape=sds((nj, 4, rj, 1408), BF16),
        compiler_params=PARAMS,
        cost_estimate=cost(0, 7 * 10**6),
        name="pack",
    )(kept_in, taken_in, kept_ex, taken_ex, got_early)
    summed, summed_o = pl.pallas_call(
        functools.partial(totals_kernel, nj),
        in_specs=[VMEM, VMEM, ANY],
        out_specs=[VMEM, VMEM],
        out_shape=[sds((4, rj, 2432), F32), sds((4, rj, 1024), F32)],
        compiler_params=PARAMS,
        cost_estimate=cost(2 * 10**6, 4 * 10**6),
        name="totals",
    )(core_exchange(sent), got_early, got_act)
    owned = exchange(summed, "fsdp")
    final = pl.pallas_call(
        assemble_kernel,
        in_specs=[VMEM] * 2,
        out_specs=VMEM,
        out_shape=sds((rj, 12416), BF16),
        compiler_params=PARAMS,
        cost_estimate=cost(0, 10**6),
        name="assemble",
    )(owned, summed_o)
    mine_all = core_exchange(jnp.broadcast_to(final[None], (nj, rj, 12416)))
    other_all = lax.ppermute(mine_all, "ctx", pair)
    half_spec = pl.BlockSpec((128, 4096), lambda h: (h, 0))
    total_in, mixer_dot, total_gate_up, extra, total_down, total_mamba_out, total_attn_out = pl.pallas_call(
        functools.partial(unpack_kernel, nj, rj),
        grid=(2,),
        in_specs=[SMEM, whole((nj, rj, 12416)), whole((nj, rj, 12416)), half_spec],
        out_specs=[
            half_spec,
            pl.BlockSpec((128, 128), lambda h: (h, 0)),
            half_spec,
            pl.BlockSpec((128, 128), lambda h: (h, 0)),
            whole((512, 1024)),
            whole((384, 1024)),
            whole((128, 1024)),
        ],
        out_shape=[
            sds((256, 4096), F32),
            sds((256, 128), F32),
            sds((256, 4096), F32),
            sds((256, 128), F32),
            sds((512, 1024), F32),
            sds((384, 1024), F32),
            sds((128, 1024), F32),
        ],
        compiler_params=PARAMS,
        cost_estimate=cost(0, 10**7),
        name="unpack",
    )(core.astype(jnp.int32).reshape(1), mine_all, other_all, w_in)
    extra = extra[:, :88].reshape(256, 4, 22)
    total_dt = extra[:, :, :6].reshape(256, 24)
    mixer_dot = mixer_dot[:, 0] + jnp.sum(total_dt * w_dt.astype(F32), axis=1)
    total_mixer = mixer_dot / mixer_gain.astype(F32)
    total_ffn = jnp.sum(extra[:, :, 6], axis=1)
    small = extra[:, :, 7:22].transpose(1, 0, 2).reshape(4, 3840)
    taps = small[:, :3200].reshape(4, 5, LCONV)
    taps = jnp.concatenate(
        [
            taps[:, :, :LX].transpose(1, 0, 2).reshape(5, 1536),
            jnp.sum(taps[:, :, LX:], axis=0),
        ],
        axis=1,
    )
    taps = lax.dynamic_slice_in_dim(taps, 448 * z, 448, axis=1)
    mine = lax.dynamic_slice_in_dim(small, z, 1, axis=0)[0]
    return (
        mixed,
        grad_tokens,
        total_in,
        total_dt,
        taps[:4],
        taps[4],
        mine[3200:3206],
        mine[3206:3212],
        mine[3212:3218],
        mine[3218:3602],
        total_mamba_out,
        total_attn_out,
        total_mixer,
        total_ffn,
        total_gate_up,
        total_down,
    )


def solution(mesh):
    row = P("fsdp", None)
    vec = P("fsdp")
    act = P("fsdp", None, "ctx", None)
    return jax.shard_map(
        per_device,
        mesh=mesh,
        in_specs=(
            act, P("fsdp", None, "ctx"), act, row, row, P(None, "fsdp"), vec, vec, vec, vec, vec,
            row, row, vec, vec, row, row,
        ),
        out_specs=(
            act, act, row, row, P(None, "fsdp"), vec, vec, vec, vec, vec, row, row, vec, vec, row, row,
        ),
        check_vma=False,
    )
```

```python
import functools
import math

import jax
import jax.numpy as jnp
from jax import lax
from jax.experimental import pallas as pl
from jax.experimental.pallas import tpu as pltpu
from jax.sharding import PartitionSpec as P

D = 1024
FF = 2048
BLK = 64
HDIM = 64
NSTATE = 128
LOCAL_HEADS = 6
LX = 384
LBC = 256
LCONV = LX + LBC
LPROJ = 1280
EXT = 72
EPS = 1e-05
ROPE_BASE = 100000000000.0
NEG = -1e30
F32 = jnp.float32
BF16 = jnp.bfloat16
NN = ((1,), (0,))
NT = ((1,), (1,))
TN = ((0,), (0,))


def dotf(a, b, dims):
    return lax.dot_general(
        a, b, (dims, ((), ())), precision=lax.Precision.HIGHEST, preferred_element_type=F32
    )


def dotb(a, b, dims):
    return lax.dot_general(
        a.astype(BF16), b.astype(BF16), (dims, ((), ())), preferred_element_type=F32
    )


def iota(shape, dim):
    return lax.broadcasted_iota(jnp.int32, shape, dim)


def sigmoid(v):
    return 1.0 / (1.0 + jnp.exp(-v))


def ssd_prep(ext, dtr, st, base, pv):
    tpos = base + iota((BLK, LCONV), 0)
    stc = jnp.broadcast_to(st[:, :1], (BLK, LCONV))
    pre = jnp.broadcast_to(pv[4:5], (BLK, LCONV))
    for tap in range(4):
        use = (tpos - (3 - tap)) >= stc
        pre = pre + jnp.where(use, pv[tap : tap + 1] * ext[5 + tap : 5 + tap + BLK], 0.0)
    sg = sigmoid(pre)
    xc = pre * sg
    lin = dtr + pv[5:6, :128]
    dt = jnp.maximum(lin, 0.0) + jnp.log1p(jnp.exp(-jnp.abs(lin)))
    ea = jnp.exp(pv[6:7, :128])
    ell = -dt * ea
    tri = (iota((BLK, BLK), 1) <= iota((BLK, BLK), 0)).astype(F32)
    eye = (iota((BLK, BLK), 1) == iota((BLK, BLK), 0)).astype(F32)
    run = dotf(tri, ell, NN)
    run_t = dotf(ell, tri, ((0,), (1,)))
    dt_t = dotf(dt, eye, TN)
    allowed = (iota((BLK, BLK), 1) <= iota((BLK, BLK), 0)) & (
        (base + iota((BLK, BLK), 1)) >= st[:, :BLK]
    )
    sw = jnp.where(st < base, jnp.exp(run), 0.0)
    last_ok = (base + iota((BLK, 128), 0)) >= st[BLK - 1 : BLK]
    fwd_decay = jnp.where(
        last_ok, jnp.exp(jnp.where(last_ok, run[BLK - 1 : BLK] - run, 0.0)), 0.0
    )
    sel = (iota((128, LX), 1) // HDIM == iota((128, LX), 0)).astype(F32)
    return dict(
        pre=pre, sg=sg, xc=xc, lin=lin, dt=dt, ea=ea, ell=ell, run=run, run_t=run_t, dt_t=dt_t,
        allowed=allowed, sw=sw, fd=fwd_decay, fw=fwd_decay * dt, sel=sel, tri=tri, tpos=tpos, stc=stc,
    )


def decay_of(p, h):
    spread = p["run"][:, h : h + 1] - p["run_t"][h : h + 1, :]
    return jnp.where(p["allowed"], jnp.exp(jnp.where(p["allowed"], spread, 0.0)), 0.0)


def to_chunks(state, out_ref, nk, pr, extra):
    for k in range(nk):
        rows = [state[h * HDIM + k * pr : h * HDIM + (k + 1) * pr] for h in range(LOCAL_HEADS)]
        out_ref[0, k, 0] = jnp.concatenate(rows + extra, axis=0).astype(BF16)


def from_chunks(ref, nk, pr):
    parts = [ref[0, k, 0].astype(F32) for k in range(nk)]
    rows = []
    for h in range(LOCAL_HEADS):
        for k in range(nk):
            rows.append(parts[k][h * pr : (h + 1) * pr])
    return jnp.concatenate(rows, axis=0)


def block_base(idx_ref, nctx):
    half = pl.program_id(0) % 2
    i = idx_ref[0]
    return jnp.where(half == 0, i, 2 * nctx - 1 - i) * BLK


def turned(v, cosine, sine):
    a, b = v[:, : HDIM // 2], v[:, HDIM // 2 :]
    return jnp.concatenate([a * cosine - b * sine, b * cosine + a * sine], axis=1)


def proj_kernel(core_ref, x_ref, mine_ref, other_ref, wdt_ref, gain_ref, cos_ref, sin_ref, *refs):
    z_ref, ext_ref, dtr_ref, q_ref, kv_ref, act_ref, w_ref = refs[-7:]
    x = x_ref[...].astype(F32)
    r = lax.rsqrt(jnp.mean(x * x, axis=1, keepdims=True) + EPS)
    act_ref[...] = (x * r * gain_ref[...]).astype(BF16)

    def place(even_ref, odd_ref):
        for src in range(4):
            w_ref[256 * src : 256 * src + 128] = even_ref[src]
            w_ref[256 * src + 128 : 256 * src + 256] = odd_ref[src]

    @pl.when(core_ref[0] == 0)
    def _():
        place(mine_ref, other_ref)

    @pl.when(core_ref[0] == 1)
    def _():
        place(other_ref, mine_ref)

    a = act_ref[...]

    def columns(lo, width):
        p = lax.dot_general(a, w_ref[:, lo : lo + width], (NN, ((), ())), preferred_element_type=F32)
        return p.reshape(8, EXT, width)

    p = columns(1024, 256)
    for j in range(8):
        seq, half = j // 2, j % 2
        own = p[j, 8:]
        cosine, sine = cos_ref[half], sin_ref[half]
        for e in range(2):
            q = turned(own[:, HDIM * e : HDIM * e + HDIM], cosine, sine).astype(BF16)
            q = (q.astype(F32) * HDIM**-0.5).astype(BF16)
            q_ref[seq, half, BLK * e : BLK * e + BLK] = q
        k = turned(own[:, 128:192], cosine, sine)
        kv_ref[seq, half] = jnp.concatenate([k, own[:, 192:]], axis=1).astype(BF16)
    z_ref[:, :, :256] = columns(0, 256)[:, 8:]
    both = columns(256, 256)
    z_ref[:, :, 256:] = both[:, 8:, :128]
    ext_ref[:, :, :128] = both[:, :, 128:]
    ext_ref[:, :, 128:384] = columns(512, 256)
    ext_ref[:, :, 384:] = columns(768, 256)
    p = lax.dot_general(a, wdt_ref[...], (NN, ((), ())), preferred_element_type=F32)
    dtr_ref[...] = p.reshape(8, EXT, 128)


def dproj_kernel(n, got_ref, z_ref, ext_ref, q_ref, cos_ref, sin_ref, *refs):
    out_ref = refs[-1]

    def step(j, acc):
        return acc + got_ref[j].astype(F32)

    kv = lax.fori_loop(1, n, step, got_ref[0].astype(F32))
    out_ref[:, :8] = jnp.zeros((8, 8, LPROJ), BF16)
    out_ref[:, :, LX : LX + LCONV] = ext_ref[...]
    for j in range(8):
        own = kv[j // 2, j % 2]
        k = turned(own[:, :HDIM], cos_ref[j % 2], -sin_ref[j % 2])
        out_ref[j, 8:, :LX] = z_ref[j].astype(BF16)
        out_ref[j, 8:, 1024:1152] = q_ref[j // 2, j % 2]
        out_ref[j, 8:, 1152:] = jnp.concatenate([k, own[:, HDIM:]], axis=1).astype(BF16)


def mid_kernel(u_ref, w_ref, ss_ref, dep_ref, out_ref):
    eye = iota((128, 128), 0) == iota((128, 128), 1)
    for a in range(4):
        part = lax.dot_general(
            u_ref[128 * a : 128 * a + 128], w_ref[...], (NN, ((), ())), preferred_element_type=F32
        )
        out_ref[a, :128] = part.astype(BF16)
        row = jnp.sum(jnp.where(eye, ss_ref[128 * a : 128 * a + 128], 0.0), axis=0, keepdims=True)
        high = row.astype(BF16).astype(F32)
        pair = jnp.concatenate([high, row - high, jnp.zeros((14, 128), F32)], axis=0)
        pair = jnp.concatenate([pair, jnp.zeros((16, D - 128), F32)], axis=1)
        out_ref[a, 128:] = pair.astype(BF16)


def hold_kernel(value_ref, dep_ref, out_ref):
    out_ref[...] = value_ref[...]


def down_kernel(inner_ref, w_ref, dep_ref, out_ref):
    out_ref[...] = lax.dot_general(
        inner_ref[...], w_ref[...], (NN, ((), ())), preferred_element_type=F32
    ).astype(BF16)


def ssd_fwd_kernel(nctx, nk, pr, idx_ref, ext_ref, dtr_ref, st_ref, pv_ref, y_ref, swx_ref, c_ref, s_ref):
    base = block_base(idx_ref, nctx)
    st = st_ref[0]
    p = ssd_prep(ext_ref[0], dtr_ref[0, 8:], st, base, pv_ref[...])
    x = p["xc"][:, :LX]
    bm = p["xc"][:, LX : LX + NSTATE].astype(BF16)
    cm = p["xc"][:, LX + NSTATE :].astype(BF16)
    inter = dotb(cm, bm, NT)
    xb = x.astype(BF16)
    outs = []
    for h in range(LOCAL_HEADS):
        mix = decay_of(p, h) * inter * p["dt_t"][h : h + 1]
        outs.append(dotb(mix, xb[:, h * HDIM : (h + 1) * HDIM], NN))
    y_ref[0] = jnp.concatenate(outs, axis=1) + pv_ref[7:8, :LX] * x
    swx_ref[0] = dotf(p["sw"], p["sel"], NN)
    c_ref[0] = cm
    fwx = dotf(p["fw"], p["sel"], NN)
    state = dotb(fwx * x, bm, TN)
    dec = jnp.where(
        st[BLK - 1 : BLK] < base,
        jnp.broadcast_to(jnp.exp(p["run_t"][:8, BLK - 1 : BLK]), (8, 128)),
        0.0,
    )
    high = dec.astype(BF16).astype(F32)
    to_chunks(state, s_ref, nk, pr, [high, dec - high])


def ssd_out_kernel(nk, pr, y_ref, swx_ref, c_ref, s_ref, z_ref, gain_ref, *refs):
    out_ref, u_ref, ss_ref = refs[-3:]
    s_in = from_chunks(s_ref, nk, pr)
    y = y_ref[0] + swx_ref[0] * dotb(c_ref[0], s_in, NT)
    z = z_ref[0]
    u = y * (z * sigmoid(z))
    out_ref[0] = y
    u_ref[0] = (u * gain_ref[...]).astype(BF16)
    ss_ref[0] = jnp.broadcast_to(jnp.sum(u * u, axis=1, keepdims=True), (BLK, 128))


def split_in_kernel(core_ref, full_ref, out_ref):
    w_ref = full_ref.at[pl.ds(pl.multiple_of(core_ref[0] * 128, 128), 128)]
    for zz in range(4):
        kv = HDIM * (zz // 2)
        out_ref[zz, :, :LX] = w_ref[:, LX * zz : LX * zz + LX]
        out_ref[zz, :, LX : 2 * LX] = w_ref[:, 1536 + LX * zz : 1536 + LX * zz + LX]
        out_ref[zz, :, 2 * LX : 1024] = w_ref[:, 3072:3328]
        out_ref[zz, :, 1024:1152] = w_ref[:, 3328 + 128 * zz : 3456 + 128 * zz]
        out_ref[zz, :, 1152:1280] = jnp.concatenate(
            [w_ref[:, 3840 + kv : 3904 + kv], w_ref[:, 3968 + kv : 4032 + kv]], axis=1
        )


def split_gate_up_kernel(w_ref, out_ref):
    for zz in range(4):
        out_ref[zz, :, :512] = w_ref[:, 512 * zz : 512 * zz + 512]
        out_ref[zz, :, 512:] = w_ref[:, FF + 512 * zz : FF + 512 * zz + 512]


def pack_kernel(nj, rj, kin_ref, gin_ref, kex_ref, gex_ref, dep_ref, out_ref):
    for a in range(4):
        part = (kin_ref[a].astype(F32) + gin_ref[a].astype(F32)).astype(BF16)
        out_ref[:, a, :, :LPROJ] = part.reshape(nj, rj, LPROJ)
        part = (kex_ref[a].astype(F32) + gex_ref[a].astype(F32)).astype(BF16)
        out_ref[:, a, :, LPROJ:] = part.reshape(nj, rj, 128)


def pack_early_kernel(nj, rj, gu_ref, o_ref, out_ref):
    for a in range(4):
        out_ref[:, a, :, :1024] = gu_ref[a].reshape(nj, rj, 1024)
    out_ref[:, :, :, 1024:] = o_ref[...].reshape(nj, 4, rj, 1024)


def totals_kernel(n, got_ref, early_ref, dep_a, dep_b, out_ref, o_ref):
    def step(j, acc):
        return acc[0] + got_ref[j].astype(F32), acc[1] + early_ref[j].astype(F32)

    first = (got_ref[0].astype(F32), early_ref[0].astype(F32))
    late, early = lax.fori_loop(1, n, step, first)
    out_ref[:, :, :1408] = late
    out_ref[:, :, 1408:] = early[:, :, :1024]
    o_ref[...] = early[:, :, 1024:]


def assemble_kernel(owned_ref, o_ref, out_ref):
    def put(lo, value):
        out_ref[:, lo : lo + value.shape[1]] = value.astype(BF16)

    shared = owned_ref[0, :, 768:1024]
    for zz in range(4):
        put(LX * zz, owned_ref[zz, :, :LX])
        put(1536 + LX * zz, owned_ref[zz, :, LX : 2 * LX])
        put(3328 + 128 * zz, owned_ref[zz, :, 1024:1152])
        put(4096 + 512 * zz, owned_ref[zz, :, 1408:1920])
        put(6144 + 512 * zz, owned_ref[zz, :, 1920:2432])
        put(8320 + 1024 * zz, o_ref[zz])
        if zz > 0:
            shared = shared + owned_ref[zz, :, 768:1024]
    put(3072, shared)
    first = owned_ref[0, :, 1152:1280] + owned_ref[1, :, 1152:1280]
    second = owned_ref[2, :, 1152:1280] + owned_ref[3, :, 1152:1280]
    put(3840, jnp.concatenate([first[:, :HDIM], second[:, :HDIM]], axis=1))
    put(3968, jnp.concatenate([first[:, HDIM:], second[:, HDIM:]], axis=1))
    extras = [owned_ref[zz, :, 1280:1302] for zz in range(4)]
    extras.append(jnp.zeros((extras[0].shape[0], 40), F32))
    put(8192, jnp.concatenate(extras, axis=1))


def unpack_kernel(nj, rj, core_ref, mine_ref, other_ref, w_ref, in_ref, mix_ref, gu_ref, ex_ref, down_ref, mo_ref, ao_ref):
    half = pl.program_id(0)
    core = core_ref[0]

    def write(src):
        total = src[:, :, :4096].reshape(128, 4096).astype(F32)
        in_ref[...] = total
        mix = jnp.sum(total * w_ref[...].astype(F32), axis=1, keepdims=True)
        mix_ref[...] = jnp.broadcast_to(mix, (128, 128))
        gu_ref[...] = src[:, :, 4096:8192].reshape(128, 4096).astype(F32)
        ex_ref[...] = src[:, :, 8192:8320].reshape(128, 128).astype(F32)
        for j in range(nj):
            for a in range(4):
                row = j * 4 * rj + a * rj
                part = src[j, :, 8320 + 1024 * a : 9344 + 1024 * a].astype(F32)

                @pl.when(half == 0)
                def _():
                    down_ref[row : row + rj] = part

                @pl.when(half == 1)
                def _():
                    if row < 384:
                        mo_ref[row : row + rj] = part
                    else:
                        ao_ref[row - 384 : row - 384 + rj] = part

    @pl.when(half == core)
    def _():
        write(mine_ref)

    @pl.when(half != core)
    def _():
        write(other_ref)


def leak_kernel(nk, pr, dy_ref, swx_ref, c_ref, out_ref):
    to_chunks(dotb(swx_ref[0] * dy_ref[0], c_ref[0], TN), out_ref, nk, pr, [])


def ssd_bwd_kernel(
    nctx, nk, pr, idx_ref, ext_ref, dtr_ref, st_ref, pv_ref, dy_ref, s_ref, g_ref, *refs
):
    dext_ref, ddt_ref, misc_ref = refs[-3:]
    base = block_base(idx_ref, nctx)
    st = st_ref[0]
    ext = ext_ref[0]
    pv = pv_ref[...]
    p = ssd_prep(ext, dtr_ref[0, 8:], st, base, pv)
    sel = p["sel"]
    x = p["xc"][:, :LX]
    bm = p["xc"][:, LX : LX + NSTATE]
    cm = p["xc"][:, LX + NSTATE :]
    bmb, cmb, xb = bm.astype(BF16), cm.astype(BF16), x.astype(BF16)
    dy = dy_ref[0]
    dyb = dy.astype(BF16)
    s_in = from_chunks(s_ref, nk, pr)
    g_out = from_chunks(g_ref, nk, pr)
    s_inb, g_outb = s_in.astype(BF16), g_out.astype(BF16)
    inter = dotb(cmb, bmb, NT)
    swx = dotf(p["sw"], sel, NN)
    fwx = dotf(p["fw"], sel, NN)
    skip = pv[7:8, :LX]
    lane = iota((BLK, 128), 1)
    d_inter = jnp.zeros((BLK, BLK), F32)
    drun = jnp.zeros((BLK, 128), F32)
    dx_parts = []
    col_rows = []
    for h in range(LOCAL_HEADS):
        sl = slice(h * HDIM, (h + 1) * HDIM)
        dec = decay_of(p, h)
        dt_row = p["dt_t"][h : h + 1]
        dec_inter = dec * inter
        d_mix = dotb(dyb[:, sl], xb[:, sl], NT)
        dx_parts.append(dotb(dec_inter * dt_row, dyb[:, sl], TN))
        d_inter = d_inter + d_mix * dec * dt_row
        f = d_mix * dec_inter
        row = jnp.sum(f * dt_row, axis=1, keepdims=True)
        drun = drun + jnp.where(lane == h, row, 0.0)
        col_rows.append(jnp.sum(f, axis=0, keepdims=True))
    col_rows.append(jnp.zeros((2, BLK), F32))
    cols = jnp.concatenate(col_rows, axis=0)
    pick = (iota((8, 128), 0) == iota((8, 128), 1)).astype(F32)
    col = dotf(cols, pick, TN)
    ddt = col
    drun = drun - p["dt"] * col
    dx = jnp.concatenate(dx_parts, axis=1) + skip * dy
    dcm = dotb(d_inter, bmb, NN)
    dbm = dotb(d_inter, cmb, TN)
    swdy = swx * dy
    yin = dotb(cmb, s_inb, NT)
    drun = drun + dotf(swdy * yin, sel, NT)
    dcm = dcm + dotb(swdy, s_inb, NN)
    back = dotb(bmb, g_outb, NT)
    dbm = dbm + dotb(fwx * x, g_outb, NN)
    dx = dx + fwx * back
    dfw = dotf(x * back, sel, NT)
    ddt = ddt + dfw * p["fd"]
    tail = dfw * p["fw"]
    drun = drun - tail
    carry = jnp.sum(s_in * g_out, axis=1, keepdims=True)
    sel_t = (iota((LX, 128), 0) // HDIM == iota((LX, 128), 1)).astype(F32)
    last = jnp.sum(tail, axis=0, keepdims=True) + p["sw"][BLK - 1 : BLK] * jnp.sum(
        carry * sel_t, axis=0, keepdims=True
    )
    drun = drun + jnp.where(iota((BLK, 128), 0) == BLK - 1, last, 0.0)
    dell = dotf(p["tri"], drun, TN)
    ddt = ddt - p["ea"] * dell
    ddtraw = ddt * sigmoid(p["lin"])
    ddtraw = jnp.where(lane < LOCAL_HEADS, ddtraw, 0.0)
    zero8 = jnp.zeros((8, 128), F32)
    ddt_ref[0] = jnp.concatenate([zero8, ddtraw], axis=0).astype(BF16)
    dxc = jnp.concatenate([dx, dbm, dcm], axis=1)
    dpre = dxc * (p["sg"] * (1.0 + p["pre"] * (1.0 - p["sg"])))
    dext = jnp.zeros((EXT, LCONV), F32)
    rows = []
    for tap in range(4):
        use = (p["tpos"] - (3 - tap)) >= p["stc"]
        term = jnp.where(use, dpre, 0.0)
        rows.append(jnp.sum(term * ext[5 + tap : 5 + tap + BLK], axis=0, keepdims=True))
        term = term * pv[tap : tap + 1]
        pieces = [jnp.zeros((5 + tap, LCONV), F32), term]
        if tap < 3:
            pieces.append(jnp.zeros((3 - tap, LCONV), F32))
        dext = dext + jnp.concatenate(pieces, axis=0)
    dext_ref[0] = dext.astype(BF16)
    rows.append(jnp.sum(dpre, axis=0, keepdims=True))
    pad = jnp.zeros((1, LCONV - LX), F32)
    rows.append(jnp.concatenate([jnp.sum(dy * x, axis=0, keepdims=True), pad], axis=1))
    pad = jnp.zeros((1, LCONV - 128), F32)
    rows.append(jnp.concatenate([jnp.sum(ddtraw, axis=0, keepdims=True), pad], axis=1))
    rows.append(jnp.concatenate([jnp.sum(dell * p["ell"], axis=0, keepdims=True), pad], axis=1))
    misc_ref[0] = jnp.concatenate(rows, axis=0)


def scan_kernel(reverse, n, pr, st_ref, dec_ref, *refs):
    out_ref = refs[-1]
    rows = LOCAL_HEADS * pr

    def step(j, half, s):
        out_ref[j, half] = s.astype(BF16)
        d = dec_ref[j, half, rows : rows + 16].astype(F32)
        d = d[:LOCAL_HEADS] + d[8 : 8 + LOCAL_HEADS]
        d = jnp.broadcast_to(d[:, None, :], (LOCAL_HEADS, pr, 128)).reshape(rows, 128)
        return d * s + st_ref[j, half, :rows].astype(F32)

    first, second = (1, 0) if reverse else (0, 1)
    s = jnp.zeros((rows, 128), F32)
    s = lax.fori_loop(0, n, lambda j, s: step(j, first, s), s)
    lax.fori_loop(0, n, lambda j, s: step(n - 1 - j, second, s), s)


def unit_of(u, gi):
    if u < 4:
        return 1, 0, u
    is_a = u < 5 + gi
    rowset = jnp.where(is_a, 0, 1)
    half = jnp.where(is_a, 0, 1)
    return rowset, half, jnp.where(is_a, u - 4, u - 5)


def unit_mask(nctx, gs, i, rowset, half, g, st):
    shape = (2 * BLK, gs * BLK)
    row = iota(shape, 0) % BLK
    col = iota(shape, 1)
    qpos = jnp.where(rowset == 0, i, 2 * nctx - 1 - i) * BLK + row
    block = g * gs + col // BLK
    kpos = jnp.where(half == 0, block, 2 * nctx - 1 - block) * BLK + col % BLK
    return (kpos <= qpos) & (kpos >= st)


def attn_fwd_kernel(nctx, gs, idx_ref, q_ref, kv_ref, st_ref, o_ref, lse_ref, s_ref, m_ref, l_ref, acc_ref):
    i = idx_ref[0]
    gi = i // gs
    m_ref[...] = jnp.full(m_ref.shape, NEG, F32)
    l_ref[...] = jnp.zeros(l_ref.shape, F32)
    acc_ref[...] = jnp.zeros(acc_ref.shape, F32)
    for u in range(9):
        rowset, half, g = unit_of(u, gi)
        kv = kv_ref[pl.ds(g * gs, gs), 0, half].reshape(gs * BLK, 128)
        s = dotb(q_ref[0, rowset], kv[:, :HDIM], NT)
        ok = unit_mask(nctx, gs, i, rowset, half, g, st_ref[0, rowset, :, :1])
        s = jnp.where(ok, s, NEG)
        s_ref[u] = s
        m_ref[rowset] = jnp.maximum(m_ref[rowset], jnp.max(s, axis=1, keepdims=True))
    for u in range(9):
        rowset, half, g = unit_of(u, gi)
        kv = kv_ref[pl.ds(g * gs, gs), 0, half].reshape(gs * BLK, 128)
        w = jnp.exp(s_ref[u] - m_ref[rowset, :, :1])
        l_ref[rowset] = l_ref[rowset] + jnp.sum(w, axis=1, keepdims=True)
        acc_ref[rowset] = acc_ref[rowset] + dotb(w, kv[:, HDIM:], NN)
    o_ref[0] = acc_ref[...] / l_ref[:, :, :HDIM]
    lse_ref[0] = m_ref[...] + jnp.log(l_ref[...])


def attn_bwd_kernel(
    nctx, gs, idx_ref, q_ref, kv_ref, st_ref, o_ref, lse_ref, do_ref, cos_ref, sin_ref, *refs
):
    out_ref, keep_ref, give_ref, del_ref, acc_ref, dq_ref = refs[-6:]
    i = idx_ref[0]
    gi = i // gs
    acc_ref[...] = jnp.zeros(acc_ref.shape, F32)
    dq_ref[...] = jnp.zeros(dq_ref.shape, F32)
    delta = jnp.sum(do_ref[0].astype(F32) * o_ref[0], axis=2, keepdims=True)
    del_ref[...] = jnp.broadcast_to(delta, del_ref.shape)
    for u in range(9):
        rowset, half, g = unit_of(u, gi)
        kv = kv_ref[pl.ds(g * gs, gs), 0, half].reshape(gs * BLK, 128)
        q = q_ref[0, rowset]
        do = do_ref[0, rowset]
        s = dotb(q, kv[:, :HDIM], NT)
        ok = unit_mask(nctx, gs, i, rowset, half, g, st_ref[0, rowset, :, :1])
        prob = jnp.exp(jnp.where(ok, s, NEG) - lse_ref[0, rowset, :, :1])
        dp = dotb(do, kv[:, HDIM:], NT)
        ds = (prob * (dp - del_ref[rowset, :, :1])).astype(BF16)
        dkv = jnp.concatenate([dotb(ds, q, TN), dotb(prob, do, TN)], axis=1)
        acc_ref[half, g] = acc_ref[half, g] + dkv
        dq_ref[rowset] = dq_ref[rowset] + dotb(ds, kv[:, :HDIM], NN)
    for half in range(2):
        parts = []
        for e in range(2):
            part = dq_ref[half, BLK * e : BLK * e + BLK] * HDIM**-0.5
            parts.append(turned(part, cos_ref[half], -sin_ref[half]))
        out_ref[0, half] = jnp.concatenate(parts, axis=1).astype(BF16)

    def write(even_ref, odd_ref):
        for src in range(4 * gs):
            g, at = src // gs, (src % gs) * BLK
            ref = odd_ref if src % 2 else even_ref
            for half in range(2):
                ref[src // 2, 0, half] = acc_ref[half, g, at : at + BLK].astype(BF16)

    @pl.when(i % 2 == 0)
    def _():
        write(keep_ref, give_ref)

    @pl.when(i % 2 == 1)
    def _():
        write(give_ref, keep_ref)


def spec(shape, index):
    return pl.BlockSpec(shape, index)


def per_pair(shape):
    return pl.BlockSpec((1,) + shape, lambda j: (j,) + (0,) * len(shape))


def whole(shape):
    return pl.BlockSpec(shape, lambda *j: (0,) * len(shape))


def chunk_spec(nk, rows):
    return pl.BlockSpec((1, nk, 1, rows, 128), lambda j: (j // 2, 0, j % 2, 0, 0))


ANY = pl.BlockSpec(memory_space=pl.ANY)
VMEM = pl.BlockSpec(memory_space=pltpu.VMEM)
SMEM = pl.BlockSpec(memory_space=pltpu.SMEM)
PARAMS = pltpu.CompilerParams(vmem_limit_bytes=16 * 1024 * 1024)
WIDER = pltpu.CompilerParams(vmem_limit_bytes=28 * 1024 * 1024)
WIDEST = pltpu.CompilerParams(vmem_limit_bytes=48 * 1024 * 1024)


def cost(flops, moved, trans=0):
    return pl.CostEstimate(flops=flops // 1000, bytes_accessed=moved // 1000, transcendentals=0)


def sds(shape, dtype):
    return jax.ShapeDtypeStruct(shape, dtype)


def exchange(parts, axis):
    return lax.all_to_all(parts, axis, 0, 0, tiled=True)


def spread(part, axis):
    return exchange(jnp.broadcast_to(part[None], (lax.axis_size(axis),) + part.shape), axis)


def shifts():
    return [(k, [(a, (a + k) % 4) for a in range(4)]) for k in (1, 2, 3)]


def ring_exchange(parts, z):
    out = parts
    for k, perm in shifts():
        sent = lax.dynamic_index_in_dim(parts, (z + k) % 4, 0, keepdims=False)
        got = lax.ppermute(sent, "fsdp", perm)
        out = lax.dynamic_update_index_in_dim(out, got, (z - k) % 4, 0)
    return out


def ring_spread(part, z):
    out = jnp.broadcast_to(part[None], (4,) + part.shape)
    for k, perm in shifts():
        got = lax.ppermute(part, "fsdp", perm)
        out = lax.dynamic_update_index_in_dim(out, got, (z - k) % 4, 0)
    return out


def ring_sum(rows, z):
    parts = rows.astype(BF16).reshape((4, -1) + rows.shape[1:])
    total = lax.dynamic_index_in_dim(parts, z, 0, keepdims=False).astype(F32)
    for k, perm in shifts():
        sent = lax.dynamic_index_in_dim(parts, (z + k) % 4, 0, keepdims=False)
        total = total + lax.ppermute(sent, "fsdp", perm).astype(F32)
    return total


def as_rows(column):
    high = lax.reduce_precision(column, 8, 7)
    pair = jnp.stack([high, column - high], axis=-2).astype(BF16)
    pads = [(0, 0)] * (pair.ndim - 2) + [(0, 14), (0, D - 128)]
    return jnp.pad(pair, pads)


def from_rows(rows):
    pair = rows[..., :2, :128].astype(F32)
    return pair[..., 0, :] + pair[..., 1, :]


def rms_of(v):
    return lax.rsqrt(jnp.mean(v * v, axis=-1, keepdims=True) + EPS)


def rms_back(v, r, dn):
    n = v * r
    return r * (dn - n * jnp.mean(dn * n, axis=-1, keepdims=True))


def matmul(a, b, dims=NN):
    return lax.dot_general(a, b, (dims, ((), ())), preferred_element_type=F32)


def per_device(
    tokens,
    doc_start,
    cotangent,
    w_in,
    w_dt,
    conv_weight,
    conv_bias,
    dt_bias,
    a_log,
    skip_gain,
    inner_gain,
    mamba_out,
    attn_out,
    mixer_gain,
    ffn_gain,
    w_gate_up,
    w_down,
):
    nctx = lax.axis_size("ctx")
    i = lax.axis_index("ctx")
    z = lax.axis_index("fsdp")
    nk = nctx // 4
    pr = HDIM // nk
    gs = nctx // 4
    rpc = 256 // nctx
    idx = i.astype(jnp.int32).reshape(1)
    last_device = i == nctx - 1
    up = [(a, a + 1) for a in range(nctx - 1)]
    down = [(b, a) for a, b in up]

    core = i % 2
    core_idx = core.astype(jnp.int32).reshape(1)
    pair = [(a, a ^ 1) for a in range(nctx)]
    send_in = pl.pallas_call(
        split_in_kernel,
        in_specs=[SMEM, VMEM],
        out_specs=VMEM,
        out_shape=sds((4, 128, LPROJ), BF16),
        compiler_params=PARAMS,
        cost_estimate=cost(0, 5 * 10**6),
        name="split_in",
    )(core_idx, w_in)
    send_gu = pl.pallas_call(
        split_gate_up_kernel,
        in_specs=[VMEM],
        out_specs=VMEM,
        out_shape=sds((4, 256, 1024), BF16),
        compiler_params=PARAMS,
        cost_estimate=cost(0, 4 * 10**6),
        name="split_gate_up",
    )(w_gate_up)
    tok = tokens[0]
    tails = tok[:, BLK - 3 :, :]
    halo_first = lax.ppermute(tails[0], "ctx", up)
    halo_second = lax.ppermute(tails[1], "ctx", down)
    halo = jnp.stack([halo_first, jnp.where(last_device, tails[0], halo_second)])
    starts_own = doc_start[0]
    flat = jnp.concatenate(
        [
            w_dt.reshape(-1),
            conv_weight.reshape(-1),
            conv_bias,
            mixer_gain,
            ffn_gain,
            (starts_own // 64).astype(BF16).reshape(-1),
            (starts_own % 64).astype(BF16).reshape(-1),
        ]
    )
    flat = jnp.pad(flat, (0, 10 * D - flat.shape[0])).reshape(2, 5, D)
    wide = ring_spread(jnp.concatenate([flat, halo, tok], axis=1), z)
    mine_in = exchange(send_in, "fsdp")
    other_in = lax.ppermute(mine_in, "ctx", pair)
    own_gu = ring_exchange(send_gu, z).reshape(D, 1024)
    grad_own = cotangent[0].reshape(128, D)
    grad_all = ring_spread(grad_own, z).reshape(512, D)
    flat = wide[:, :, :5, :].reshape(4, 10 * D)
    full_dt = flat[:, :6144].reshape(D, 24)
    own_dt = jnp.pad(lax.dynamic_slice_in_dim(full_dt, 6 * z, 6, axis=1), ((0, 0), (0, 122)))
    full_conv = flat[:, 6144:7936].reshape(4, 4, 448).transpose(1, 0, 2).reshape(4, 1792)
    full_bias = flat[:, 7936:8384].reshape(1, 1792)
    full_taps = jnp.concatenate([full_conv, full_bias], axis=0).astype(F32)
    mixer_scale = flat[:, 8384:8640].reshape(D).astype(F32)
    ffn_scale = flat[:, 8640:8896].reshape(D).astype(F32)
    starts = (
        flat[:, 8896:9024].astype(jnp.int32) * 64 + flat[:, 9024:9152].astype(jnp.int32)
    ).reshape(8, BLK)
    own_taps = jnp.concatenate(
        [lax.dynamic_slice_in_dim(full_taps, LX * z, LX, axis=1), full_taps[:, 1536:]], axis=1
    )

    def lanes(v):
        return jnp.pad(v.astype(F32), (0, LCONV - v.shape[0]))[None]

    pv = jnp.concatenate(
        [own_taps, lanes(dt_bias), lanes(a_log), lanes(jnp.repeat(skip_gain, HDIM))], axis=0
    )
    inner_scale = inner_gain.astype(F32)

    rows = 8 * EXT
    st_wide = jnp.broadcast_to(starts[:, :, None], (8, BLK, 128))
    blocks = jnp.stack([i, 2 * nctx - 1 - i])
    positions = blocks[:, None] * BLK + jnp.arange(BLK, dtype=jnp.int32)[None, :]
    freq = jnp.exp(
        jnp.arange(HDIM // 2, dtype=F32) * (-2.0 * math.log(ROPE_BASE) / HDIM)
    )
    angle = positions.astype(F32)[:, :, None] * freq
    cosine, sine = jnp.cos(angle), jnp.sin(angle)
    gate_z, conv_ext, raw_dt, query, kv_own, act_one, own_in = pl.pallas_call(
        proj_kernel,
        in_specs=[SMEM] + [VMEM] * 7 + [ANY] * 2,
        out_specs=[VMEM] * 7,
        out_shape=[
            sds((8, BLK, LX), F32),
            sds((8, EXT, LCONV), F32),
            sds((8, EXT, 128), F32),
            sds((4, 2, 2 * BLK, HDIM), BF16),
            sds((4, 2, BLK, 128), BF16),
            sds((rows, D), BF16),
            sds((D, LPROJ), BF16),
        ],
        compiler_params=WIDER,
        cost_estimate=cost(2 * 10**9, 8 * 10**6),
        name="proj",
    )(
        core_idx, wide.reshape(rows, D), mine_in, other_in, own_dt, mixer_scale[None],
        cosine, sine, pv, st_wide,
    )

    srows = LOCAL_HEADS * pr
    ssd_in = (idx, conv_ext, raw_dt, st_wide, pv)
    ssd_in_specs = [
        SMEM,
        per_pair((EXT, LCONV)),
        per_pair((EXT, 128)),
        per_pair((BLK, 128)),
        whole((8, LCONV)),
    ]
    y_local, swx, c_mat, state_out = pl.pallas_call(
        functools.partial(ssd_fwd_kernel, nctx, nk, pr),
        grid=(8,),
        in_specs=ssd_in_specs,
        out_specs=[
            per_pair((BLK, LX)),
            per_pair((BLK, LX)),
            per_pair((BLK, 128)),
            chunk_spec(nk, srows + 16),
        ],
        out_shape=[
            sds((8, BLK, LX), F32),
            sds((8, BLK, LX), F32),
            sds((8, BLK, 128), BF16),
            sds((4, nk, 2, srows + 16, 128), BF16),
        ],
        compiler_params=PARAMS,
        cost_estimate=cost(2 * 10**9, 6 * 10**6),
        name="ssd_fwd",
    )(*ssd_in)
    got = exchange(state_out.reshape(nctx, 2, srows + 16, 128), "ctx")
    kv_all = lax.all_gather(kv_own, "ctx")

    st_rows = jnp.broadcast_to(
        starts.reshape(4, 2, 1, BLK, 1), (4, 2, 2, BLK, 128)
    ).reshape(4, 2, 2 * BLK, 128)
    def chain(reverse, terms, *after):
        return pl.pallas_call(
            functools.partial(scan_kernel, reverse, nctx, pr),
            in_specs=[VMEM, VMEM] + [ANY] * len(after),
            out_specs=VMEM,
            out_shape=sds((nctx, 2, srows, 128), BF16),
            compiler_params=PARAMS,
            cost_estimate=cost(10**7, 3 * 10**6),
            name="chain",
        )(terms, got, *after)

    entry = exchange(chain(False, got, st_rows), "ctx").reshape(4, nk, 2, srows, 128)

    row_spec = pl.BlockSpec((1, 2, 2 * BLK, HDIM), lambda s: (s, 0, 0, 0))
    wide_spec = pl.BlockSpec((1, 2, 2 * BLK, 128), lambda s: (s, 0, 0, 0))
    kv_spec = pl.BlockSpec((nctx, 1, 2, BLK, 128), lambda s: (0, s, 0, 0, 0))
    attn_o, lse = pl.pallas_call(
        functools.partial(attn_fwd_kernel, nctx, gs),
        grid=(4,),
        in_specs=[SMEM, row_spec, kv_spec, wide_spec],
        out_specs=[row_spec, wide_spec],
        out_shape=[sds((4, 2, 2 * BLK, HDIM), F32), sds((4, 2, 2 * BLK, 128), F32)],
        scratch_shapes=[
            pltpu.VMEM((9, 2 * BLK, gs * BLK), F32),
            pltpu.VMEM((2, 2 * BLK, 128), F32),
            pltpu.VMEM((2, 2 * BLK, 128), F32),
            pltpu.VMEM((2, 2 * BLK, HDIM), F32),
        ],
        compiler_params=PARAMS,
        cost_estimate=cost(4 * 10**9, 8 * 10**6, 2 * 10**6),
        name="attn_fwd",
    )(idx, query, kv_all, st_rows)
    act_attn = (
        attn_o.reshape(4, 2, 2, BLK, HDIM).transpose(0, 1, 3, 2, 4).reshape(512, 128).astype(BF16)
    )

    mamba_y, scaled_u, squares = pl.pallas_call(
        functools.partial(ssd_out_kernel, nk, pr),
        grid=(8,),
        in_specs=[
            per_pair((BLK, LX)),
            per_pair((BLK, LX)),
            per_pair((BLK, 128)),
            chunk_spec(nk, srows),
            per_pair((BLK, LX)),
            whole((1, LX)),
        ]
        + [ANY] * 3,
        out_specs=[per_pair((BLK, LX)), per_pair((BLK, LX)), per_pair((BLK, 128))],
        out_shape=[
            sds((8, BLK, LX), F32),
            sds((8, BLK, LX), BF16),
            sds((8, BLK, 128), F32),
        ],
        compiler_params=PARAMS,
        cost_estimate=cost(10**9, 6 * 10**6),
        name="ssd_out",
    )(y_local, swx, c_mat, entry, gate_z, inner_scale[None], attn_o, own_gu, grad_all)

    def gather_sum(part_rows):
        got_rows = exchange(part_rows.astype(BF16).reshape((4, -1) + part_rows.shape[1:]), "fsdp")
        return jnp.sum(got_rows.astype(F32), axis=0)

    attn_mid = ring_sum(matmul(act_attn, attn_out), z)
    part_rows = pl.pallas_call(
        mid_kernel,
        in_specs=[VMEM] * 3 + [ANY],
        out_specs=VMEM,
        out_shape=sds((4, 144, D), BF16),
        compiler_params=PARAMS,
        cost_estimate=cost(4 * 10**8, 3 * 10**6),
        name="mid_part",
    )(scaled_u.reshape(512, LX), mamba_out, squares.reshape(512, 128), attn_mid)
    got_part = exchange(part_rows, "fsdp")
    scaled_mid = jnp.sum(got_part[:, :128].astype(F32), axis=0)
    square_sum = jnp.sum(from_rows(got_part[:, 128:]), axis=0)
    own_r = lax.rsqrt(square_sum.reshape(128, 1) * (1.0 / 1536) + EPS)
    mamba_mid = scaled_mid * own_r
    middle = tok.reshape(128, D).astype(F32) + mamba_mid + attn_mid
    mid_r = rms_of(middle)
    norm_two = middle * mid_r
    def spread_rows(values, column):
        sent = jnp.concatenate([values.astype(BF16), as_rows(column.reshape(128))], axis=0)
        got_rows = spread(sent, "fsdp").reshape(4, 144, D)
        return got_rows[:, :128].reshape(512, D), from_rows(got_rows[:, 128:]).reshape(512, 1)

    act_two, inner_r = spread_rows(norm_two * ffn_scale, own_r)
    y_flat = mamba_y.reshape(512, LX)
    z_flat = gate_z.reshape(512, LX)
    z_sig = sigmoid(z_flat)
    z_silu = z_flat * z_sig
    norm_in = y_flat * z_silu * inner_r
    act_mamba = (norm_in * inner_scale).astype(BF16)

    gate_up = matmul(act_two, own_gu)
    gate_val, up_val = gate_up[:, :512], gate_up[:, 512:]
    gate_sig = sigmoid(gate_val)
    gate_silu = gate_val * gate_sig
    inner = (gate_silu * up_val).astype(BF16)
    grad_inner = matmul(grad_all, w_down, NT)
    grad_gate = grad_inner * up_val * (gate_sig * (1.0 + gate_val * (1.0 - gate_sig)))
    grad_gu = jnp.concatenate([grad_gate, grad_inner * gate_silu], axis=1).astype(BF16)
    grad_act_two = gather_sum(matmul(grad_gu, own_gu, NT))
    grad_down = matmul(inner, grad_all, TN).astype(BF16)
    grad_gate_up = matmul(act_two, grad_gu, TN).astype(BF16)
    grad_ffn_gain = jnp.sum(grad_act_two * norm_two, axis=0)
    grad_middle = grad_own.astype(F32) + rms_back(middle, mid_r, grad_act_two * ffn_scale)
    own_mix = grad_middle.astype(BF16)
    own_dots = jnp.sum(own_mix.astype(F32) * mamba_mid, axis=1) * (1.0 / 1536)
    grad_mix, dots = spread_rows(own_mix, own_dots)

    down_part = pl.pallas_call(
        down_kernel,
        in_specs=[VMEM, VMEM, ANY],
        out_specs=VMEM,
        out_shape=sds((512, D), BF16),
        compiler_params=PARAMS,
        cost_estimate=cost(5 * 10**8, 3 * 10**6),
        name="down",
    )(inner, w_down, grad_mix)
    mixed = (middle + ring_sum(down_part, z)).astype(BF16).reshape(1, 2, BLK, D)

    grad_m = matmul(grad_mix, mamba_out, NT)
    grad_n = grad_m * inner_scale
    grad_attn = matmul(grad_mix, attn_out, NT).astype(BF16)
    grad_attn = (
        grad_attn.reshape(4, 2, BLK, 2, HDIM).transpose(0, 1, 3, 2, 4).reshape(4, 2, 2 * BLK, HDIM)
    )
    grad_mamba_out = matmul(act_mamba, grad_mix, TN).astype(BF16)
    grad_attn_out = matmul(act_attn, grad_mix, TN).astype(BF16)
    def halves(v):
        v = v.reshape(4, 2, 128, v.shape[-1])
        keep = lax.dynamic_index_in_dim(v, core, 1, keepdims=False)
        give = lax.dynamic_index_in_dim(v, 1 - core, 1, keepdims=False)
        return keep, lax.ppermute(give, "ctx", pair)

    kept, taken = halves(grad_gate_up)
    pair_gu = (kept.astype(F32) + taken.astype(F32)).astype(BF16)
    out_grads = jnp.concatenate([grad_mamba_out, grad_attn_out], axis=0)
    kept = jnp.where(core == 0, grad_down, out_grads)
    taken = lax.ppermute(jnp.where(core == 0, out_grads, grad_down), "ctx", pair)
    pair_o = (kept.astype(F32) + taken.astype(F32)).astype(BF16)
    grad_inner_gain = jnp.sum(grad_m * norm_in, axis=0)
    grad_u = inner_r * (grad_n - norm_in * dots)
    grad_y = (grad_u * z_silu).reshape(8, BLK, LX)
    grad_z = grad_u * y_flat * (z_sig * (1.0 + z_flat * (1.0 - z_sig)))

    leak = pl.pallas_call(
        functools.partial(leak_kernel, nk, pr),
        grid=(8,),
        in_specs=[per_pair((BLK, LX)), per_pair((BLK, LX)), per_pair((BLK, 128))],
        out_specs=chunk_spec(nk, srows),
        out_shape=sds((4, nk, 2, srows, 128), BF16),
        compiler_params=PARAMS,
        cost_estimate=cost(10**9, 4 * 10**6),
        name="leak",
    )(grad_y, swx, c_mat)
    got_leak = exchange(leak.reshape(nctx, 2, srows, 128), "ctx")
    half_kv_spec = pl.BlockSpec((nctx // 2, 1, 2, BLK, 128), lambda s: (0, s, 0, 0, 0))
    grad_query, keep_kv, give_kv = pl.pallas_call(
        functools.partial(attn_bwd_kernel, nctx, gs),
        grid=(4,),
        in_specs=[SMEM, row_spec, kv_spec, wide_spec, row_spec, wide_spec, row_spec]
        + [whole((2, BLK, HDIM // 2))] * 2
        + [ANY] * 5,
        out_specs=[
            pl.BlockSpec((1, 2, BLK, 128), lambda s: (s, 0, 0, 0)),
            half_kv_spec,
            half_kv_spec,
        ],
        out_shape=[
            sds((4, 2, BLK, 128), BF16),
            sds((nctx // 2, 4, 2, BLK, 128), BF16),
            sds((nctx // 2, 4, 2, BLK, 128), BF16),
        ],
        scratch_shapes=[
            pltpu.VMEM((2, 2 * BLK, 128), F32),
            pltpu.VMEM((2, 4, gs * BLK, 128), F32),
            pltpu.VMEM((2, 2 * BLK, HDIM), F32),
        ],
        compiler_params=PARAMS,
        cost_estimate=cost(8 * 10**9, 16 * 10**6, 2 * 10**6),
        name="attn_bwd",
    )(
        idx, query, kv_all, st_rows, attn_o, lse, grad_attn, cosine, sine,
        leak, grad_gate_up, grad_down, grad_mamba_out, grad_attn_out,
    )
    chained = chain(True, got_leak, give_kv)
    grad_exit = exchange(chained, "ctx").reshape(4, nk, 2, srows, 128)
    give_kv = pl.pallas_call(
        hold_kernel,
        in_specs=[VMEM, ANY],
        out_specs=VMEM,
        out_shape=sds(give_kv.shape, BF16),
        compiler_params=PARAMS,
        cost_estimate=cost(0, 4 * 10**6),
        name="hold",
    )(give_kv, chained)
    taken_kv = lax.ppermute(give_kv, "ctx", pair)
    pair_kv = (keep_kv.astype(F32) + taken_kv.astype(F32)).astype(BF16)
    nj = nctx // 2
    rj = 128 // nj
    groups = [[2 * j + c for j in range(nj)] for c in range(2)]
    grad_ext, grad_dt, misc = pl.pallas_call(
        functools.partial(ssd_bwd_kernel, nctx, nk, pr),
        grid=(8,),
        in_specs=ssd_in_specs
        + [per_pair((BLK, LX)), chunk_spec(nk, srows), chunk_spec(nk, srows)],
        out_specs=[per_pair((EXT, LCONV)), per_pair((EXT, 128)), per_pair((8, LCONV))],
        out_shape=[
            sds((8, EXT, LCONV), BF16),
            sds((8, EXT, 128), BF16),
            sds((8, 8, LCONV), F32),
        ],
        compiler_params=PARAMS,
        cost_estimate=cost(4 * 10**9, 8 * 10**6),
        name="ssd_bwd",
    )(*ssd_in, grad_y, entry, grad_exit)

    grad_dt = grad_dt.reshape(rows, 128)
    grad_dtw = matmul(act_one, grad_dt, TN)
    misc = jnp.sum(misc, axis=0)
    grad_skip = jnp.sum(misc[5, :LX].reshape(LOCAL_HEADS, HDIM), axis=1)
    small = jnp.concatenate(
        [misc[:5].reshape(-1), misc[6, :6], misc[7, :6], grad_skip, grad_inner_gain]
    )
    small = jnp.pad(small, (0, 3840 - small.shape[0])).reshape(1, 256, 15)
    small = jnp.broadcast_to(small, (4, 256, 15)).reshape(D, 15)
    extras = jnp.concatenate(
        [
            grad_dtw[:, :6],
            grad_ffn_gain[:, None],
            small,
            jnp.zeros((D, 106), F32),
        ],
        axis=1,
    ).astype(BF16)
    early = pl.pallas_call(
        functools.partial(pack_early_kernel, nj, rj),
        in_specs=[VMEM] * 2,
        out_specs=VMEM,
        out_shape=sds((nj, 4, rj, 2048), BF16),
        compiler_params=PARAMS,
        cost_estimate=cost(0, 4 * 10**6),
        name="pack_early",
    )(pair_gu, pair_o)

    def core_exchange(parts):
        return lax.all_to_all(parts, "ctx", 0, 0, axis_index_groups=groups, tiled=True)

    grad_proj = pl.pallas_call(
        functools.partial(dproj_kernel, nj),
        in_specs=[VMEM] * 6 + [ANY] * 2,
        out_specs=VMEM,
        out_shape=sds((8, EXT, LPROJ), BF16),
        compiler_params=PARAMS,
        cost_estimate=cost(2 * 10**6, 4 * 10**6),
        name="dproj",
    )(
        core_exchange(pair_kv), grad_z.reshape(8, BLK, LX), grad_ext, grad_query, cosine, sine,
        early, extras,
    ).reshape(rows, LPROJ)
    got_early = core_exchange(early)
    grad_act = matmul(grad_proj, own_in, NT) + matmul(grad_dt, own_dt, NT)

    got_act = ring_sum(grad_act, z).reshape(2, EXT, D)
    halo_back = got_act[:, 5:8].astype(BF16)
    to_first = lax.ppermute(halo_back[0], "ctx", down).astype(F32)
    to_second = lax.ppermute(jnp.where(last_device, 0.0, halo_back[1]), "ctx", up).astype(F32)
    to_first = to_first + jnp.where(last_device, got_act[1, 5:8], 0.0)
    tail_add = jnp.pad(jnp.stack([to_first, to_second]), ((0, 0), (BLK - 3, 0), (0, 0)))
    own_act = (got_act[:, 8:] + tail_add).reshape(128, D)
    hidden = tok.reshape(128, D).astype(F32)
    grad_tokens = grad_middle + rms_back(hidden, rms_of(hidden), own_act * mixer_scale)
    grad_tokens = grad_tokens.reshape(1, 2, BLK, D)

    grad_in = matmul(act_one, grad_proj, TN).astype(BF16)
    kept_in, taken_in = halves(grad_in)
    kept_ex, taken_ex = halves(extras)
    sent = pl.pallas_call(
        functools.partial(pack_kernel, nj, rj),
        in_specs=[VMEM] * 4 + [ANY],
        out_specs=VMEM,
        out_shape=sds((nj, 4, rj, 1408), BF16),
        compiler_params=PARAMS,
        cost_estimate=cost(0, 7 * 10**6),
        name="pack",
    )(kept_in, taken_in, kept_ex, taken_ex, got_early)
    summed, summed_o = pl.pallas_call(
        functools.partial(totals_kernel, nj),
        in_specs=[VMEM, VMEM, ANY, ANY],
        out_specs=[VMEM, VMEM],
        out_shape=[sds((4, rj, 2432), F32), sds((4, rj, 1024), F32)],
        compiler_params=PARAMS,
        cost_estimate=cost(2 * 10**6, 4 * 10**6),
        name="totals",
    )(core_exchange(sent), got_early, got_act, mixed)
    owned = exchange(summed, "fsdp")
    final = pl.pallas_call(
        assemble_kernel,
        in_specs=[VMEM] * 2,
        out_specs=VMEM,
        out_shape=sds((rj, 12416), BF16),
        compiler_params=PARAMS,
        cost_estimate=cost(0, 10**6),
        name="assemble",
    )(owned, summed_o)
    mine_all = core_exchange(jnp.broadcast_to(final[None], (nj, rj, 12416)))
    other_all = lax.ppermute(mine_all, "ctx", pair)
    half_spec = pl.BlockSpec((128, 4096), lambda h: (h, 0))
    total_in, mixer_dot, total_gate_up, extra, total_down, total_mamba_out, total_attn_out = pl.pallas_call(
        functools.partial(unpack_kernel, nj, rj),
        grid=(2,),
        in_specs=[SMEM, whole((nj, rj, 12416)), whole((nj, rj, 12416)), half_spec],
        out_specs=[
            half_spec,
            pl.BlockSpec((128, 128), lambda h: (h, 0)),
            half_spec,
            pl.BlockSpec((128, 128), lambda h: (h, 0)),
            whole((512, 1024)),
            whole((384, 1024)),
            whole((128, 1024)),
        ],
        out_shape=[
            sds((256, 4096), F32),
            sds((256, 128), F32),
            sds((256, 4096), F32),
            sds((256, 128), F32),
            sds((512, 1024), F32),
            sds((384, 1024), F32),
            sds((128, 1024), F32),
        ],
        compiler_params=WIDEST,
        cost_estimate=cost(0, 10**7),
        name="unpack",
    )(core_idx, mine_all, other_all, w_in)
    extra = extra[:, :88].reshape(256, 4, 22)
    total_dt = extra[:, :, :6].reshape(256, 24)
    mixer_dot = mixer_dot[:, 0] + jnp.sum(total_dt * w_dt.astype(F32), axis=1)
    total_mixer = mixer_dot / mixer_gain.astype(F32)
    total_ffn = jnp.sum(extra[:, :, 6], axis=1)
    small = extra[:, :, 7:22].transpose(1, 0, 2).reshape(4, 3840)
    taps = small[:, :3200].reshape(4, 5, LCONV)
    taps = jnp.concatenate(
        [
            taps[:, :, :LX].transpose(1, 0, 2).reshape(5, 1536),
            jnp.sum(taps[:, :, LX:], axis=0),
        ],
        axis=1,
    )
    taps = lax.dynamic_slice_in_dim(taps, 448 * z, 448, axis=1)
    mine = lax.dynamic_slice_in_dim(small, z, 1, axis=0)[0]
    return (
        mixed,
        grad_tokens,
        total_in,
        total_dt,
        taps[:4],
        taps[4],
        mine[3200:3206],
        mine[3206:3212],
        mine[3212:3218],
        mine[3218:3602],
        total_mamba_out,
        total_attn_out,
        total_mixer,
        total_ffn,
        total_gate_up,
        total_down,
    )


def solution(mesh):
    row = P("fsdp", None)
    vec = P("fsdp")
    act = P("fsdp", None, "ctx", None)
    return jax.shard_map(
        per_device,
        mesh=mesh,
        in_specs=(
            act, P("fsdp", None, "ctx"), act, row, row, P(None, "fsdp"), vec, vec, vec, vec, vec,
            row, row, vec, vec, row, row,
        ),
        out_specs=(
            act, act, row, row, P(None, "fsdp"), vec, vec, vec, vec, vec, row, row, vec, vec, row, row,
        ),
        check_vma=False,
    )
```

```python
import functools
import math

import jax
import jax.numpy as jnp
from jax import lax
from jax.experimental import pallas as pl
from jax.experimental.pallas import tpu as pltpu
from jax.sharding import PartitionSpec as P

D = 1024
FF = 2048
BLK = 64
HDIM = 64
NSTATE = 128
LOCAL_HEADS = 6
LX = 384
LBC = 256
LCONV = LX + LBC
LPROJ = 1280
EXT = 72
EPS = 1e-05
ROPE_BASE = 100000000000.0
NEG = -1e30
F32 = jnp.float32
BF16 = jnp.bfloat16
NN = ((1,), (0,))
NT = ((1,), (1,))
TN = ((0,), (0,))


def dotf(a, b, dims):
    return lax.dot_general(
        a, b, (dims, ((), ())), precision=lax.Precision.HIGHEST, preferred_element_type=F32
    )


def dotb(a, b, dims):
    return lax.dot_general(
        a.astype(BF16), b.astype(BF16), (dims, ((), ())), preferred_element_type=F32
    )


def iota(shape, dim):
    return lax.broadcasted_iota(jnp.int32, shape, dim)


def sigmoid(v):
    return 1.0 / (1.0 + jnp.exp(-v))


def ssd_prep(ext, dtr, st, base, pv):
    tpos = base + iota((BLK, LCONV), 0)
    stc = jnp.broadcast_to(st[:, :1], (BLK, LCONV))
    pre = jnp.broadcast_to(pv[4:5], (BLK, LCONV))
    for tap in range(4):
        use = (tpos - (3 - tap)) >= stc
        pre = pre + jnp.where(use, pv[tap : tap + 1] * ext[5 + tap : 5 + tap + BLK], 0.0)
    sg = sigmoid(pre)
    xc = pre * sg
    lin = dtr + pv[5:6, :128]
    dt = jnp.maximum(lin, 0.0) + jnp.log1p(jnp.exp(-jnp.abs(lin)))
    ea = jnp.exp(pv[6:7, :128])
    ell = -dt * ea
    tri = (iota((BLK, BLK), 1) <= iota((BLK, BLK), 0)).astype(F32)
    eye = (iota((BLK, BLK), 1) == iota((BLK, BLK), 0)).astype(F32)
    run = dotf(tri, ell, NN)
    run_t = dotf(ell, tri, ((0,), (1,)))
    dt_t = dotf(dt, eye, TN)
    allowed = (iota((BLK, BLK), 1) <= iota((BLK, BLK), 0)) & (
        (base + iota((BLK, BLK), 1)) >= st[:, :BLK]
    )
    sw = jnp.where(st < base, jnp.exp(run), 0.0)
    last_ok = (base + iota((BLK, 128), 0)) >= st[BLK - 1 : BLK]
    fwd_decay = jnp.where(
        last_ok, jnp.exp(jnp.where(last_ok, run[BLK - 1 : BLK] - run, 0.0)), 0.0
    )
    sel = (iota((128, LX), 1) // HDIM == iota((128, LX), 0)).astype(F32)
    return dict(
        pre=pre, sg=sg, xc=xc, lin=lin, dt=dt, ea=ea, ell=ell, run=run, run_t=run_t, dt_t=dt_t,
        allowed=allowed, sw=sw, fd=fwd_decay, fw=fwd_decay * dt, sel=sel, tri=tri, tpos=tpos, stc=stc,
    )


def decay_of(p, h):
    spread = p["run"][:, h : h + 1] - p["run_t"][h : h + 1, :]
    return jnp.where(p["allowed"], jnp.exp(jnp.where(p["allowed"], spread, 0.0)), 0.0)


def to_chunks(state, out_ref, nk, pr, extra):
    for k in range(nk):
        rows = [state[h * HDIM + k * pr : h * HDIM + (k + 1) * pr] for h in range(LOCAL_HEADS)]
        out_ref[0, k, 0] = jnp.concatenate(rows + extra, axis=0).astype(BF16)


def from_chunks(ref, nk, pr):
    parts = [ref[0, k, 0].astype(F32) for k in range(nk)]
    rows = []
    for h in range(LOCAL_HEADS):
        for k in range(nk):
            rows.append(parts[k][h * pr : (h + 1) * pr])
    return jnp.concatenate(rows, axis=0)


def block_base(idx_ref, nctx):
    half = pl.program_id(0) % 2
    i = idx_ref[0]
    return jnp.where(half == 0, i, 2 * nctx - 1 - i) * BLK


def turned(v, cosine, sine):
    a, b = v[:, : HDIM // 2], v[:, HDIM // 2 :]
    return jnp.concatenate([a * cosine - b * sine, b * cosine + a * sine], axis=1)


def proj_kernel(core_ref, x_ref, mine_ref, other_ref, wdt_ref, gain_ref, cos_ref, sin_ref, *refs):
    z_ref, ext_ref, dtr_ref, q_ref, kv_ref, act_ref, w_ref = refs[-7:]
    x = x_ref[...].astype(F32)
    r = lax.rsqrt(jnp.mean(x * x, axis=1, keepdims=True) + EPS)
    act_ref[...] = (x * r * gain_ref[...]).astype(BF16)

    def place(even_ref, odd_ref):
        for src in range(4):
            w_ref[256 * src : 256 * src + 128] = even_ref[src]
            w_ref[256 * src + 128 : 256 * src + 256] = odd_ref[src]

    @pl.when(core_ref[0] == 0)
    def _():
        place(mine_ref, other_ref)

    @pl.when(core_ref[0] == 1)
    def _():
        place(other_ref, mine_ref)

    a = act_ref[...]

    def columns(lo, width):
        p = lax.dot_general(a, w_ref[:, lo : lo + width], (NN, ((), ())), preferred_element_type=F32)
        return p.reshape(8, EXT, width)

    p = columns(1024, 256)
    for j in range(8):
        seq, half = j // 2, j % 2
        own = p[j, 8:]
        cosine, sine = cos_ref[half], sin_ref[half]
        for e in range(2):
            q = turned(own[:, HDIM * e : HDIM * e + HDIM], cosine, sine).astype(BF16)
            q = (q.astype(F32) * HDIM**-0.5).astype(BF16)
            q_ref[seq, half, BLK * e : BLK * e + BLK] = q
        k = turned(own[:, 128:192], cosine, sine)
        kv_ref[seq, half] = jnp.concatenate([k, own[:, 192:]], axis=1).astype(BF16)
    z_ref[:, :, :256] = columns(0, 256)[:, 8:]
    both = columns(256, 256)
    z_ref[:, :, 256:] = both[:, 8:, :128]
    ext_ref[:, :, :128] = both[:, :, 128:]
    ext_ref[:, :, 128:384] = columns(512, 256)
    ext_ref[:, :, 384:] = columns(768, 256)
    p = lax.dot_general(a, wdt_ref[...], (NN, ((), ())), preferred_element_type=F32)
    dtr_ref[...] = p.reshape(8, EXT, 128)


def dproj_kernel(n, got_ref, z_ref, ext_ref, q_ref, cos_ref, sin_ref, *refs):
    out_ref = refs[-1]

    def step(j, acc):
        return acc + got_ref[j].astype(F32)

    kv = lax.fori_loop(1, n, step, got_ref[0].astype(F32))
    out_ref[:, :8] = jnp.zeros((8, 8, LPROJ), BF16)
    out_ref[:, :, LX : LX + LCONV] = ext_ref[...]
    for j in range(8):
        own = kv[j // 2, j % 2]
        k = turned(own[:, :HDIM], cos_ref[j % 2], -sin_ref[j % 2])
        out_ref[j, 8:, :LX] = z_ref[j]
        out_ref[j, 8:, 1024:1152] = q_ref[j // 2, j % 2]
        out_ref[j, 8:, 1152:] = jnp.concatenate([k, own[:, HDIM:]], axis=1).astype(BF16)


def mid_kernel(u_ref, w_ref, ss_ref, dep_ref, out_ref):
    eye = iota((128, 128), 0) == iota((128, 128), 1)
    for a in range(4):
        part = lax.dot_general(
            u_ref[128 * a : 128 * a + 128], w_ref[...], (NN, ((), ())), preferred_element_type=F32
        )
        out_ref[a, :128] = part.astype(BF16)
        row = jnp.sum(jnp.where(eye, ss_ref[128 * a : 128 * a + 128], 0.0), axis=0, keepdims=True)
        high = row.astype(BF16).astype(F32)
        pair = jnp.concatenate([high, row - high, jnp.zeros((14, 128), F32)], axis=0)
        pair = jnp.concatenate([pair, jnp.zeros((16, D - 128), F32)], axis=1)
        out_ref[a, 128:] = pair.astype(BF16)


def hold_kernel(value_ref, dep_ref, out_ref):
    out_ref[...] = value_ref[...]


def down_kernel(inner_ref, w_ref, dep_ref, out_ref):
    out_ref[...] = lax.dot_general(
        inner_ref[...], w_ref[...], (NN, ((), ())), preferred_element_type=F32
    ).astype(BF16)


def ssd_fwd_kernel(nctx, nk, pr, idx_ref, ext_ref, dtr_ref, st_ref, pv_ref, y_ref, swx_ref, c_ref, s_ref):
    base = block_base(idx_ref, nctx)
    st = st_ref[0]
    p = ssd_prep(ext_ref[0], dtr_ref[0, 8:], st, base, pv_ref[...])
    x = p["xc"][:, :LX]
    bm = p["xc"][:, LX : LX + NSTATE].astype(BF16)
    cm = p["xc"][:, LX + NSTATE :].astype(BF16)
    inter = dotb(cm, bm, NT)
    xb = x.astype(BF16)
    outs = []
    for h in range(LOCAL_HEADS):
        mix = decay_of(p, h) * inter * p["dt_t"][h : h + 1]
        outs.append(dotb(mix, xb[:, h * HDIM : (h + 1) * HDIM], NN))
    y_ref[0] = jnp.concatenate(outs, axis=1) + pv_ref[7:8, :LX] * x
    swx_ref[0] = dotf(p["sw"], p["sel"], NN)
    c_ref[0] = cm
    fwx = dotf(p["fw"], p["sel"], NN)
    state = dotb(fwx * x, bm, TN)
    dec = jnp.where(
        st[BLK - 1 : BLK] < base,
        jnp.broadcast_to(jnp.exp(p["run_t"][:8, BLK - 1 : BLK]), (8, 128)),
        0.0,
    )
    high = dec.astype(BF16).astype(F32)
    to_chunks(state, s_ref, nk, pr, [high, dec - high])


def ssd_out_kernel(nk, pr, y_ref, swx_ref, c_ref, s_ref, z_ref, gain_ref, *refs):
    out_ref, u_ref, ss_ref = refs[-3:]
    s_in = from_chunks(s_ref, nk, pr)
    y = y_ref[0] + swx_ref[0] * dotb(c_ref[0], s_in, NT)
    z = z_ref[0]
    u = y * (z * sigmoid(z))
    out_ref[0] = y
    u_ref[0] = (u * gain_ref[...]).astype(BF16)
    ss_ref[0] = jnp.broadcast_to(jnp.sum(u * u, axis=1, keepdims=True), (BLK, 128))


def split_in_kernel(core_ref, full_ref, out_ref):
    w_ref = full_ref.at[pl.ds(pl.multiple_of(core_ref[0] * 128, 128), 128)]
    for zz in range(4):
        kv = HDIM * (zz // 2)
        out_ref[zz, :, :LX] = w_ref[:, LX * zz : LX * zz + LX]
        out_ref[zz, :, LX : 2 * LX] = w_ref[:, 1536 + LX * zz : 1536 + LX * zz + LX]
        out_ref[zz, :, 2 * LX : 1024] = w_ref[:, 3072:3328]
        out_ref[zz, :, 1024:1152] = w_ref[:, 3328 + 128 * zz : 3456 + 128 * zz]
        out_ref[zz, :, 1152:1280] = jnp.concatenate(
            [w_ref[:, 3840 + kv : 3904 + kv], w_ref[:, 3968 + kv : 4032 + kv]], axis=1
        )


def split_gate_up_kernel(z_ref, w_ref, *outs):
    for k in range(4):
        lo = pl.multiple_of(lax.rem(z_ref[0] + k, 4) * 512, 512)
        outs[k][:, :512] = w_ref[:, pl.ds(lo, 512)]
        outs[k][:, 512:] = w_ref[:, pl.ds(FF + lo, 512)]


def place_kernel(z_ref, *refs):
    outs = refs[8:]
    for which in range(2):
        for k in range(4):
            outs[which][lax.rem(z_ref[0] + 4 - k, 4)] = refs[4 * which + k][...]


def total_kernel(n, got_ref, *refs):
    def step(j, acc):
        return acc + got_ref[j].astype(F32)

    refs[-1][...] = lax.fori_loop(1, n, step, got_ref[0].astype(F32))


def pack_kernel(nj, rj, kin_ref, gin_ref, kex_ref, gex_ref, dep_ref, out_ref):
    for a in range(4):
        part = (kin_ref[a].astype(F32) + gin_ref[a].astype(F32)).astype(BF16)
        out_ref[:, a, :, :LPROJ] = part.reshape(nj, rj, LPROJ)
        part = (kex_ref[a].astype(F32) + gex_ref[a].astype(F32)).astype(BF16)
        out_ref[:, a, :, LPROJ:] = part.reshape(nj, rj, 128)


def pack_early_kernel(nj, rj, gu_ref, o_ref, out_ref):
    for a in range(4):
        out_ref[:, a, :, :1024] = gu_ref[a].reshape(nj, rj, 1024)
    out_ref[:, :, :, 1024:] = o_ref[...].reshape(nj, 4, rj, 1024)


def assemble_kernel(owned_ref, *refs):
    out_ref = refs[-1]

    def put(lo, value):
        out_ref[:, lo : lo + value.shape[1]] = value.astype(BF16)

    shared = owned_ref[0, :, 768:1024]
    for zz in range(4):
        put(LX * zz, owned_ref[zz, :, :LX])
        put(1536 + LX * zz, owned_ref[zz, :, LX : 2 * LX])
        put(3328 + 128 * zz, owned_ref[zz, :, 1024:1152])
        if zz > 0:
            shared = shared + owned_ref[zz, :, 768:1024]
    put(3072, shared)
    first = owned_ref[0, :, 1152:1280] + owned_ref[1, :, 1152:1280]
    second = owned_ref[2, :, 1152:1280] + owned_ref[3, :, 1152:1280]
    put(3840, jnp.concatenate([first[:, :HDIM], second[:, :HDIM]], axis=1))
    put(3968, jnp.concatenate([first[:, HDIM:], second[:, HDIM:]], axis=1))
    extras = [owned_ref[zz, :, 1280:1302] for zz in range(4)]
    extras.append(jnp.zeros((extras[0].shape[0], 40), F32))
    put(4096, jnp.concatenate(extras, axis=1))


def assemble_early_kernel(gu_ref, o_ref, dep_ref, out_ref):
    for zz in range(4):
        out_ref[:, 512 * zz : 512 * zz + 512] = gu_ref[zz, :, :512]
        out_ref[:, 2048 + 512 * zz : 2560 + 512 * zz] = gu_ref[zz, :, 512:]
        out_ref[:, 4096 + 1024 * zz : 5120 + 1024 * zz] = o_ref[zz].astype(BF16)


def by_half(core_ref, mine_ref, other_ref, write):
    half = pl.program_id(0)

    @pl.when(half == core_ref[0])
    def _():
        write(mine_ref, half)

    @pl.when(half != core_ref[0])
    def _():
        write(other_ref, half)


def unpack_early_kernel(nj, rj, core_ref, mine_ref, other_ref, gu_ref, down_ref, mo_ref, ao_ref):
    def write(src, half):
        gu_ref[...] = src[:, :, :4096].reshape(128, 4096).astype(F32)
        for j in range(nj):
            for a in range(4):
                row = j * 4 * rj + a * rj
                part = src[j, :, 4096 + 1024 * a : 5120 + 1024 * a].astype(F32)

                @pl.when(half == 0)
                def _():
                    down_ref[row : row + rj] = part

                @pl.when(half == 1)
                def _():
                    if row < 384:
                        mo_ref[row : row + rj] = part
                    else:
                        ao_ref[row - 384 : row - 384 + rj] = part

    by_half(core_ref, mine_ref, other_ref, write)


def unpack_kernel(core_ref, mine_ref, other_ref, w_ref, dep_ref, in_ref, mix_ref, ex_ref):
    def write(src, half):
        total = src[:, :, :4096].reshape(128, 4096).astype(F32)
        in_ref[...] = total
        mix = jnp.sum(total * w_ref[...].astype(F32), axis=1, keepdims=True)
        mix_ref[...] = jnp.broadcast_to(mix, (128, 128))
        ex_ref[...] = src[:, :, 4096:].reshape(128, 128).astype(F32)

    by_half(core_ref, mine_ref, other_ref, write)


def post_mix_kernel(
    nk, pr, rows_ref, rtail_ref, mo_ref, ao_ref, y_ref, z_ref, gain_ref, swx_ref, c_ref,
    mix_ref, do_ref, act_ref, dy_ref, dz_ref, gg_ref, leak_ref
):
    eye = iota((128, 128), 0) == iota((128, 128), 1)

    def column(pair):
        pair = pair.astype(F32)
        return jnp.sum(jnp.where(eye, pair[:1] + pair[1:2], 0.0), axis=1, keepdims=True)

    mix = rows_ref[:, :128].reshape(512, D)
    mix_ref[...] = mix
    d_act = lax.dot_general(mix, mo_ref[...], (NT, ((), ())), preferred_element_type=F32)
    d_attn = lax.dot_general(mix, ao_ref[...], (NT, ((), ())), preferred_element_type=F32)
    gain = gain_ref[...]
    gg = jnp.zeros((1, LX), F32)
    for s in range(4):
        own = slice(128 * s, 128 * s + 128)
        dots = column(rows_ref[s, 128:144, :128])
        r = column(rtail_ref[s])
        y = y_ref[2 * s : 2 * s + 2].reshape(128, LX)
        z = z_ref[2 * s : 2 * s + 2].reshape(128, LX)
        sig = sigmoid(z)
        silu = z * sig
        n = y * silu * r
        act_ref[own] = (n * gain).astype(BF16)
        gg = gg + jnp.sum(d_act[own] * n, axis=0, keepdims=True)
        du = r * (d_act[own] * gain - n * dots)
        dy = du * silu
        dy_ref[2 * s : 2 * s + 2] = dy.reshape(2, BLK, LX)
        dz = du * y * (sig * (1.0 + z * (1.0 - sig)))
        dz_ref[2 * s : 2 * s + 2] = dz.astype(BF16).reshape(2, BLK, LX)
        for half in range(2):
            mine = slice(BLK * half, BLK * half + BLK)
            for e in range(2):
                part = d_attn[128 * s + BLK * half : 128 * s + BLK * half + BLK]
                do_ref[s, half, BLK * e : BLK * e + BLK] = part[
                    :, HDIM * e : HDIM * e + HDIM
                ].astype(BF16)
            state = dotb(swx_ref[2 * s + half] * dy[mine], c_ref[2 * s + half], TN)
            for k in range(nk):
                piece = [
                    state[h * HDIM + k * pr : h * HDIM + (k + 1) * pr] for h in range(LOCAL_HEADS)
                ]
                leak_ref[s, k, half] = jnp.concatenate(piece, axis=0).astype(BF16)
    gg_ref[...] = gg


def grad_act_kernel(dp_ref, w_ref, ddt_ref, wdt_ref, dep_ref, out_ref):
    for lo in range(0, D, 256):
        part = lax.dot_general(
            dp_ref[...], w_ref[lo : lo + 256], (NT, ((), ())), preferred_element_type=F32
        )
        part = part + lax.dot_general(
            ddt_ref[...], wdt_ref[lo : lo + 256], (NT, ((), ())), preferred_element_type=F32
        )
        out_ref[:, lo : lo + 256] = part.astype(BF16)


def ssd_bwd_kernel(
    nctx, nk, pr, idx_ref, ext_ref, dtr_ref, st_ref, pv_ref, dy_ref, s_ref, g_ref, *refs
):
    dext_ref, ddt_ref, misc_ref = refs[-3:]
    base = block_base(idx_ref, nctx)
    st = st_ref[0]
    ext = ext_ref[0]
    pv = pv_ref[...]
    p = ssd_prep(ext, dtr_ref[0, 8:], st, base, pv)
    sel = p["sel"]
    x = p["xc"][:, :LX]
    bm = p["xc"][:, LX : LX + NSTATE]
    cm = p["xc"][:, LX + NSTATE :]
    bmb, cmb, xb = bm.astype(BF16), cm.astype(BF16), x.astype(BF16)
    dy = dy_ref[0]
    dyb = dy.astype(BF16)
    s_in = from_chunks(s_ref, nk, pr)
    g_out = from_chunks(g_ref, nk, pr)
    s_inb, g_outb = s_in.astype(BF16), g_out.astype(BF16)
    inter = dotb(cmb, bmb, NT)
    swx = dotf(p["sw"], sel, NN)
    fwx = dotf(p["fw"], sel, NN)
    skip = pv[7:8, :LX]
    lane = iota((BLK, 128), 1)
    d_inter = jnp.zeros((BLK, BLK), F32)
    drun = jnp.zeros((BLK, 128), F32)
    dx_parts = []
    col_rows = []
    for h in range(LOCAL_HEADS):
        sl = slice(h * HDIM, (h + 1) * HDIM)
        dec = decay_of(p, h)
        dt_row = p["dt_t"][h : h + 1]
        dec_inter = dec * inter
        d_mix = dotb(dyb[:, sl], xb[:, sl], NT)
        dx_parts.append(dotb(dec_inter * dt_row, dyb[:, sl], TN))
        d_inter = d_inter + d_mix * dec * dt_row
        f = d_mix * dec_inter
        row = jnp.sum(f * dt_row, axis=1, keepdims=True)
        drun = drun + jnp.where(lane == h, row, 0.0)
        col_rows.append(jnp.sum(f, axis=0, keepdims=True))
    col_rows.append(jnp.zeros((2, BLK), F32))
    cols = jnp.concatenate(col_rows, axis=0)
    pick = (iota((8, 128), 0) == iota((8, 128), 1)).astype(F32)
    col = dotf(cols, pick, TN)
    ddt = col
    drun = drun - p["dt"] * col
    dx = jnp.concatenate(dx_parts, axis=1) + skip * dy
    dcm = dotb(d_inter, bmb, NN)
    dbm = dotb(d_inter, cmb, TN)
    swdy = swx * dy
    yin = dotb(cmb, s_inb, NT)
    drun = drun + dotf(swdy * yin, sel, NT)
    dcm = dcm + dotb(swdy, s_inb, NN)
    back = dotb(bmb, g_outb, NT)
    dbm = dbm + dotb(fwx * x, g_outb, NN)
    dx = dx + fwx * back
    dfw = dotf(x * back, sel, NT)
    ddt = ddt + dfw * p["fd"]
    tail = dfw * p["fw"]
    drun = drun - tail
    carry = jnp.sum(s_in * g_out, axis=1, keepdims=True)
    sel_t = (iota((LX, 128), 0) // HDIM == iota((LX, 128), 1)).astype(F32)
    last = jnp.sum(tail, axis=0, keepdims=True) + p["sw"][BLK - 1 : BLK] * jnp.sum(
        carry * sel_t, axis=0, keepdims=True
    )
    drun = drun + jnp.where(iota((BLK, 128), 0) == BLK - 1, last, 0.0)
    dell = dotf(p["tri"], drun, TN)
    ddt = ddt - p["ea"] * dell
    ddtraw = ddt * sigmoid(p["lin"])
    ddtraw = jnp.where(lane < LOCAL_HEADS, ddtraw, 0.0)
    zero8 = jnp.zeros((8, 128), F32)
    ddt_ref[0] = jnp.concatenate([zero8, ddtraw], axis=0).astype(BF16)
    dxc = jnp.concatenate([dx, dbm, dcm], axis=1)
    dpre = dxc * (p["sg"] * (1.0 + p["pre"] * (1.0 - p["sg"])))
    dext = jnp.zeros((EXT, LCONV), F32)
    rows = []
    for tap in range(4):
        use = (p["tpos"] - (3 - tap)) >= p["stc"]
        term = jnp.where(use, dpre, 0.0)
        rows.append(jnp.sum(term * ext[5 + tap : 5 + tap + BLK], axis=0, keepdims=True))
        term = term * pv[tap : tap + 1]
        pieces = [jnp.zeros((5 + tap, LCONV), F32), term]
        if tap < 3:
            pieces.append(jnp.zeros((3 - tap, LCONV), F32))
        dext = dext + jnp.concatenate(pieces, axis=0)
    dext_ref[0] = dext.astype(BF16)
    rows.append(jnp.sum(dpre, axis=0, keepdims=True))
    pad = jnp.zeros((1, LCONV - LX), F32)
    rows.append(jnp.concatenate([jnp.sum(dy * x, axis=0, keepdims=True), pad], axis=1))
    pad = jnp.zeros((1, LCONV - 128), F32)
    rows.append(jnp.concatenate([jnp.sum(ddtraw, axis=0, keepdims=True), pad], axis=1))
    rows.append(jnp.concatenate([jnp.sum(dell * p["ell"], axis=0, keepdims=True), pad], axis=1))
    misc_ref[0] = jnp.concatenate(rows, axis=0)


def scan_kernel(reverse, n, pr, st_ref, dec_ref, *refs):
    out_ref = refs[-1]
    rows = LOCAL_HEADS * pr

    def step(j, half, s):
        out_ref[j, half] = s.astype(BF16)
        d = dec_ref[j, half, rows : rows + 16].astype(F32)
        d = d[:LOCAL_HEADS] + d[8 : 8 + LOCAL_HEADS]
        d = jnp.broadcast_to(d[:, None, :], (LOCAL_HEADS, pr, 128)).reshape(rows, 128)
        return d * s + st_ref[j, half, :rows].astype(F32)

    first, second = (1, 0) if reverse else (0, 1)
    s = jnp.zeros((rows, 128), F32)
    s = lax.fori_loop(0, n, lambda j, s: step(j, first, s), s)
    lax.fori_loop(0, n, lambda j, s: step(n - 1 - j, second, s), s)


def unit_of(u, gi):
    if u < 4:
        return 1, 0, u
    is_a = u < 5 + gi
    rowset = jnp.where(is_a, 0, 1)
    half = jnp.where(is_a, 0, 1)
    return rowset, half, jnp.where(is_a, u - 4, u - 5)


def unit_mask(nctx, gs, i, rowset, half, g, st):
    shape = (2 * BLK, gs * BLK)
    row = iota(shape, 0) % BLK
    col = iota(shape, 1)
    qpos = jnp.where(rowset == 0, i, 2 * nctx - 1 - i) * BLK + row
    block = g * gs + col // BLK
    kpos = jnp.where(half == 0, block, 2 * nctx - 1 - block) * BLK + col % BLK
    return (kpos <= qpos) & (kpos >= st)


def attn_fwd_kernel(nctx, gs, idx_ref, q_ref, kv_ref, st_ref, o_ref, lse_ref, s_ref, m_ref, l_ref, acc_ref):
    i = idx_ref[0]
    gi = i // gs
    m_ref[...] = jnp.full(m_ref.shape, NEG, F32)
    l_ref[...] = jnp.zeros(l_ref.shape, F32)
    acc_ref[...] = jnp.zeros(acc_ref.shape, F32)
    for u in range(9):
        rowset, half, g = unit_of(u, gi)
        kv = kv_ref[pl.ds(g * gs, gs), 0, half].reshape(gs * BLK, 128)
        s = dotb(q_ref[0, rowset], kv[:, :HDIM], NT)
        ok = unit_mask(nctx, gs, i, rowset, half, g, st_ref[0, rowset, :, :1])
        s = jnp.where(ok, s, NEG)
        s_ref[u] = s
        m_ref[rowset] = jnp.maximum(m_ref[rowset], jnp.max(s, axis=1, keepdims=True))
    for u in range(9):
        rowset, half, g = unit_of(u, gi)
        kv = kv_ref[pl.ds(g * gs, gs), 0, half].reshape(gs * BLK, 128)
        w = jnp.exp(s_ref[u] - m_ref[rowset, :, :1])
        l_ref[rowset] = l_ref[rowset] + jnp.sum(w, axis=1, keepdims=True)
        acc_ref[rowset] = acc_ref[rowset] + dotb(w, kv[:, HDIM:], NN)
    o_ref[0] = acc_ref[...] / l_ref[:, :, :HDIM]
    lse_ref[0] = m_ref[...] + jnp.log(l_ref[...])


def attn_bwd_kernel(
    nctx, gs, idx_ref, q_ref, kv_ref, st_ref, o_ref, lse_ref, do_ref, cos_ref, sin_ref, *refs
):
    out_ref, keep_ref, give_ref, del_ref, acc_ref, dq_ref = refs[-6:]
    i = idx_ref[0]
    gi = i // gs
    acc_ref[...] = jnp.zeros(acc_ref.shape, F32)
    dq_ref[...] = jnp.zeros(dq_ref.shape, F32)
    delta = jnp.sum(do_ref[0].astype(F32) * o_ref[0], axis=2, keepdims=True)
    del_ref[...] = jnp.broadcast_to(delta, del_ref.shape)
    for u in range(9):
        rowset, half, g = unit_of(u, gi)
        kv = kv_ref[pl.ds(g * gs, gs), 0, half].reshape(gs * BLK, 128)
        q = q_ref[0, rowset]
        do = do_ref[0, rowset]
        s = dotb(q, kv[:, :HDIM], NT)
        ok = unit_mask(nctx, gs, i, rowset, half, g, st_ref[0, rowset, :, :1])
        prob = jnp.exp(jnp.where(ok, s, NEG) - lse_ref[0, rowset, :, :1])
        dp = dotb(do, kv[:, HDIM:], NT)
        ds = (prob * (dp - del_ref[rowset, :, :1])).astype(BF16)
        dkv = jnp.concatenate([dotb(ds, q, TN), dotb(prob, do, TN)], axis=1)
        acc_ref[half, g] = acc_ref[half, g] + dkv
        dq_ref[rowset] = dq_ref[rowset] + dotb(ds, kv[:, :HDIM], NN)
    for half in range(2):
        parts = []
        for e in range(2):
            part = dq_ref[half, BLK * e : BLK * e + BLK] * HDIM**-0.5
            parts.append(turned(part, cos_ref[half], -sin_ref[half]))
        out_ref[0, half] = jnp.concatenate(parts, axis=1).astype(BF16)

    def write(even_ref, odd_ref):
        for src in range(4 * gs):
            g, at = src // gs, (src % gs) * BLK
            ref = odd_ref if src % 2 else even_ref
            for half in range(2):
                ref[src // 2, 0, half] = acc_ref[half, g, at : at + BLK].astype(BF16)

    @pl.when(i % 2 == 0)
    def _():
        write(keep_ref, give_ref)

    @pl.when(i % 2 == 1)
    def _():
        write(give_ref, keep_ref)


def spec(shape, index):
    return pl.BlockSpec(shape, index)


def per_pair(shape):
    return pl.BlockSpec((1,) + shape, lambda j: (j,) + (0,) * len(shape))


def whole(shape):
    return pl.BlockSpec(shape, lambda *j: (0,) * len(shape))


def chunk_spec(nk, rows):
    return pl.BlockSpec((1, nk, 1, rows, 128), lambda j: (j // 2, 0, j % 2, 0, 0))


ANY = pl.BlockSpec(memory_space=pl.ANY)
VMEM = pl.BlockSpec(memory_space=pltpu.VMEM)
SMEM = pl.BlockSpec(memory_space=pltpu.SMEM)
PARAMS = pltpu.CompilerParams(vmem_limit_bytes=16 * 1024 * 1024)
WIDER = pltpu.CompilerParams(vmem_limit_bytes=28 * 1024 * 1024)
WIDEST = pltpu.CompilerParams(vmem_limit_bytes=48 * 1024 * 1024)


def cost(flops, moved, trans=0):
    return pl.CostEstimate(flops=flops // 1000, bytes_accessed=moved // 1000, transcendentals=0)


def sds(shape, dtype):
    return jax.ShapeDtypeStruct(shape, dtype)


def exchange(parts, axis):
    return lax.all_to_all(parts, axis, 0, 0, tiled=True)


def spread(part, axis):
    return exchange(jnp.broadcast_to(part[None], (lax.axis_size(axis),) + part.shape), axis)


def shifts():
    return [(k, [(a, (a + k) % 4) for a in range(4)]) for k in (1, 2, 3)]


def ring_exchange(parts, z):
    out = parts
    for k, perm in shifts():
        sent = lax.dynamic_index_in_dim(parts, (z + k) % 4, 0, keepdims=False)
        got = lax.ppermute(sent, "fsdp", perm)
        out = lax.dynamic_update_index_in_dim(out, got, (z - k) % 4, 0)
    return out


def ring_spread(part, z):
    out = jnp.broadcast_to(part[None], (4,) + part.shape)
    for k, perm in shifts():
        got = lax.ppermute(part, "fsdp", perm)
        out = lax.dynamic_update_index_in_dim(out, got, (z - k) % 4, 0)
    return out


def ring_sum(rows, z):
    parts = rows.astype(BF16).reshape((4, -1) + rows.shape[1:])
    total = lax.dynamic_index_in_dim(parts, z, 0, keepdims=False).astype(F32)
    for k, perm in shifts():
        sent = lax.dynamic_index_in_dim(parts, (z + k) % 4, 0, keepdims=False)
        total = total + lax.ppermute(sent, "fsdp", perm).astype(F32)
    return total


def as_rows(column):
    high = lax.reduce_precision(column, 8, 7)
    pair = jnp.stack([high, column - high], axis=-2).astype(BF16)
    pads = [(0, 0)] * (pair.ndim - 2) + [(0, 14), (0, D - 128)]
    return jnp.pad(pair, pads)


def from_rows(rows):
    pair = rows[..., :2, :128].astype(F32)
    return pair[..., 0, :] + pair[..., 1, :]


def rms_of(v):
    return lax.rsqrt(jnp.mean(v * v, axis=-1, keepdims=True) + EPS)


def rms_back(v, r, dn):
    n = v * r
    return r * (dn - n * jnp.mean(dn * n, axis=-1, keepdims=True))


def matmul(a, b, dims=NN):
    return lax.dot_general(a, b, (dims, ((), ())), preferred_element_type=F32)


def per_device(
    tokens,
    doc_start,
    cotangent,
    w_in,
    w_dt,
    conv_weight,
    conv_bias,
    dt_bias,
    a_log,
    skip_gain,
    inner_gain,
    mamba_out,
    attn_out,
    mixer_gain,
    ffn_gain,
    w_gate_up,
    w_down,
):
    nctx = lax.axis_size("ctx")
    i = lax.axis_index("ctx")
    z = lax.axis_index("fsdp")
    nk = nctx // 4
    pr = HDIM // nk
    gs = nctx // 4
    rpc = 256 // nctx
    idx = i.astype(jnp.int32).reshape(1)
    last_device = i == nctx - 1
    up = [(a, a + 1) for a in range(nctx - 1)]
    down = [(b, a) for a, b in up]

    core = i % 2
    core_idx = core.astype(jnp.int32).reshape(1)
    pair = [(a, a ^ 1) for a in range(nctx)]
    send_in = pl.pallas_call(
        split_in_kernel,
        in_specs=[SMEM, VMEM],
        out_specs=VMEM,
        out_shape=sds((4, 128, LPROJ), BF16),
        compiler_params=PARAMS,
        cost_estimate=cost(0, 5 * 10**6),
        name="split_in",
    )(core_idx, w_in)
    z_idx = z.astype(jnp.int32).reshape(1)
    gu_parts = pl.pallas_call(
        split_gate_up_kernel,
        in_specs=[SMEM, VMEM],
        out_specs=[VMEM] * 4,
        out_shape=[sds((256, 1024), BF16)] * 4,
        compiler_params=PARAMS,
        cost_estimate=cost(0, 4 * 10**6),
        name="split_gate_up",
    )(z_idx, w_gate_up)
    tok = tokens[0]
    tails = tok[:, BLK - 3 :, :]
    halo_first = lax.ppermute(tails[0], "ctx", up)
    halo_second = lax.ppermute(tails[1], "ctx", down)
    halo = jnp.stack([halo_first, jnp.where(last_device, tails[0], halo_second)])
    starts_own = doc_start[0]
    flat = jnp.concatenate(
        [
            w_dt.reshape(-1),
            conv_weight.reshape(-1),
            conv_bias,
            mixer_gain,
            ffn_gain,
            (starts_own // 64).astype(BF16).reshape(-1),
            (starts_own % 64).astype(BF16).reshape(-1),
        ]
    )
    flat = jnp.pad(flat, (0, 10 * D - flat.shape[0])).reshape(2, 5, D)
    wide = ring_spread(jnp.concatenate([flat, halo, tok], axis=1), z)
    mine_in = exchange(send_in, "fsdp")
    other_in = lax.ppermute(mine_in, "ctx", pair)
    grad_own = cotangent[0].reshape(128, D)
    own_gu, grad_all = pl.pallas_call(
        place_kernel,
        in_specs=[SMEM] + [VMEM] * 8,
        out_specs=[VMEM] * 2,
        out_shape=[sds((4, 256, 1024), BF16), sds((4, 128, D), BF16)],
        compiler_params=PARAMS,
        cost_estimate=cost(0, 6 * 10**6),
        name="place",
    )(
        z_idx,
        gu_parts[0],
        *[lax.ppermute(gu_parts[k], "fsdp", perm) for k, perm in shifts()],
        grad_own,
        *[lax.ppermute(grad_own, "fsdp", perm) for _, perm in shifts()],
    )
    own_gu = own_gu.reshape(D, 1024)
    grad_all = grad_all.reshape(512, D)
    flat = wide[:, :, :5, :].reshape(4, 10 * D)
    full_dt = flat[:, :6144].reshape(D, 24)
    own_dt = jnp.pad(lax.dynamic_slice_in_dim(full_dt, 6 * z, 6, axis=1), ((0, 0), (0, 122)))
    full_conv = flat[:, 6144:7936].reshape(4, 4, 448).transpose(1, 0, 2).reshape(4, 1792)
    full_bias = flat[:, 7936:8384].reshape(1, 1792)
    full_taps = jnp.concatenate([full_conv, full_bias], axis=0).astype(F32)
    mixer_scale = flat[:, 8384:8640].reshape(D).astype(F32)
    ffn_scale = flat[:, 8640:8896].reshape(D).astype(F32)
    starts = (
        flat[:, 8896:9024].astype(jnp.int32) * 64 + flat[:, 9024:9152].astype(jnp.int32)
    ).reshape(8, BLK)
    own_taps = jnp.concatenate(
        [lax.dynamic_slice_in_dim(full_taps, LX * z, LX, axis=1), full_taps[:, 1536:]], axis=1
    )

    def lanes(v):
        return jnp.pad(v.astype(F32), (0, LCONV - v.shape[0]))[None]

    pv = jnp.concatenate(
        [own_taps, lanes(dt_bias), lanes(a_log), lanes(jnp.repeat(skip_gain, HDIM))], axis=0
    )
    inner_scale = inner_gain.astype(F32)

    rows = 8 * EXT
    st_wide = jnp.broadcast_to(starts[:, :, None], (8, BLK, 128))
    blocks = jnp.stack([i, 2 * nctx - 1 - i])
    positions = blocks[:, None] * BLK + jnp.arange(BLK, dtype=jnp.int32)[None, :]
    freq = jnp.exp(
        jnp.arange(HDIM // 2, dtype=F32) * (-2.0 * math.log(ROPE_BASE) / HDIM)
    )
    angle = positions.astype(F32)[:, :, None] * freq
    cosine, sine = jnp.cos(angle), jnp.sin(angle)
    gate_z, conv_ext, raw_dt, query, kv_own, act_one, own_in = pl.pallas_call(
        proj_kernel,
        in_specs=[SMEM] + [VMEM] * 7 + [ANY] * 6,
        out_specs=[VMEM] * 7,
        out_shape=[
            sds((8, BLK, LX), F32),
            sds((8, EXT, LCONV), F32),
            sds((8, EXT, 128), F32),
            sds((4, 2, 2 * BLK, HDIM), BF16),
            sds((4, 2, BLK, 128), BF16),
            sds((rows, D), BF16),
            sds((D, LPROJ), BF16),
        ],
        compiler_params=WIDER,
        cost_estimate=cost(2 * 10**9, 8 * 10**6),
        name="proj",
    )(
        core_idx, wide.reshape(rows, D), mine_in, other_in, own_dt, mixer_scale[None],
        cosine, sine, pv, st_wide, *gu_parts,
    )

    srows = LOCAL_HEADS * pr
    ssd_in = (idx, conv_ext, raw_dt, st_wide, pv)
    ssd_in_specs = [
        SMEM,
        per_pair((EXT, LCONV)),
        per_pair((EXT, 128)),
        per_pair((BLK, 128)),
        whole((8, LCONV)),
    ]
    y_local, swx, c_mat, state_out = pl.pallas_call(
        functools.partial(ssd_fwd_kernel, nctx, nk, pr),
        grid=(8,),
        in_specs=ssd_in_specs,
        out_specs=[
            per_pair((BLK, LX)),
            per_pair((BLK, LX)),
            per_pair((BLK, 128)),
            chunk_spec(nk, srows + 16),
        ],
        out_shape=[
            sds((8, BLK, LX), F32),
            sds((8, BLK, LX), F32),
            sds((8, BLK, 128), BF16),
            sds((4, nk, 2, srows + 16, 128), BF16),
        ],
        compiler_params=PARAMS,
        cost_estimate=cost(2 * 10**9, 6 * 10**6),
        name="ssd_fwd",
    )(*ssd_in)
    got = exchange(state_out.reshape(nctx, 2, srows + 16, 128), "ctx")
    kv_all = lax.all_gather(kv_own, "ctx")

    st_rows = jnp.broadcast_to(
        starts.reshape(4, 2, 1, BLK, 1), (4, 2, 2, BLK, 128)
    ).reshape(4, 2, 2 * BLK, 128)
    def chain(reverse, terms, *after):
        return pl.pallas_call(
            functools.partial(scan_kernel, reverse, nctx, pr),
            in_specs=[VMEM, VMEM] + [ANY] * len(after),
            out_specs=VMEM,
            out_shape=sds((nctx, 2, srows, 128), BF16),
            compiler_params=PARAMS,
            cost_estimate=cost(10**7, 3 * 10**6),
            name="chain",
        )(terms, got, *after)

    entry = exchange(chain(False, got, st_rows), "ctx").reshape(4, nk, 2, srows, 128)

    row_spec = pl.BlockSpec((1, 2, 2 * BLK, HDIM), lambda s: (s, 0, 0, 0))
    wide_spec = pl.BlockSpec((1, 2, 2 * BLK, 128), lambda s: (s, 0, 0, 0))
    kv_spec = pl.BlockSpec((nctx, 1, 2, BLK, 128), lambda s: (0, s, 0, 0, 0))
    attn_o, lse = pl.pallas_call(
        functools.partial(attn_fwd_kernel, nctx, gs),
        grid=(4,),
        in_specs=[SMEM, row_spec, kv_spec, wide_spec],
        out_specs=[row_spec, wide_spec],
        out_shape=[sds((4, 2, 2 * BLK, HDIM), F32), sds((4, 2, 2 * BLK, 128), F32)],
        scratch_shapes=[
            pltpu.VMEM((9, 2 * BLK, gs * BLK), F32),
            pltpu.VMEM((2, 2 * BLK, 128), F32),
            pltpu.VMEM((2, 2 * BLK, 128), F32),
            pltpu.VMEM((2, 2 * BLK, HDIM), F32),
        ],
        compiler_params=PARAMS,
        cost_estimate=cost(4 * 10**9, 8 * 10**6, 2 * 10**6),
        name="attn_fwd",
    )(idx, query, kv_all, st_rows)
    act_attn = (
        attn_o.reshape(4, 2, 2, BLK, HDIM).transpose(0, 1, 3, 2, 4).reshape(512, 128).astype(BF16)
    )

    mamba_y, scaled_u, squares = pl.pallas_call(
        functools.partial(ssd_out_kernel, nk, pr),
        grid=(8,),
        in_specs=[
            per_pair((BLK, LX)),
            per_pair((BLK, LX)),
            per_pair((BLK, 128)),
            chunk_spec(nk, srows),
            per_pair((BLK, LX)),
            whole((1, LX)),
        ]
        + [ANY] * 3,
        out_specs=[per_pair((BLK, LX)), per_pair((BLK, LX)), per_pair((BLK, 128))],
        out_shape=[
            sds((8, BLK, LX), F32),
            sds((8, BLK, LX), BF16),
            sds((8, BLK, 128), F32),
        ],
        compiler_params=PARAMS,
        cost_estimate=cost(10**9, 6 * 10**6),
        name="ssd_out",
    )(y_local, swx, c_mat, entry, gate_z, inner_scale[None], attn_o, own_gu, grad_all)

    def gather_sum(part_rows):
        got_rows = exchange(part_rows.astype(BF16).reshape((4, -1) + part_rows.shape[1:]), "fsdp")
        return jnp.sum(got_rows.astype(F32), axis=0)

    attn_mid = ring_sum(matmul(act_attn, attn_out), z)
    part_rows = pl.pallas_call(
        mid_kernel,
        in_specs=[VMEM] * 3 + [ANY],
        out_specs=VMEM,
        out_shape=sds((4, 144, D), BF16),
        compiler_params=PARAMS,
        cost_estimate=cost(4 * 10**8, 3 * 10**6),
        name="mid_part",
    )(scaled_u.reshape(512, LX), mamba_out, squares.reshape(512, 128), attn_mid)
    got_part = exchange(part_rows, "fsdp")
    scaled_mid = jnp.sum(got_part[:, :128].astype(F32), axis=0)
    square_sum = jnp.sum(from_rows(got_part[:, 128:]), axis=0)
    own_r = lax.rsqrt(square_sum.reshape(128, 1) * (1.0 / 1536) + EPS)
    mamba_mid = scaled_mid * own_r
    middle = tok.reshape(128, D).astype(F32) + mamba_mid + attn_mid
    mid_r = rms_of(middle)
    norm_two = middle * mid_r
    def spread_rows(values, column):
        sent = jnp.concatenate([values.astype(BF16), as_rows(column.reshape(128))], axis=0)
        return spread(sent, "fsdp").reshape(4, 144, D)

    act_two = spread_rows(norm_two * ffn_scale, own_r)
    r_tail = act_two[:, 128:, :128]
    act_two = act_two[:, :128].reshape(512, D)

    gate_up = matmul(act_two, own_gu)
    gate_val, up_val = gate_up[:, :512], gate_up[:, 512:]
    gate_sig = sigmoid(gate_val)
    gate_silu = gate_val * gate_sig
    inner = (gate_silu * up_val).astype(BF16)
    grad_inner = matmul(grad_all, w_down, NT)
    grad_gate = grad_inner * up_val * (gate_sig * (1.0 + gate_val * (1.0 - gate_sig)))
    grad_gu = jnp.concatenate([grad_gate, grad_inner * gate_silu], axis=1).astype(BF16)
    grad_act_two = gather_sum(matmul(grad_gu, own_gu, NT))
    grad_down = matmul(inner, grad_all, TN).astype(BF16)
    grad_gate_up = matmul(act_two, grad_gu, TN).astype(BF16)
    grad_ffn_gain = jnp.sum(grad_act_two * norm_two, axis=0)
    grad_middle = grad_own.astype(F32) + rms_back(middle, mid_r, grad_act_two * ffn_scale)
    own_mix = grad_middle.astype(BF16)
    own_dots = jnp.sum(own_mix.astype(F32) * mamba_mid, axis=1) * (1.0 / 1536)
    grad_rows = spread_rows(own_mix, own_dots)
    grad_mix, grad_attn, act_mamba, grad_y, grad_z, grad_inner_gain, leak = pl.pallas_call(
        functools.partial(post_mix_kernel, nk, pr),
        in_specs=[VMEM] * 9,
        out_specs=[VMEM] * 7,
        out_shape=[
            sds((512, D), BF16),
            sds((4, 2, 2 * BLK, HDIM), BF16),
            sds((512, LX), BF16),
            sds((8, BLK, LX), F32),
            sds((8, BLK, LX), BF16),
            sds((1, LX), F32),
            sds((4, nk, 2, srows, 128), BF16),
        ],
        compiler_params=WIDER,
        cost_estimate=cost(10**9, 8 * 10**6),
        name="post_mix",
    )(
        grad_rows, r_tail, mamba_out, attn_out, mamba_y, gate_z, inner_scale[None], swx, c_mat
    )

    down_part = pl.pallas_call(
        down_kernel,
        in_specs=[VMEM, VMEM, ANY],
        out_specs=VMEM,
        out_shape=sds((512, D), BF16),
        compiler_params=PARAMS,
        cost_estimate=cost(5 * 10**8, 3 * 10**6),
        name="down",
    )(inner, w_down, grad_mix)
    mixed = (middle + ring_sum(down_part, z)).astype(BF16).reshape(1, 2, BLK, D)

    grad_mamba_out = matmul(act_mamba, grad_mix, TN).astype(BF16)
    grad_attn_out = matmul(act_attn, grad_mix, TN).astype(BF16)
    def halves(v):
        v = v.reshape(4, 2, 128, v.shape[-1])
        keep = lax.dynamic_index_in_dim(v, core, 1, keepdims=False)
        give = lax.dynamic_index_in_dim(v, 1 - core, 1, keepdims=False)
        return keep, lax.ppermute(give, "ctx", pair)

    kept, taken = halves(grad_gate_up)
    pair_gu = (kept.astype(F32) + taken.astype(F32)).astype(BF16)
    out_grads = jnp.concatenate([grad_mamba_out, grad_attn_out], axis=0)
    kept = jnp.where(core == 0, grad_down, out_grads)
    taken = lax.ppermute(jnp.where(core == 0, out_grads, grad_down), "ctx", pair)
    pair_o = (kept.astype(F32) + taken.astype(F32)).astype(BF16)
    got_leak = exchange(leak.reshape(nctx, 2, srows, 128), "ctx")
    half_kv_spec = pl.BlockSpec((nctx // 2, 1, 2, BLK, 128), lambda s: (0, s, 0, 0, 0))
    grad_query, keep_kv, give_kv = pl.pallas_call(
        functools.partial(attn_bwd_kernel, nctx, gs),
        grid=(4,),
        in_specs=[SMEM, row_spec, kv_spec, wide_spec, row_spec, wide_spec, row_spec]
        + [whole((2, BLK, HDIM // 2))] * 2
        + [ANY] * 5,
        out_specs=[
            pl.BlockSpec((1, 2, BLK, 128), lambda s: (s, 0, 0, 0)),
            half_kv_spec,
            half_kv_spec,
        ],
        out_shape=[
            sds((4, 2, BLK, 128), BF16),
            sds((nctx // 2, 4, 2, BLK, 128), BF16),
            sds((nctx // 2, 4, 2, BLK, 128), BF16),
        ],
        scratch_shapes=[
            pltpu.VMEM((2, 2 * BLK, 128), F32),
            pltpu.VMEM((2, 4, gs * BLK, 128), F32),
            pltpu.VMEM((2, 2 * BLK, HDIM), F32),
        ],
        compiler_params=PARAMS,
        cost_estimate=cost(8 * 10**9, 16 * 10**6, 2 * 10**6),
        name="attn_bwd",
    )(
        idx, query, kv_all, st_rows, attn_o, lse, grad_attn, cosine, sine,
        leak, grad_gate_up, grad_down, grad_mamba_out, grad_attn_out,
    )
    chained = chain(True, got_leak, give_kv)
    grad_exit = exchange(chained, "ctx").reshape(4, nk, 2, srows, 128)
    give_kv = pl.pallas_call(
        hold_kernel,
        in_specs=[VMEM, ANY],
        out_specs=VMEM,
        out_shape=sds(give_kv.shape, BF16),
        compiler_params=PARAMS,
        cost_estimate=cost(0, 4 * 10**6),
        name="hold",
    )(give_kv, chained)
    taken_kv = lax.ppermute(give_kv, "ctx", pair)
    pair_kv = (keep_kv.astype(F32) + taken_kv.astype(F32)).astype(BF16)
    nj = nctx // 2
    rj = 128 // nj
    groups = [[2 * j + c for j in range(nj)] for c in range(2)]
    grad_ext, grad_dt, misc = pl.pallas_call(
        functools.partial(ssd_bwd_kernel, nctx, nk, pr),
        grid=(8,),
        in_specs=ssd_in_specs
        + [per_pair((BLK, LX)), chunk_spec(nk, srows), chunk_spec(nk, srows)],
        out_specs=[per_pair((EXT, LCONV)), per_pair((EXT, 128)), per_pair((8, LCONV))],
        out_shape=[
            sds((8, EXT, LCONV), BF16),
            sds((8, EXT, 128), BF16),
            sds((8, 8, LCONV), F32),
        ],
        compiler_params=PARAMS,
        cost_estimate=cost(4 * 10**9, 8 * 10**6),
        name="ssd_bwd",
    )(*ssd_in, grad_y, entry, grad_exit)

    grad_dt = grad_dt.reshape(rows, 128)
    grad_dtw = matmul(act_one, grad_dt, TN)
    misc = jnp.sum(misc, axis=0)
    grad_skip = jnp.sum(misc[5, :LX].reshape(LOCAL_HEADS, HDIM), axis=1)
    small = jnp.concatenate(
        [misc[:5].reshape(-1), misc[6, :6], misc[7, :6], grad_skip, grad_inner_gain[0]]
    )
    small = jnp.pad(small, (0, 3840 - small.shape[0])).reshape(1, 256, 15)
    small = jnp.broadcast_to(small, (4, 256, 15)).reshape(D, 15)
    extras = jnp.concatenate(
        [
            grad_dtw[:, :6],
            grad_ffn_gain[:, None],
            small,
            jnp.zeros((D, 106), F32),
        ],
        axis=1,
    ).astype(BF16)
    early = pl.pallas_call(
        functools.partial(pack_early_kernel, nj, rj),
        in_specs=[VMEM] * 2,
        out_specs=VMEM,
        out_shape=sds((nj, 4, rj, 2048), BF16),
        compiler_params=PARAMS,
        cost_estimate=cost(0, 4 * 10**6),
        name="pack_early",
    )(pair_gu, pair_o)

    def core_exchange(parts):
        return lax.all_to_all(parts, "ctx", 0, 0, axis_index_groups=groups, tiled=True)

    grad_proj = pl.pallas_call(
        functools.partial(dproj_kernel, nj),
        in_specs=[VMEM] * 6 + [ANY] * 2,
        out_specs=VMEM,
        out_shape=sds((8, EXT, LPROJ), BF16),
        compiler_params=PARAMS,
        cost_estimate=cost(2 * 10**6, 4 * 10**6),
        name="dproj",
    )(
        core_exchange(pair_kv), grad_z, grad_ext, grad_query, cosine, sine,
        early, extras,
    ).reshape(rows, LPROJ)
    got_early = core_exchange(early)

    grad_in = matmul(act_one, grad_proj, TN).astype(BF16)
    kept_in, taken_in = halves(grad_in)
    kept_ex, taken_ex = halves(extras)
    sent = pl.pallas_call(
        functools.partial(pack_kernel, nj, rj),
        in_specs=[VMEM] * 4 + [ANY],
        out_specs=VMEM,
        out_shape=sds((nj, 4, rj, 1408), BF16),
        compiler_params=PARAMS,
        cost_estimate=cost(0, 7 * 10**6),
        name="pack",
    )(kept_in, taken_in, kept_ex, taken_ex, got_early)
    got_late = core_exchange(sent)
    grad_act = pl.pallas_call(
        grad_act_kernel,
        in_specs=[VMEM] * 4 + [ANY],
        out_specs=VMEM,
        out_shape=sds((rows, D), BF16),
        compiler_params=PARAMS,
        cost_estimate=cost(2 * 10**9, 6 * 10**6),
        name="grad_act",
    )(grad_proj, own_in, grad_dt, own_dt, got_late)
    got_act = ring_sum(grad_act, z).reshape(2, EXT, D)
    halo_back = got_act[:, 5:8].astype(BF16)
    to_first = lax.ppermute(halo_back[0], "ctx", down).astype(F32)
    to_second = lax.ppermute(jnp.where(last_device, 0.0, halo_back[1]), "ctx", up).astype(F32)
    to_first = to_first + jnp.where(last_device, got_act[1, 5:8], 0.0)
    tail_add = jnp.pad(jnp.stack([to_first, to_second]), ((0, 0), (BLK - 3, 0), (0, 0)))
    own_act = (got_act[:, 8:] + tail_add).reshape(128, D)
    hidden = tok.reshape(128, D).astype(F32)
    grad_tokens = grad_middle + rms_back(hidden, rms_of(hidden), own_act * mixer_scale)
    grad_tokens = grad_tokens.reshape(1, 2, BLK, D)

    def total(got_parts, *after):
        return pl.pallas_call(
            functools.partial(total_kernel, nj),
            in_specs=[VMEM] + [ANY] * len(after),
            out_specs=VMEM,
            out_shape=sds(got_parts.shape[1:], F32),
            compiler_params=PARAMS,
            cost_estimate=cost(2 * 10**6, 4 * 10**6),
            name="total",
        )(got_parts, *after)

    summed = total(got_early, sent)
    owned_gu = ring_exchange(summed[:, :, :1024].astype(BF16), z)
    final_early = pl.pallas_call(
        assemble_early_kernel,
        in_specs=[VMEM] * 2 + [ANY],
        out_specs=VMEM,
        out_shape=sds((rj, 8192), BF16),
        compiler_params=PARAMS,
        cost_estimate=cost(0, 10**6),
        name="assemble_early",
    )(owned_gu, summed[:, :, 1024:], got_late)
    mine_early = core_exchange(jnp.broadcast_to(final_early[None], (nj, rj, 8192)))
    other_early = lax.ppermute(mine_early, "ctx", pair)
    owned = ring_exchange(total(got_late), z)
    final = pl.pallas_call(
        assemble_kernel,
        in_specs=[VMEM] + [ANY] * 3,
        out_specs=VMEM,
        out_shape=sds((rj, 4224), BF16),
        compiler_params=PARAMS,
        cost_estimate=cost(0, 10**6),
        name="assemble",
    )(owned, mine_early, grad_tokens, mixed)
    mine_all = core_exchange(jnp.broadcast_to(final[None], (nj, rj, 4224)))
    other_all = lax.ppermute(mine_all, "ctx", pair)
    half_spec = pl.BlockSpec((128, 4096), lambda h: (h, 0))
    total_gate_up, total_down, total_mamba_out, total_attn_out = pl.pallas_call(
        functools.partial(unpack_early_kernel, nj, rj),
        grid=(2,),
        in_specs=[SMEM, whole((nj, rj, 8192)), whole((nj, rj, 8192))],
        out_specs=[half_spec, whole((512, 1024)), whole((384, 1024)), whole((128, 1024))],
        out_shape=[
            sds((256, 4096), F32),
            sds((512, 1024), F32),
            sds((384, 1024), F32),
            sds((128, 1024), F32),
        ],
        compiler_params=WIDER,
        cost_estimate=cost(0, 10**7),
        name="unpack_early",
    )(core_idx, mine_early, other_early)
    total_in, mixer_dot, extra = pl.pallas_call(
        unpack_kernel,
        grid=(2,),
        in_specs=[SMEM, whole((nj, rj, 4224)), whole((nj, rj, 4224)), half_spec, ANY],
        out_specs=[
            half_spec,
            pl.BlockSpec((128, 128), lambda h: (h, 0)),
            pl.BlockSpec((128, 128), lambda h: (h, 0)),
        ],
        out_shape=[sds((256, 4096), F32), sds((256, 128), F32), sds((256, 128), F32)],
        compiler_params=WIDER,
        cost_estimate=cost(0, 10**7),
        name="unpack",
    )(core_idx, mine_all, other_all, w_in, total_attn_out)
    extra = extra[:, :88].reshape(256, 4, 22)
    total_dt = extra[:, :, :6].reshape(256, 24)
    mixer_dot = mixer_dot[:, 0] + jnp.sum(total_dt * w_dt.astype(F32), axis=1)
    total_mixer = mixer_dot / mixer_gain.astype(F32)
    total_ffn = jnp.sum(extra[:, :, 6], axis=1)
    small = extra[:, :, 7:22].transpose(1, 0, 2).reshape(4, 3840)
    taps = small[:, :3200].reshape(4, 5, LCONV)
    taps = jnp.concatenate(
        [
            taps[:, :, :LX].transpose(1, 0, 2).reshape(5, 1536),
            jnp.sum(taps[:, :, LX:], axis=0),
        ],
        axis=1,
    )
    taps = lax.dynamic_slice_in_dim(taps, 448 * z, 448, axis=1)
    mine = lax.dynamic_slice_in_dim(small, z, 1, axis=0)[0]
    return (
        mixed,
        grad_tokens,
        total_in,
        total_dt,
        taps[:4],
        taps[4],
        mine[3200:3206],
        mine[3206:3212],
        mine[3212:3218],
        mine[3218:3602],
        total_mamba_out,
        total_attn_out,
        total_mixer,
        total_ffn,
        total_gate_up,
        total_down,
    )


def solution(mesh):
    row = P("fsdp", None)
    vec = P("fsdp")
    act = P("fsdp", None, "ctx", None)
    return jax.shard_map(
        per_device,
        mesh=mesh,
        in_specs=(
            act, P("fsdp", None, "ctx"), act, row, row, P(None, "fsdp"), vec, vec, vec, vec, vec,
            row, row, vec, vec, row, row,
        ),
        out_specs=(
            act, act, row, row, P(None, "fsdp"), vec, vec, vec, vec, vec, row, row, vec, vec, row, row,
        ),
        check_vma=False,
    )
```

```python
import functools
import math

import jax
import jax.numpy as jnp
from jax import lax
from jax.experimental import pallas as pl
from jax.experimental.pallas import tpu as pltpu
from jax.sharding import PartitionSpec as P

D = 1024
FF = 2048
BLK = 64
HDIM = 64
NSTATE = 128
LOCAL_HEADS = 6
LX = 384
LBC = 256
LCONV = LX + LBC
LPROJ = 1280
EXT = 72
EPS = 1e-05
ROPE_BASE = 100000000000.0
NEG = -1e30
F32 = jnp.float32
BF16 = jnp.bfloat16
NN = ((1,), (0,))
NT = ((1,), (1,))
TN = ((0,), (0,))


def dotf(a, b, dims):
    return lax.dot_general(
        a, b, (dims, ((), ())), precision=lax.Precision.HIGHEST, preferred_element_type=F32
    )


def dotb(a, b, dims):
    return lax.dot_general(
        a.astype(BF16), b.astype(BF16), (dims, ((), ())), preferred_element_type=F32
    )


def iota(shape, dim):
    return lax.broadcasted_iota(jnp.int32, shape, dim)


def sigmoid(v):
    return 1.0 / (1.0 + jnp.exp(-v))


def ssd_prep(ext, dtr, st, base, pv):
    tpos = base + iota((BLK, LCONV), 0)
    stc = jnp.broadcast_to(st[:, :1], (BLK, LCONV))
    pre = jnp.broadcast_to(pv[4:5], (BLK, LCONV))
    for tap in range(4):
        use = (tpos - (3 - tap)) >= stc
        pre = pre + jnp.where(use, pv[tap : tap + 1] * ext[5 + tap : 5 + tap + BLK], 0.0)
    sg = sigmoid(pre)
    xc = pre * sg
    lin = dtr + pv[5:6, :128]
    dt = jnp.maximum(lin, 0.0) + jnp.log1p(jnp.exp(-jnp.abs(lin)))
    ea = jnp.exp(pv[6:7, :128])
    ell = -dt * ea
    tri = (iota((BLK, BLK), 1) <= iota((BLK, BLK), 0)).astype(F32)
    eye = (iota((BLK, BLK), 1) == iota((BLK, BLK), 0)).astype(F32)
    run = dotf(tri, ell, NN)
    run_t = dotf(ell, tri, ((0,), (1,)))
    dt_t = dotf(dt, eye, TN)
    allowed = (iota((BLK, BLK), 1) <= iota((BLK, BLK), 0)) & (
        (base + iota((BLK, BLK), 1)) >= st[:, :BLK]
    )
    sw = jnp.where(st < base, jnp.exp(run), 0.0)
    last_ok = (base + iota((BLK, 128), 0)) >= st[BLK - 1 : BLK]
    fwd_decay = jnp.where(
        last_ok, jnp.exp(jnp.where(last_ok, run[BLK - 1 : BLK] - run, 0.0)), 0.0
    )
    sel = (iota((128, LX), 1) // HDIM == iota((128, LX), 0)).astype(F32)
    return dict(
        pre=pre, sg=sg, xc=xc, lin=lin, dt=dt, ea=ea, ell=ell, run=run, run_t=run_t, dt_t=dt_t,
        allowed=allowed, sw=sw, fd=fwd_decay, fw=fwd_decay * dt, sel=sel, tri=tri, tpos=tpos, stc=stc,
    )


def decay_of(p, h):
    spread = p["run"][:, h : h + 1] - p["run_t"][h : h + 1, :]
    return jnp.where(p["allowed"], jnp.exp(jnp.where(p["allowed"], spread, 0.0)), 0.0)


def to_chunks(state, out_ref, nk, pr, extra):
    for k in range(nk):
        rows = [state[h * HDIM + k * pr : h * HDIM + (k + 1) * pr] for h in range(LOCAL_HEADS)]
        out_ref[0, k, 0] = jnp.concatenate(rows + extra, axis=0).astype(BF16)


def from_chunks(ref, nk, pr):
    parts = [ref[0, k, 0].astype(F32) for k in range(nk)]
    rows = []
    for h in range(LOCAL_HEADS):
        for k in range(nk):
            rows.append(parts[k][h * pr : (h + 1) * pr])
    return jnp.concatenate(rows, axis=0)


def block_base(idx_ref, nctx):
    half = pl.program_id(0) % 2
    i = idx_ref[0]
    return jnp.where(half == 0, i, 2 * nctx - 1 - i) * BLK


def turned(v, cosine, sine):
    a, b = v[:, : HDIM // 2], v[:, HDIM // 2 :]
    return jnp.concatenate([a * cosine - b * sine, b * cosine + a * sine], axis=1)


def proj_kernel(core_ref, x_ref, mine_ref, other_ref, wdt_ref, gain_ref, cos_ref, sin_ref, *refs):
    z_ref, ext_ref, dtr_ref, q_ref, kv_ref, act_ref, w_ref = refs[-7:]
    x = x_ref[...].astype(F32)
    r = lax.rsqrt(jnp.mean(x * x, axis=1, keepdims=True) + EPS)
    act_ref[...] = (x * r * gain_ref[...]).astype(BF16)

    def place(even_ref, odd_ref):
        for src in range(4):
            w_ref[256 * src : 256 * src + 128] = even_ref[src]
            w_ref[256 * src + 128 : 256 * src + 256] = odd_ref[src]

    @pl.when(core_ref[0] == 0)
    def _():
        place(mine_ref, other_ref)

    @pl.when(core_ref[0] == 1)
    def _():
        place(other_ref, mine_ref)

    a = act_ref[...]

    def columns(lo, width):
        p = lax.dot_general(a, w_ref[:, lo : lo + width], (NN, ((), ())), preferred_element_type=F32)
        return p.reshape(8, EXT, width)

    p = columns(1024, 256)
    for j in range(8):
        seq, half = j // 2, j % 2
        own = p[j, 8:]
        cosine, sine = cos_ref[half], sin_ref[half]
        for e in range(2):
            q = turned(own[:, HDIM * e : HDIM * e + HDIM], cosine, sine).astype(BF16)
            q = (q.astype(F32) * HDIM**-0.5).astype(BF16)
            q_ref[seq, half, BLK * e : BLK * e + BLK] = q
        k = turned(own[:, 128:192], cosine, sine)
        kv_ref[seq, half] = jnp.concatenate([k, own[:, 192:]], axis=1).astype(BF16)
    z_ref[:, :, :256] = columns(0, 256)[:, 8:].astype(BF16)
    both = columns(256, 256)
    z_ref[:, :, 256:] = both[:, 8:, :128].astype(BF16)
    ext_ref[:, :, :128] = both[:, :, 128:]
    ext_ref[:, :, 128:384] = columns(512, 256)
    ext_ref[:, :, 384:] = columns(768, 256)
    p = lax.dot_general(a, wdt_ref[...], (NN, ((), ())), preferred_element_type=F32)
    dtr_ref[...] = p.reshape(8, EXT, 128)


def dproj_kernel(n, got_ref, z_ref, ext_ref, q_ref, cos_ref, sin_ref, *refs):
    out_ref = refs[-1]

    def step(j, acc):
        return acc + got_ref[j].astype(F32)

    kv = lax.fori_loop(1, n, step, got_ref[0].astype(F32))
    out_ref[:, :8] = jnp.zeros((8, 8, LPROJ), BF16)
    out_ref[:, :, LX : LX + LCONV] = ext_ref[...]
    for j in range(8):
        own = kv[j // 2, j % 2]
        k = turned(own[:, :HDIM], cos_ref[j % 2], -sin_ref[j % 2])
        out_ref[j, 8:, :LX] = z_ref[j]
        out_ref[j, 8:, 1024:1152] = q_ref[j // 2, j % 2]
        out_ref[j, 8:, 1152:] = jnp.concatenate([k, own[:, HDIM:]], axis=1).astype(BF16)


def mid_kernel(u_ref, w_ref, ss_ref, dep_ref, out_ref):
    eye = iota((128, 128), 0) == iota((128, 128), 1)
    for a in range(4):
        part = lax.dot_general(
            u_ref[128 * a : 128 * a + 128], w_ref[...], (NN, ((), ())), preferred_element_type=F32
        )
        out_ref[a, :128] = part.astype(BF16)
        row = jnp.sum(jnp.where(eye, ss_ref[128 * a : 128 * a + 128], 0.0), axis=0, keepdims=True)
        high = row.astype(BF16).astype(F32)
        pair = jnp.concatenate([high, row - high, jnp.zeros((14, 128), F32)], axis=0)
        pair = jnp.concatenate([pair, jnp.zeros((16, D - 128), F32)], axis=1)
        out_ref[a, 128:] = pair.astype(BF16)


def hold_kernel(value_ref, dep_ref, out_ref):
    out_ref[...] = value_ref[...]


def down_kernel(inner_ref, w_ref, dep_ref, out_ref):
    out_ref[...] = lax.dot_general(
        inner_ref[...], w_ref[...], (NN, ((), ())), preferred_element_type=F32
    ).astype(BF16)


def ssd_fwd_kernel(nctx, nk, pr, idx_ref, ext_ref, dtr_ref, st_ref, pv_ref, y_ref, swx_ref, c_ref, s_ref):
    base = block_base(idx_ref, nctx)
    st = st_ref[0]
    p = ssd_prep(ext_ref[0], dtr_ref[0, 8:], st, base, pv_ref[...])
    x = p["xc"][:, :LX]
    bm = p["xc"][:, LX : LX + NSTATE].astype(BF16)
    cm = p["xc"][:, LX + NSTATE :].astype(BF16)
    inter = dotb(cm, bm, NT)
    xb = x.astype(BF16)
    outs = []
    for h in range(LOCAL_HEADS):
        mix = decay_of(p, h) * inter * p["dt_t"][h : h + 1]
        outs.append(dotb(mix, xb[:, h * HDIM : (h + 1) * HDIM], NN))
    y_ref[0] = (jnp.concatenate(outs, axis=1) + pv_ref[7:8, :LX] * x).astype(BF16)
    swx_ref[0] = dotf(p["sw"], p["sel"], NN).astype(BF16)
    c_ref[0] = cm
    fwx = dotf(p["fw"], p["sel"], NN)
    state = dotb(fwx * x, bm, TN)
    dec = jnp.where(
        st[BLK - 1 : BLK] < base,
        jnp.broadcast_to(jnp.exp(p["run_t"][:8, BLK - 1 : BLK]), (8, 128)),
        0.0,
    )
    high = dec.astype(BF16).astype(F32)
    to_chunks(state, s_ref, nk, pr, [high, dec - high])


def ssd_out_kernel(nk, pr, y_ref, swx_ref, c_ref, s_ref, z_ref, gain_ref, *refs):
    out_ref, u_ref, ss_ref = refs[-3:]
    s_in = from_chunks(s_ref, nk, pr)
    y = y_ref[0].astype(F32) + swx_ref[0].astype(F32) * dotb(c_ref[0], s_in, NT)
    z = z_ref[0].astype(F32)
    u = y * (z * sigmoid(z))
    out_ref[0] = y.astype(BF16)
    u_ref[0] = (u * gain_ref[...]).astype(BF16)
    ss_ref[0] = jnp.broadcast_to(jnp.sum(u * u, axis=1, keepdims=True), (BLK, 128))


def split_in_kernel(core_ref, full_ref, out_ref):
    w_ref = full_ref.at[pl.ds(pl.multiple_of(core_ref[0] * 128, 128), 128)]
    for zz in range(4):
        kv = HDIM * (zz // 2)
        out_ref[zz, :, :LX] = w_ref[:, LX * zz : LX * zz + LX]
        out_ref[zz, :, LX : 2 * LX] = w_ref[:, 1536 + LX * zz : 1536 + LX * zz + LX]
        out_ref[zz, :, 2 * LX : 1024] = w_ref[:, 3072:3328]
        out_ref[zz, :, 1024:1152] = w_ref[:, 3328 + 128 * zz : 3456 + 128 * zz]
        out_ref[zz, :, 1152:1280] = jnp.concatenate(
            [w_ref[:, 3840 + kv : 3904 + kv], w_ref[:, 3968 + kv : 4032 + kv]], axis=1
        )


def split_gate_up_kernel(z_ref, w_ref, g_ref, *outs):
    for k in range(4):
        outs[k][256:] = g_ref[...]
        lo = pl.multiple_of(lax.rem(z_ref[0] + k, 4) * 512, 512)
        outs[k][:256, :512] = w_ref[:, pl.ds(lo, 512)]
        outs[k][:256, 512:] = w_ref[:, pl.ds(FF + lo, 512)]


def place_kernel(z_ref, *refs):
    for k in range(4):
        at = lax.rem(z_ref[0] + 4 - k, 4)
        refs[4][at] = refs[k][:256]
        refs[5][at] = refs[k][256:]


def total_kernel(n, got_ref, *refs):
    def step(j, acc):
        return acc + got_ref[j].astype(F32)

    refs[-1][...] = lax.fori_loop(1, n, step, got_ref[0].astype(F32))


def pack_kernel(nj, rj, kin_ref, gin_ref, kex_ref, gex_ref, dep_ref, out_ref):
    for a in range(4):
        part = (kin_ref[a].astype(F32) + gin_ref[a].astype(F32)).astype(BF16)
        out_ref[:, a, :, :LPROJ] = part.reshape(nj, rj, LPROJ)
        part = (kex_ref[a].astype(F32) + gex_ref[a].astype(F32)).astype(BF16)
        out_ref[:, a, :, LPROJ:] = part.reshape(nj, rj, 128)


def pack_early_kernel(nj, rj, gu_ref, o_ref, out_ref):
    for a in range(4):
        out_ref[:, a, :, :1024] = gu_ref[a].reshape(nj, rj, 1024)
    out_ref[:, :, :, 1024:] = o_ref[...].reshape(nj, 4, rj, 1024)


def assemble_kernel(owned_ref, *refs):
    out_ref = refs[-1]

    def put(lo, value):
        out_ref[:, lo : lo + value.shape[1]] = value.astype(BF16)

    shared = owned_ref[0, :, 768:1024]
    for zz in range(4):
        put(LX * zz, owned_ref[zz, :, :LX])
        put(1536 + LX * zz, owned_ref[zz, :, LX : 2 * LX])
        put(3328 + 128 * zz, owned_ref[zz, :, 1024:1152])
        if zz > 0:
            shared = shared + owned_ref[zz, :, 768:1024]
    put(3072, shared)
    first = owned_ref[0, :, 1152:1280] + owned_ref[1, :, 1152:1280]
    second = owned_ref[2, :, 1152:1280] + owned_ref[3, :, 1152:1280]
    put(3840, jnp.concatenate([first[:, :HDIM], second[:, :HDIM]], axis=1))
    put(3968, jnp.concatenate([first[:, HDIM:], second[:, HDIM:]], axis=1))
    extras = [owned_ref[zz, :, 1280:1302] for zz in range(4)]
    extras.append(jnp.zeros((extras[0].shape[0], 40), F32))
    put(4096, jnp.concatenate(extras, axis=1))


def assemble_early_kernel(gu_ref, o_ref, dep_ref, out_ref):
    for zz in range(4):
        out_ref[:, 512 * zz : 512 * zz + 512] = gu_ref[zz, :, :512]
        out_ref[:, 2048 + 512 * zz : 2560 + 512 * zz] = gu_ref[zz, :, 512:]
        out_ref[:, 4096 + 1024 * zz : 5120 + 1024 * zz] = o_ref[zz].astype(BF16)


def by_half(core_ref, mine_ref, other_ref, write):
    half = pl.program_id(0)

    @pl.when(half == core_ref[0])
    def _():
        write(mine_ref, half)

    @pl.when(half != core_ref[0])
    def _():
        write(other_ref, half)


def unpack_early_kernel(nj, rj, core_ref, mine_ref, other_ref, gu_ref, down_ref, mo_ref, ao_ref):
    def write(src, half):
        gu_ref[...] = src[:, :, :4096].reshape(128, 4096).astype(F32)
        for j in range(nj):
            for a in range(4):
                row = j * 4 * rj + a * rj
                part = src[j, :, 4096 + 1024 * a : 5120 + 1024 * a].astype(F32)

                @pl.when(half == 0)
                def _():
                    down_ref[row : row + rj] = part

                @pl.when(half == 1)
                def _():
                    if row < 384:
                        mo_ref[row : row + rj] = part
                    else:
                        ao_ref[row - 384 : row - 384 + rj] = part

    by_half(core_ref, mine_ref, other_ref, write)


def unpack_kernel(core_ref, mine_ref, other_ref, w_ref, dep_ref, in_ref, mix_ref, ex_ref):
    def write(src, half):
        total = src[:, :, :4096].reshape(128, 4096).astype(F32)
        in_ref[...] = total
        mix = jnp.sum(total * w_ref[...].astype(F32), axis=1, keepdims=True)
        mix_ref[...] = jnp.broadcast_to(mix, (128, 128))
        ex_ref[...] = src[:, :, 4096:].reshape(128, 128).astype(F32)

    by_half(core_ref, mine_ref, other_ref, write)


def post_mix_kernel(
    nk, pr, rows_ref, rtail_ref, mo_ref, ao_ref, y_ref, z_ref, gain_ref, swx_ref, c_ref,
    mix_ref, do_ref, act_ref, dy_ref, dz_ref, gg_ref, leak_ref
):
    eye = iota((128, 128), 0) == iota((128, 128), 1)

    def column(pair):
        pair = pair.astype(F32)
        return jnp.sum(jnp.where(eye, pair[:1] + pair[1:2], 0.0), axis=1, keepdims=True)

    mix = rows_ref[:, :128].reshape(512, D)
    mix_ref[...] = mix
    d_act = lax.dot_general(mix, mo_ref[...], (NT, ((), ())), preferred_element_type=F32)
    d_attn = lax.dot_general(mix, ao_ref[...], (NT, ((), ())), preferred_element_type=F32)
    gain = gain_ref[...]
    gg = jnp.zeros((1, LX), F32)
    for s in range(4):
        own = slice(128 * s, 128 * s + 128)
        dots = column(rows_ref[s, 128:144, :128])
        r = column(rtail_ref[s])
        y = y_ref[2 * s : 2 * s + 2].astype(F32).reshape(128, LX)
        z = z_ref[2 * s : 2 * s + 2].astype(F32).reshape(128, LX)
        sig = sigmoid(z)
        silu = z * sig
        n = y * silu * r
        act_ref[own] = (n * gain).astype(BF16)
        gg = gg + jnp.sum(d_act[own] * n, axis=0, keepdims=True)
        du = r * (d_act[own] * gain - n * dots)
        dy = du * silu
        dy_ref[2 * s : 2 * s + 2] = dy.astype(BF16).reshape(2, BLK, LX)
        dz = du * y * (sig * (1.0 + z * (1.0 - sig)))
        dz_ref[2 * s : 2 * s + 2] = dz.astype(BF16).reshape(2, BLK, LX)
        for half in range(2):
            mine = slice(BLK * half, BLK * half + BLK)
            for e in range(2):
                part = d_attn[128 * s + BLK * half : 128 * s + BLK * half + BLK]
                do_ref[s, half, BLK * e : BLK * e + BLK] = part[
                    :, HDIM * e : HDIM * e + HDIM
                ].astype(BF16)
            state = dotb(swx_ref[2 * s + half].astype(F32) * dy[mine], c_ref[2 * s + half], TN)
            for k in range(nk):
                piece = [
                    state[h * HDIM + k * pr : h * HDIM + (k + 1) * pr] for h in range(LOCAL_HEADS)
                ]
                leak_ref[s, k, half] = jnp.concatenate(piece, axis=0).astype(BF16)
    gg_ref[...] = gg


def grad_act_kernel(dp_ref, w_ref, ddt_ref, wdt_ref, dep_ref, out_ref):
    for lo in range(0, D, 256):
        part = lax.dot_general(
            dp_ref[...], w_ref[lo : lo + 256], (NT, ((), ())), preferred_element_type=F32
        )
        part = part + lax.dot_general(
            ddt_ref[...], wdt_ref[lo : lo + 256], (NT, ((), ())), preferred_element_type=F32
        )
        out_ref[:, lo : lo + 256] = part.astype(BF16)


def ssd_bwd_kernel(
    nctx, nk, pr, idx_ref, ext_ref, dtr_ref, st_ref, pv_ref, dy_ref, s_ref, g_ref, *refs
):
    dext_ref, ddt_ref, misc_ref = refs[-3:]
    base = block_base(idx_ref, nctx)
    st = st_ref[0]
    ext = ext_ref[0]
    pv = pv_ref[...]
    p = ssd_prep(ext, dtr_ref[0, 8:], st, base, pv)
    sel = p["sel"]
    x = p["xc"][:, :LX]
    bm = p["xc"][:, LX : LX + NSTATE]
    cm = p["xc"][:, LX + NSTATE :]
    bmb, cmb, xb = bm.astype(BF16), cm.astype(BF16), x.astype(BF16)
    dyb = dy_ref[0]
    dy = dyb.astype(F32)
    s_in = from_chunks(s_ref, nk, pr)
    g_out = from_chunks(g_ref, nk, pr)
    s_inb, g_outb = s_in.astype(BF16), g_out.astype(BF16)
    inter = dotb(cmb, bmb, NT)
    swx = dotf(p["sw"], sel, NN)
    fwx = dotf(p["fw"], sel, NN)
    skip = pv[7:8, :LX]
    lane = iota((BLK, 128), 1)
    d_inter = jnp.zeros((BLK, BLK), F32)
    drun = jnp.zeros((BLK, 128), F32)
    dx_parts = []
    col_rows = []
    for h in range(LOCAL_HEADS):
        sl = slice(h * HDIM, (h + 1) * HDIM)
        dec = decay_of(p, h)
        dt_row = p["dt_t"][h : h + 1]
        dec_inter = dec * inter
        d_mix = dotb(dyb[:, sl], xb[:, sl], NT)
        dx_parts.append(dotb(dec_inter * dt_row, dyb[:, sl], TN))
        d_inter = d_inter + d_mix * dec * dt_row
        f = d_mix * dec_inter
        row = jnp.sum(f * dt_row, axis=1, keepdims=True)
        drun = drun + jnp.where(lane == h, row, 0.0)
        col_rows.append(jnp.sum(f, axis=0, keepdims=True))
    col_rows.append(jnp.zeros((2, BLK), F32))
    cols = jnp.concatenate(col_rows, axis=0)
    pick = (iota((8, 128), 0) == iota((8, 128), 1)).astype(F32)
    col = dotf(cols, pick, TN)
    ddt = col
    drun = drun - p["dt"] * col
    dx = jnp.concatenate(dx_parts, axis=1) + skip * dy
    dcm = dotb(d_inter, bmb, NN)
    dbm = dotb(d_inter, cmb, TN)
    swdy = swx * dy
    yin = dotb(cmb, s_inb, NT)
    drun = drun + dotf(swdy * yin, sel, NT)
    dcm = dcm + dotb(swdy, s_inb, NN)
    back = dotb(bmb, g_outb, NT)
    dbm = dbm + dotb(fwx * x, g_outb, NN)
    dx = dx + fwx * back
    dfw = dotf(x * back, sel, NT)
    ddt = ddt + dfw * p["fd"]
    tail = dfw * p["fw"]
    drun = drun - tail
    carry = jnp.sum(s_in * g_out, axis=1, keepdims=True)
    sel_t = (iota((LX, 128), 0) // HDIM == iota((LX, 128), 1)).astype(F32)
    last = jnp.sum(tail, axis=0, keepdims=True) + p["sw"][BLK - 1 : BLK] * jnp.sum(
        carry * sel_t, axis=0, keepdims=True
    )
    drun = drun + jnp.where(iota((BLK, 128), 0) == BLK - 1, last, 0.0)
    dell = dotf(p["tri"], drun, TN)
    ddt = ddt - p["ea"] * dell
    ddtraw = ddt * sigmoid(p["lin"])
    ddtraw = jnp.where(lane < LOCAL_HEADS, ddtraw, 0.0)
    zero8 = jnp.zeros((8, 128), F32)
    ddt_ref[0] = jnp.concatenate([zero8, ddtraw], axis=0).astype(BF16)
    dxc = jnp.concatenate([dx, dbm, dcm], axis=1)
    dpre = dxc * (p["sg"] * (1.0 + p["pre"] * (1.0 - p["sg"])))
    dext = jnp.zeros((EXT, LCONV), F32)
    rows = []
    for tap in range(4):
        use = (p["tpos"] - (3 - tap)) >= p["stc"]
        term = jnp.where(use, dpre, 0.0)
        rows.append(jnp.sum(term * ext[5 + tap : 5 + tap + BLK], axis=0, keepdims=True))
        term = term * pv[tap : tap + 1]
        pieces = [jnp.zeros((5 + tap, LCONV), F32), term]
        if tap < 3:
            pieces.append(jnp.zeros((3 - tap, LCONV), F32))
        dext = dext + jnp.concatenate(pieces, axis=0)
    dext_ref[0] = dext.astype(BF16)
    rows.append(jnp.sum(dpre, axis=0, keepdims=True))
    pad = jnp.zeros((1, LCONV - LX), F32)
    rows.append(jnp.concatenate([jnp.sum(dy * x, axis=0, keepdims=True), pad], axis=1))
    pad = jnp.zeros((1, LCONV - 128), F32)
    rows.append(jnp.concatenate([jnp.sum(ddtraw, axis=0, keepdims=True), pad], axis=1))
    rows.append(jnp.concatenate([jnp.sum(dell * p["ell"], axis=0, keepdims=True), pad], axis=1))
    misc_ref[0] = jnp.concatenate(rows, axis=0)


def scan_kernel(reverse, n, pr, st_ref, dec_ref, *refs):
    out_ref = refs[-1]
    rows = LOCAL_HEADS * pr

    def step(j, half, s):
        out_ref[j, half] = s.astype(BF16)
        d = dec_ref[j, half, rows : rows + 16].astype(F32)
        d = d[:LOCAL_HEADS] + d[8 : 8 + LOCAL_HEADS]
        d = jnp.broadcast_to(d[:, None, :], (LOCAL_HEADS, pr, 128)).reshape(rows, 128)
        return d * s + st_ref[j, half, :rows].astype(F32)

    first, second = (1, 0) if reverse else (0, 1)
    s = jnp.zeros((rows, 128), F32)
    s = lax.fori_loop(0, n, lambda j, s: step(j, first, s), s)
    lax.fori_loop(0, n, lambda j, s: step(n - 1 - j, second, s), s)


def unit_of(u, gi):
    if u < 4:
        return 1, 0, u
    is_a = u < 5 + gi
    rowset = jnp.where(is_a, 0, 1)
    half = jnp.where(is_a, 0, 1)
    return rowset, half, jnp.where(is_a, u - 4, u - 5)


def unit_mask(nctx, gs, i, rowset, half, g, st):
    shape = (2 * BLK, gs * BLK)
    row = iota(shape, 0) % BLK
    col = iota(shape, 1)
    qpos = jnp.where(rowset == 0, i, 2 * nctx - 1 - i) * BLK + row
    block = g * gs + col // BLK
    kpos = jnp.where(half == 0, block, 2 * nctx - 1 - block) * BLK + col % BLK
    return (kpos <= qpos) & (kpos >= st)


def attn_fwd_kernel(nctx, gs, idx_ref, q_ref, kv_ref, st_ref, o_ref, lse_ref, s_ref, m_ref, l_ref, acc_ref):
    i = idx_ref[0]
    gi = i // gs
    m_ref[...] = jnp.full(m_ref.shape, NEG, F32)
    l_ref[...] = jnp.zeros(l_ref.shape, F32)
    acc_ref[...] = jnp.zeros(acc_ref.shape, F32)
    for u in range(9):
        rowset, half, g = unit_of(u, gi)
        kv = kv_ref[pl.ds(g * gs, gs), 0, half].reshape(gs * BLK, 128)
        s = dotb(q_ref[0, rowset], kv[:, :HDIM], NT)
        ok = unit_mask(nctx, gs, i, rowset, half, g, st_ref[0, rowset, :, :1])
        s = jnp.where(ok, s, NEG)
        s_ref[u] = s
        m_ref[rowset] = jnp.maximum(m_ref[rowset], jnp.max(s, axis=1, keepdims=True))
    for u in range(9):
        rowset, half, g = unit_of(u, gi)
        kv = kv_ref[pl.ds(g * gs, gs), 0, half].reshape(gs * BLK, 128)
        w = jnp.exp(s_ref[u] - m_ref[rowset, :, :1])
        l_ref[rowset] = l_ref[rowset] + jnp.sum(w, axis=1, keepdims=True)
        acc_ref[rowset] = acc_ref[rowset] + dotb(w, kv[:, HDIM:], NN)
    o_ref[0] = acc_ref[...] / l_ref[:, :, :HDIM]
    lse_ref[0] = m_ref[...] + jnp.log(l_ref[...])


def attn_bwd_kernel(
    nctx, gs, idx_ref, q_ref, kv_ref, st_ref, o_ref, lse_ref, do_ref, cos_ref, sin_ref, *refs
):
    out_ref, keep_ref, give_ref, del_ref, acc_ref, dq_ref = refs[-6:]
    i = idx_ref[0]
    gi = i // gs
    acc_ref[...] = jnp.zeros(acc_ref.shape, F32)
    dq_ref[...] = jnp.zeros(dq_ref.shape, F32)
    delta = jnp.sum(do_ref[0].astype(F32) * o_ref[0], axis=2, keepdims=True)
    del_ref[...] = jnp.broadcast_to(delta, del_ref.shape)
    for u in range(9):
        rowset, half, g = unit_of(u, gi)
        kv = kv_ref[pl.ds(g * gs, gs), 0, half].reshape(gs * BLK, 128)
        q = q_ref[0, rowset]
        do = do_ref[0, rowset]
        s = dotb(q, kv[:, :HDIM], NT)
        ok = unit_mask(nctx, gs, i, rowset, half, g, st_ref[0, rowset, :, :1])
        prob = jnp.exp(jnp.where(ok, s, NEG) - lse_ref[0, rowset, :, :1])
        dp = dotb(do, kv[:, HDIM:], NT)
        ds = (prob * (dp - del_ref[rowset, :, :1])).astype(BF16)
        dkv = jnp.concatenate([dotb(ds, q, TN), dotb(prob, do, TN)], axis=1)
        acc_ref[half, g] = acc_ref[half, g] + dkv
        dq_ref[rowset] = dq_ref[rowset] + dotb(ds, kv[:, :HDIM], NN)
    for half in range(2):
        parts = []
        for e in range(2):
            part = dq_ref[half, BLK * e : BLK * e + BLK] * HDIM**-0.5
            parts.append(turned(part, cos_ref[half], -sin_ref[half]))
        out_ref[0, half] = jnp.concatenate(parts, axis=1).astype(BF16)

    def write(even_ref, odd_ref):
        for src in range(4 * gs):
            g, at = src // gs, (src % gs) * BLK
            ref = odd_ref if src % 2 else even_ref
            for half in range(2):
                ref[src // 2, 0, half] = acc_ref[half, g, at : at + BLK].astype(BF16)

    @pl.when(i % 2 == 0)
    def _():
        write(keep_ref, give_ref)

    @pl.when(i % 2 == 1)
    def _():
        write(give_ref, keep_ref)


def spec(shape, index):
    return pl.BlockSpec(shape, index)


def per_pair(shape):
    return pl.BlockSpec((1,) + shape, lambda j: (j,) + (0,) * len(shape))


def whole(shape):
    return pl.BlockSpec(shape, lambda *j: (0,) * len(shape))


def chunk_spec(nk, rows):
    return pl.BlockSpec((1, nk, 1, rows, 128), lambda j: (j // 2, 0, j % 2, 0, 0))


ANY = pl.BlockSpec(memory_space=pl.ANY)
VMEM = pl.BlockSpec(memory_space=pltpu.VMEM)
SMEM = pl.BlockSpec(memory_space=pltpu.SMEM)
PARAMS = pltpu.CompilerParams(vmem_limit_bytes=16 * 1024 * 1024)
WIDER = pltpu.CompilerParams(vmem_limit_bytes=28 * 1024 * 1024)
WIDEST = pltpu.CompilerParams(vmem_limit_bytes=48 * 1024 * 1024)


def cost(flops, moved, trans=0):
    return pl.CostEstimate(flops=flops // 1000, bytes_accessed=moved // 1000, transcendentals=0)


def sds(shape, dtype):
    return jax.ShapeDtypeStruct(shape, dtype)


def exchange(parts, axis):
    return lax.all_to_all(parts, axis, 0, 0, tiled=True)


def spread(part, axis):
    return exchange(jnp.broadcast_to(part[None], (lax.axis_size(axis),) + part.shape), axis)


def shifts():
    return [(k, [(a, (a + k) % 4) for a in range(4)]) for k in (1, 2, 3)]


def ring_exchange(parts, z):
    out = parts
    for k, perm in shifts():
        sent = lax.dynamic_index_in_dim(parts, (z + k) % 4, 0, keepdims=False)
        got = lax.ppermute(sent, "fsdp", perm)
        out = lax.dynamic_update_index_in_dim(out, got, (z - k) % 4, 0)
    return out


def ring_spread(part, z):
    out = jnp.broadcast_to(part[None], (4,) + part.shape)
    for k, perm in shifts():
        got = lax.ppermute(part, "fsdp", perm)
        out = lax.dynamic_update_index_in_dim(out, got, (z - k) % 4, 0)
    return out


def ring_sum(rows, z):
    parts = rows.astype(BF16).reshape((4, -1) + rows.shape[1:])
    total = lax.dynamic_index_in_dim(parts, z, 0, keepdims=False).astype(F32)
    for k, perm in shifts():
        sent = lax.dynamic_index_in_dim(parts, (z + k) % 4, 0, keepdims=False)
        total = total + lax.ppermute(sent, "fsdp", perm).astype(F32)
    return total


def as_rows(column):
    high = lax.reduce_precision(column, 8, 7)
    pair = jnp.stack([high, column - high], axis=-2).astype(BF16)
    pads = [(0, 0)] * (pair.ndim - 2) + [(0, 14), (0, D - 128)]
    return jnp.pad(pair, pads)


def from_rows(rows):
    pair = rows[..., :2, :128].astype(F32)
    return pair[..., 0, :] + pair[..., 1, :]


def rms_of(v):
    return lax.rsqrt(jnp.mean(v * v, axis=-1, keepdims=True) + EPS)


def rms_back(v, r, dn):
    n = v * r
    return r * (dn - n * jnp.mean(dn * n, axis=-1, keepdims=True))


def matmul(a, b, dims=NN):
    return lax.dot_general(a, b, (dims, ((), ())), preferred_element_type=F32)


def per_device(
    tokens,
    doc_start,
    cotangent,
    w_in,
    w_dt,
    conv_weight,
    conv_bias,
    dt_bias,
    a_log,
    skip_gain,
    inner_gain,
    mamba_out,
    attn_out,
    mixer_gain,
    ffn_gain,
    w_gate_up,
    w_down,
):
    nctx = lax.axis_size("ctx")
    i = lax.axis_index("ctx")
    z = lax.axis_index("fsdp")
    nk = nctx // 4
    pr = HDIM // nk
    gs = nctx // 4
    rpc = 256 // nctx
    idx = i.astype(jnp.int32).reshape(1)
    last_device = i == nctx - 1
    up = [(a, a + 1) for a in range(nctx - 1)]
    down = [(b, a) for a, b in up]

    core = i % 2
    core_idx = core.astype(jnp.int32).reshape(1)
    pair = [(a, a ^ 1) for a in range(nctx)]
    send_in = pl.pallas_call(
        split_in_kernel,
        in_specs=[SMEM, VMEM],
        out_specs=VMEM,
        out_shape=sds((4, 128, LPROJ), BF16),
        compiler_params=PARAMS,
        cost_estimate=cost(0, 5 * 10**6),
        name="split_in",
    )(core_idx, w_in)
    z_idx = z.astype(jnp.int32).reshape(1)
    grad_own = cotangent[0].reshape(128, D)
    gu_parts = pl.pallas_call(
        split_gate_up_kernel,
        in_specs=[SMEM, VMEM, VMEM],
        out_specs=[VMEM] * 4,
        out_shape=[sds((384, 1024), BF16)] * 4,
        compiler_params=PARAMS,
        cost_estimate=cost(0, 4 * 10**6),
        name="split_gate_up",
    )(z_idx, w_gate_up, grad_own)
    tok = tokens[0]
    tails = tok[:, BLK - 3 :, :]
    halo_first = lax.ppermute(tails[0], "ctx", up)
    halo_second = lax.ppermute(tails[1], "ctx", down)
    halo = jnp.stack([halo_first, jnp.where(last_device, tails[0], halo_second)])
    starts_own = doc_start[0]
    flat = jnp.concatenate(
        [
            w_dt.reshape(-1),
            conv_weight.reshape(-1),
            conv_bias,
            mixer_gain,
            ffn_gain,
            (starts_own // 64).astype(BF16).reshape(-1),
            (starts_own % 64).astype(BF16).reshape(-1),
        ]
    )
    flat = jnp.pad(flat, (0, 10 * D - flat.shape[0])).reshape(2, 5, D)
    wide = ring_spread(jnp.concatenate([flat, halo, tok], axis=1), z)
    mine_in = exchange(send_in, "fsdp")
    other_in = lax.ppermute(mine_in, "ctx", pair)
    own_gu, grad_all = pl.pallas_call(
        place_kernel,
        in_specs=[SMEM] + [VMEM] * 4,
        out_specs=[VMEM] * 2,
        out_shape=[sds((4, 256, 1024), BF16), sds((4, 128, D), BF16)],
        compiler_params=PARAMS,
        cost_estimate=cost(0, 6 * 10**6),
        name="place",
    )(
        z_idx,
        gu_parts[0],
        *[lax.ppermute(gu_parts[k], "fsdp", perm) for k, perm in shifts()],
    )
    own_gu = own_gu.reshape(D, 1024)
    grad_all = grad_all.reshape(512, D)
    flat = wide[:, :, :5, :].reshape(4, 10 * D)
    full_dt = flat[:, :6144].reshape(D, 24)
    own_dt = jnp.pad(lax.dynamic_slice_in_dim(full_dt, 6 * z, 6, axis=1), ((0, 0), (0, 122)))
    full_conv = flat[:, 6144:7936].reshape(4, 4, 448).transpose(1, 0, 2).reshape(4, 1792)
    full_bias = flat[:, 7936:8384].reshape(1, 1792)
    full_taps = jnp.concatenate([full_conv, full_bias], axis=0).astype(F32)
    mixer_scale = flat[:, 8384:8640].reshape(D).astype(F32)
    ffn_scale = flat[:, 8640:8896].reshape(D).astype(F32)
    starts = (
        flat[:, 8896:9024].astype(jnp.int32) * 64 + flat[:, 9024:9152].astype(jnp.int32)
    ).reshape(8, BLK)
    own_taps = jnp.concatenate(
        [lax.dynamic_slice_in_dim(full_taps, LX * z, LX, axis=1), full_taps[:, 1536:]], axis=1
    )

    def lanes(v):
        return jnp.pad(v.astype(F32), (0, LCONV - v.shape[0]))[None]

    pv = jnp.concatenate(
        [own_taps, lanes(dt_bias), lanes(a_log), lanes(jnp.repeat(skip_gain, HDIM))], axis=0
    )
    inner_scale = inner_gain.astype(F32)

    rows = 8 * EXT
    st_wide = jnp.broadcast_to(starts[:, :, None], (8, BLK, 128))
    blocks = jnp.stack([i, 2 * nctx - 1 - i])
    positions = blocks[:, None] * BLK + jnp.arange(BLK, dtype=jnp.int32)[None, :]
    freq = jnp.exp(
        jnp.arange(HDIM // 2, dtype=F32) * (-2.0 * math.log(ROPE_BASE) / HDIM)
    )
    angle = positions.astype(F32)[:, :, None] * freq
    cosine, sine = jnp.cos(angle), jnp.sin(angle)
    gate_z, conv_ext, raw_dt, query, kv_own, act_one, own_in = pl.pallas_call(
        proj_kernel,
        in_specs=[SMEM] + [VMEM] * 7 + [ANY] * 6,
        out_specs=[VMEM] * 7,
        out_shape=[
            sds((8, BLK, LX), BF16),
            sds((8, EXT, LCONV), F32),
            sds((8, EXT, 128), F32),
            sds((4, 2, 2 * BLK, HDIM), BF16),
            sds((4, 2, BLK, 128), BF16),
            sds((rows, D), BF16),
            sds((D, LPROJ), BF16),
        ],
        compiler_params=WIDER,
        cost_estimate=cost(2 * 10**9, 8 * 10**6),
        name="proj",
    )(
        core_idx, wide.reshape(rows, D), mine_in, other_in, own_dt, mixer_scale[None],
        cosine, sine, pv, st_wide, *gu_parts,
    )

    srows = LOCAL_HEADS * pr
    ssd_in = (idx, conv_ext, raw_dt, st_wide, pv)
    ssd_in_specs = [
        SMEM,
        per_pair((EXT, LCONV)),
        per_pair((EXT, 128)),
        per_pair((BLK, 128)),
        whole((8, LCONV)),
    ]
    y_local, swx, c_mat, state_out = pl.pallas_call(
        functools.partial(ssd_fwd_kernel, nctx, nk, pr),
        grid=(8,),
        in_specs=ssd_in_specs,
        out_specs=[
            per_pair((BLK, LX)),
            per_pair((BLK, LX)),
            per_pair((BLK, 128)),
            chunk_spec(nk, srows + 16),
        ],
        out_shape=[
            sds((8, BLK, LX), BF16),
            sds((8, BLK, LX), BF16),
            sds((8, BLK, 128), BF16),
            sds((4, nk, 2, srows + 16, 128), BF16),
        ],
        compiler_params=PARAMS,
        cost_estimate=cost(2 * 10**9, 6 * 10**6),
        name="ssd_fwd",
    )(*ssd_in)
    got = exchange(state_out.reshape(nctx, 2, srows + 16, 128), "ctx")
    kv_all = lax.all_gather(kv_own, "ctx")

    st_rows = jnp.broadcast_to(
        starts.reshape(4, 2, 1, BLK, 1), (4, 2, 2, BLK, 128)
    ).reshape(4, 2, 2 * BLK, 128)
    def chain(reverse, terms, *after):
        return pl.pallas_call(
            functools.partial(scan_kernel, reverse, nctx, pr),
            in_specs=[VMEM, VMEM] + [ANY] * len(after),
            out_specs=VMEM,
            out_shape=sds((nctx, 2, srows, 128), BF16),
            compiler_params=PARAMS,
            cost_estimate=cost(10**7, 3 * 10**6),
            name="chain",
        )(terms, got, *after)

    entry = exchange(chain(False, got, st_rows), "ctx").reshape(4, nk, 2, srows, 128)

    row_spec = pl.BlockSpec((1, 2, 2 * BLK, HDIM), lambda s: (s, 0, 0, 0))
    wide_spec = pl.BlockSpec((1, 2, 2 * BLK, 128), lambda s: (s, 0, 0, 0))
    kv_spec = pl.BlockSpec((nctx, 1, 2, BLK, 128), lambda s: (0, s, 0, 0, 0))
    attn_o, lse = pl.pallas_call(
        functools.partial(attn_fwd_kernel, nctx, gs),
        grid=(4,),
        in_specs=[SMEM, row_spec, kv_spec, wide_spec],
        out_specs=[row_spec, wide_spec],
        out_shape=[sds((4, 2, 2 * BLK, HDIM), F32), sds((4, 2, 2 * BLK, 128), F32)],
        scratch_shapes=[
            pltpu.VMEM((9, 2 * BLK, gs * BLK), F32),
            pltpu.VMEM((2, 2 * BLK, 128), F32),
            pltpu.VMEM((2, 2 * BLK, 128), F32),
            pltpu.VMEM((2, 2 * BLK, HDIM), F32),
        ],
        compiler_params=PARAMS,
        cost_estimate=cost(4 * 10**9, 8 * 10**6, 2 * 10**6),
        name="attn_fwd",
    )(idx, query, kv_all, st_rows)
    act_attn = (
        attn_o.reshape(4, 2, 2, BLK, HDIM).transpose(0, 1, 3, 2, 4).reshape(512, 128).astype(BF16)
    )

    mamba_y, scaled_u, squares = pl.pallas_call(
        functools.partial(ssd_out_kernel, nk, pr),
        grid=(8,),
        in_specs=[
            per_pair((BLK, LX)),
            per_pair((BLK, LX)),
            per_pair((BLK, 128)),
            chunk_spec(nk, srows),
            per_pair((BLK, LX)),
            whole((1, LX)),
        ]
        + [ANY] * 3,
        out_specs=[per_pair((BLK, LX)), per_pair((BLK, LX)), per_pair((BLK, 128))],
        out_shape=[
            sds((8, BLK, LX), BF16),
            sds((8, BLK, LX), BF16),
            sds((8, BLK, 128), F32),
        ],
        compiler_params=PARAMS,
        cost_estimate=cost(10**9, 6 * 10**6),
        name="ssd_out",
    )(y_local, swx, c_mat, entry, gate_z, inner_scale[None], attn_o, own_gu, grad_all)

    def gather_sum(part_rows):
        got_rows = exchange(part_rows.astype(BF16).reshape((4, -1) + part_rows.shape[1:]), "fsdp")
        return jnp.sum(got_rows.astype(F32), axis=0)

    attn_mid = ring_sum(matmul(act_attn, attn_out), z)
    part_rows = pl.pallas_call(
        mid_kernel,
        in_specs=[VMEM] * 3 + [ANY],
        out_specs=VMEM,
        out_shape=sds((4, 144, D), BF16),
        compiler_params=PARAMS,
        cost_estimate=cost(4 * 10**8, 3 * 10**6),
        name="mid_part",
    )(scaled_u.reshape(512, LX), mamba_out, squares.reshape(512, 128), attn_mid)
    got_part = exchange(part_rows, "fsdp")
    scaled_mid = jnp.sum(got_part[:, :128].astype(F32), axis=0)
    square_sum = jnp.sum(from_rows(got_part[:, 128:]), axis=0)
    own_r = lax.rsqrt(square_sum.reshape(128, 1) * (1.0 / 1536) + EPS)
    mamba_mid = scaled_mid * own_r
    middle = tok.reshape(128, D).astype(F32) + mamba_mid + attn_mid
    mid_r = rms_of(middle)
    norm_two = middle * mid_r
    def spread_rows(values, column):
        sent = jnp.concatenate([values.astype(BF16), as_rows(column.reshape(128))], axis=0)
        return spread(sent, "fsdp").reshape(4, 144, D)

    act_two = spread_rows(norm_two * ffn_scale, own_r)
    r_tail = act_two[:, 128:, :128]
    act_two = act_two[:, :128].reshape(512, D)

    gate_up = matmul(act_two, own_gu)
    gate_val, up_val = gate_up[:, :512], gate_up[:, 512:]
    gate_sig = sigmoid(gate_val)
    gate_silu = gate_val * gate_sig
    inner = (gate_silu * up_val).astype(BF16)
    grad_inner = matmul(grad_all, w_down, NT)
    grad_gate = grad_inner * up_val * (gate_sig * (1.0 + gate_val * (1.0 - gate_sig)))
    grad_gu = jnp.concatenate([grad_gate, grad_inner * gate_silu], axis=1).astype(BF16)
    grad_act_two = gather_sum(matmul(grad_gu, own_gu, NT))
    grad_down = matmul(inner, grad_all, TN).astype(BF16)
    grad_gate_up = matmul(act_two, grad_gu, TN).astype(BF16)
    grad_ffn_gain = jnp.sum(grad_act_two * norm_two, axis=0)
    grad_middle = grad_own.astype(F32) + rms_back(middle, mid_r, grad_act_two * ffn_scale)
    own_mix = grad_middle.astype(BF16)
    own_dots = jnp.sum(own_mix.astype(F32) * mamba_mid, axis=1) * (1.0 / 1536)
    grad_rows = spread_rows(own_mix, own_dots)
    grad_mix, grad_attn, act_mamba, grad_y, grad_z, grad_inner_gain, leak = pl.pallas_call(
        functools.partial(post_mix_kernel, nk, pr),
        in_specs=[VMEM] * 9,
        out_specs=[VMEM] * 7,
        out_shape=[
            sds((512, D), BF16),
            sds((4, 2, 2 * BLK, HDIM), BF16),
            sds((512, LX), BF16),
            sds((8, BLK, LX), BF16),
            sds((8, BLK, LX), BF16),
            sds((1, LX), F32),
            sds((4, nk, 2, srows, 128), BF16),
        ],
        compiler_params=WIDER,
        cost_estimate=cost(10**9, 8 * 10**6),
        name="post_mix",
    )(
        grad_rows, r_tail, mamba_out, attn_out, mamba_y, gate_z, inner_scale[None], swx, c_mat
    )

    down_part = pl.pallas_call(
        down_kernel,
        in_specs=[VMEM, VMEM, ANY],
        out_specs=VMEM,
        out_shape=sds((512, D), BF16),
        compiler_params=PARAMS,
        cost_estimate=cost(5 * 10**8, 3 * 10**6),
        name="down",
    )(inner, w_down, grad_mix)
    mixed = (middle + ring_sum(down_part, z)).astype(BF16).reshape(1, 2, BLK, D)

    grad_mamba_out = matmul(act_mamba, grad_mix, TN).astype(BF16)
    grad_attn_out = matmul(act_attn, grad_mix, TN).astype(BF16)
    def halves(v):
        v = v.reshape(4, 2, 128, v.shape[-1])
        keep = lax.dynamic_index_in_dim(v, core, 1, keepdims=False)
        give = lax.dynamic_index_in_dim(v, 1 - core, 1, keepdims=False)
        return keep, lax.ppermute(give, "ctx", pair)

    kept, taken = halves(grad_gate_up)
    pair_gu = (kept.astype(F32) + taken.astype(F32)).astype(BF16)
    out_grads = jnp.concatenate([grad_mamba_out, grad_attn_out], axis=0)
    kept = jnp.where(core == 0, grad_down, out_grads)
    taken = lax.ppermute(jnp.where(core == 0, out_grads, grad_down), "ctx", pair)
    pair_o = (kept.astype(F32) + taken.astype(F32)).astype(BF16)
    got_leak = exchange(leak.reshape(nctx, 2, srows, 128), "ctx")
    half_kv_spec = pl.BlockSpec((nctx // 2, 1, 2, BLK, 128), lambda s: (0, s, 0, 0, 0))
    grad_query, keep_kv, give_kv = pl.pallas_call(
        functools.partial(attn_bwd_kernel, nctx, gs),
        grid=(4,),
        in_specs=[SMEM, row_spec, kv_spec, wide_spec, row_spec, wide_spec, row_spec]
        + [whole((2, BLK, HDIM // 2))] * 2
        + [ANY] * 5,
        out_specs=[
            pl.BlockSpec((1, 2, BLK, 128), lambda s: (s, 0, 0, 0)),
            half_kv_spec,
            half_kv_spec,
        ],
        out_shape=[
            sds((4, 2, BLK, 128), BF16),
            sds((nctx // 2, 4, 2, BLK, 128), BF16),
            sds((nctx // 2, 4, 2, BLK, 128), BF16),
        ],
        scratch_shapes=[
            pltpu.VMEM((2, 2 * BLK, 128), F32),
            pltpu.VMEM((2, 4, gs * BLK, 128), F32),
            pltpu.VMEM((2, 2 * BLK, HDIM), F32),
        ],
        compiler_params=PARAMS,
        cost_estimate=cost(8 * 10**9, 16 * 10**6, 2 * 10**6),
        name="attn_bwd",
    )(
        idx, query, kv_all, st_rows, attn_o, lse, grad_attn, cosine, sine,
        leak, grad_gate_up, grad_down, grad_mamba_out, grad_attn_out,
    )
    chained = chain(True, got_leak, give_kv)
    grad_exit = exchange(chained, "ctx").reshape(4, nk, 2, srows, 128)
    give_kv = pl.pallas_call(
        hold_kernel,
        in_specs=[VMEM, ANY],
        out_specs=VMEM,
        out_shape=sds(give_kv.shape, BF16),
        compiler_params=PARAMS,
        cost_estimate=cost(0, 4 * 10**6),
        name="hold",
    )(give_kv, chained)
    taken_kv = lax.ppermute(give_kv, "ctx", pair)
    pair_kv = (keep_kv.astype(F32) + taken_kv.astype(F32)).astype(BF16)
    nj = nctx // 2
    rj = 128 // nj
    groups = [[2 * j + c for j in range(nj)] for c in range(2)]
    grad_ext, grad_dt, misc = pl.pallas_call(
        functools.partial(ssd_bwd_kernel, nctx, nk, pr),
        grid=(8,),
        in_specs=ssd_in_specs
        + [per_pair((BLK, LX)), chunk_spec(nk, srows), chunk_spec(nk, srows)],
        out_specs=[per_pair((EXT, LCONV)), per_pair((EXT, 128)), per_pair((8, LCONV))],
        out_shape=[
            sds((8, EXT, LCONV), BF16),
            sds((8, EXT, 128), BF16),
            sds((8, 8, LCONV), F32),
        ],
        compiler_params=PARAMS,
        cost_estimate=cost(4 * 10**9, 8 * 10**6),
        name="ssd_bwd",
    )(*ssd_in, grad_y, entry, grad_exit)

    grad_dt = grad_dt.reshape(rows, 128)
    grad_dtw = matmul(act_one, grad_dt, TN)
    misc = jnp.sum(misc, axis=0)
    grad_skip = jnp.sum(misc[5, :LX].reshape(LOCAL_HEADS, HDIM), axis=1)
    small = jnp.concatenate(
        [misc[:5].reshape(-1), misc[6, :6], misc[7, :6], grad_skip, grad_inner_gain[0]]
    )
    small = jnp.pad(small, (0, 3840 - small.shape[0])).reshape(1, 256, 15)
    small = jnp.broadcast_to(small, (4, 256, 15)).reshape(D, 15)
    extras = jnp.concatenate(
        [
            grad_dtw[:, :6],
            grad_ffn_gain[:, None],
            small,
            jnp.zeros((D, 106), F32),
        ],
        axis=1,
    ).astype(BF16)
    early = pl.pallas_call(
        functools.partial(pack_early_kernel, nj, rj),
        in_specs=[VMEM] * 2,
        out_specs=VMEM,
        out_shape=sds((nj, 4, rj, 2048), BF16),
        compiler_params=PARAMS,
        cost_estimate=cost(0, 4 * 10**6),
        name="pack_early",
    )(pair_gu, pair_o)

    def core_exchange(parts):
        return lax.all_to_all(parts, "ctx", 0, 0, axis_index_groups=groups, tiled=True)

    grad_proj = pl.pallas_call(
        functools.partial(dproj_kernel, nj),
        in_specs=[VMEM] * 6 + [ANY] * 2,
        out_specs=VMEM,
        out_shape=sds((8, EXT, LPROJ), BF16),
        compiler_params=PARAMS,
        cost_estimate=cost(2 * 10**6, 4 * 10**6),
        name="dproj",
    )(
        core_exchange(pair_kv), grad_z, grad_ext, grad_query, cosine, sine,
        early, extras,
    ).reshape(rows, LPROJ)
    got_early = core_exchange(early)

    grad_in = matmul(act_one, grad_proj, TN).astype(BF16)
    kept_in, taken_in = halves(grad_in)
    kept_ex, taken_ex = halves(extras)
    sent = pl.pallas_call(
        functools.partial(pack_kernel, nj, rj),
        in_specs=[VMEM] * 4 + [ANY],
        out_specs=VMEM,
        out_shape=sds((nj, 4, rj, 1408), BF16),
        compiler_params=PARAMS,
        cost_estimate=cost(0, 7 * 10**6),
        name="pack",
    )(kept_in, taken_in, kept_ex, taken_ex, got_early)
    got_late = core_exchange(sent)
    grad_act = pl.pallas_call(
        grad_act_kernel,
        in_specs=[VMEM] * 4 + [ANY],
        out_specs=VMEM,
        out_shape=sds((rows, D), BF16),
        compiler_params=PARAMS,
        cost_estimate=cost(2 * 10**9, 6 * 10**6),
        name="grad_act",
    )(grad_proj, own_in, grad_dt, own_dt, got_late)
    got_act = ring_sum(grad_act, z).reshape(2, EXT, D)
    halo_back = got_act[:, 5:8].astype(BF16)
    to_first = lax.ppermute(halo_back[0], "ctx", down).astype(F32)
    to_second = lax.ppermute(jnp.where(last_device, 0.0, halo_back[1]), "ctx", up).astype(F32)
    to_first = to_first + jnp.where(last_device, got_act[1, 5:8], 0.0)
    tail_add = jnp.pad(jnp.stack([to_first, to_second]), ((0, 0), (BLK - 3, 0), (0, 0)))
    own_act = (got_act[:, 8:] + tail_add).reshape(128, D)
    hidden = tok.reshape(128, D).astype(F32)
    grad_tokens = grad_middle + rms_back(hidden, rms_of(hidden), own_act * mixer_scale)
    grad_tokens = grad_tokens.reshape(1, 2, BLK, D)

    def total(got_parts, *after):
        return pl.pallas_call(
            functools.partial(total_kernel, nj),
            in_specs=[VMEM] + [ANY] * len(after),
            out_specs=VMEM,
            out_shape=sds(got_parts.shape[1:], F32),
            compiler_params=PARAMS,
            cost_estimate=cost(2 * 10**6, 4 * 10**6),
            name="total",
        )(got_parts, *after)

    summed = total(got_early, sent)
    owned_gu = ring_exchange(summed[:, :, :1024].astype(BF16), z)
    final_early = pl.pallas_call(
        assemble_early_kernel,
        in_specs=[VMEM] * 2 + [ANY],
        out_specs=VMEM,
        out_shape=sds((rj, 8192), BF16),
        compiler_params=PARAMS,
        cost_estimate=cost(0, 10**6),
        name="assemble_early",
    )(owned_gu, summed[:, :, 1024:], got_late)
    mine_early = core_exchange(jnp.broadcast_to(final_early[None], (nj, rj, 8192)))
    other_early = lax.ppermute(mine_early, "ctx", pair)
    owned = ring_exchange(total(got_late), z)
    final = pl.pallas_call(
        assemble_kernel,
        in_specs=[VMEM] + [ANY] * 3,
        out_specs=VMEM,
        out_shape=sds((rj, 4224), BF16),
        compiler_params=PARAMS,
        cost_estimate=cost(0, 10**6),
        name="assemble",
    )(owned, mine_early, grad_tokens, mixed)
    mine_all = core_exchange(jnp.broadcast_to(final[None], (nj, rj, 4224)))
    other_all = lax.ppermute(mine_all, "ctx", pair)
    half_spec = pl.BlockSpec((128, 4096), lambda h: (h, 0))
    total_gate_up, total_down, total_mamba_out, total_attn_out = pl.pallas_call(
        functools.partial(unpack_early_kernel, nj, rj),
        grid=(2,),
        in_specs=[SMEM, whole((nj, rj, 8192)), whole((nj, rj, 8192))],
        out_specs=[half_spec, whole((512, 1024)), whole((384, 1024)), whole((128, 1024))],
        out_shape=[
            sds((256, 4096), F32),
            sds((512, 1024), F32),
            sds((384, 1024), F32),
            sds((128, 1024), F32),
        ],
        compiler_params=WIDER,
        cost_estimate=cost(0, 10**7),
        name="unpack_early",
    )(core_idx, mine_early, other_early)
    total_in, mixer_dot, extra = pl.pallas_call(
        unpack_kernel,
        grid=(2,),
        in_specs=[SMEM, whole((nj, rj, 4224)), whole((nj, rj, 4224)), half_spec, ANY],
        out_specs=[
            half_spec,
            pl.BlockSpec((128, 128), lambda h: (h, 0)),
            pl.BlockSpec((128, 128), lambda h: (h, 0)),
        ],
        out_shape=[sds((256, 4096), F32), sds((256, 128), F32), sds((256, 128), F32)],
        compiler_params=WIDER,
        cost_estimate=cost(0, 10**7),
        name="unpack",
    )(core_idx, mine_all, other_all, w_in, total_attn_out)
    extra = extra[:, :88].reshape(256, 4, 22)
    total_dt = extra[:, :, :6].reshape(256, 24)
    mixer_dot = mixer_dot[:, 0] + jnp.sum(total_dt * w_dt.astype(F32), axis=1)
    total_mixer = mixer_dot / mixer_gain.astype(F32)
    total_ffn = jnp.sum(extra[:, :, 6], axis=1)
    small = extra[:, :, 7:22].transpose(1, 0, 2).reshape(4, 3840)
    taps = small[:, :3200].reshape(4, 5, LCONV)
    taps = jnp.concatenate(
        [
            taps[:, :, :LX].transpose(1, 0, 2).reshape(5, 1536),
            jnp.sum(taps[:, :, LX:], axis=0),
        ],
        axis=1,
    )
    taps = lax.dynamic_slice_in_dim(taps, 448 * z, 448, axis=1)
    mine = lax.dynamic_slice_in_dim(small, z, 1, axis=0)[0]
    return (
        mixed,
        grad_tokens,
        total_in,
        total_dt,
        taps[:4],
        taps[4],
        mine[3200:3206],
        mine[3206:3212],
        mine[3212:3218],
        mine[3218:3602],
        total_mamba_out,
        total_attn_out,
        total_mixer,
        total_ffn,
        total_gate_up,
        total_down,
    )


def solution(mesh):
    row = P("fsdp", None)
    vec = P("fsdp")
    act = P("fsdp", None, "ctx", None)
    return jax.shard_map(
        per_device,
        mesh=mesh,
        in_specs=(
            act, P("fsdp", None, "ctx"), act, row, row, P(None, "fsdp"), vec, vec, vec, vec, vec,
            row, row, vec, vec, row, row,
        ),
        out_specs=(
            act, act, row, row, P(None, "fsdp"), vec, vec, vec, vec, vec, row, row, vec, vec, row, row,
        ),
        check_vma=False,
    )
```
